32 devices in a mesh: pool: 8 (over z, x), blk: 4 (over y, core).
Axes of the slice: x: 2, y: 2, z: 4, core: 2. Of those that a mesh axis runs over, the one named last changes fastest.
Arguments:
- queries: bfloat16 [4096, 4096], P(('pool', 'blk')), may hold values from -26 to 26
- suffix_kv: bfloat16 [4096, 1024], P(('pool', 'blk')), may hold values from -5 to 5
- cache: bfloat16 [128, 128, 1024], P('pool'), may hold values from -6 to 6
- cache_scale: bfloat16 [128, 8], P('pool'), may hold values from 0.5 to 2
- prefix_len: int32 [8], replicated, may hold values from 1 to 2048, as said below
- suffix_len: int32 [8], replicated, may hold values from 256 to 512, as said below
- block_table: int32 [8, 16], replicated, may hold values from 0 to 127, as said below
- session_group: int32 [8], replicated, may hold values from 0 to 7, each once
Outputs:
- attention_out: bfloat16 [4096, 4096], P(('pool', 'blk'))
The draws below stay inside these ranges and needn't reach their ends.
Inputs may be any that keep to these rules, and one draw needn't show every extreme that they name: `prefix_len`: one session's prefix is exactly 2048 tokens long. `suffix_len`: one session has exactly 512 live suffix tokens. `block_table`: entry [s, j] = h * 16 + r names slot r of holder h (the rows h * 16 to h * 16 + 15 of cache); every storage slot is named exactly once; within each aligned run of 8 blocks of a session (blocks c * 8 to c * 8 + 7) every holder appears once, so a holder holds exactly 2 of each session's table entries. Entries past a session's length are named but hold no live tokens.
All inputs are finite; a program needn't handle non-finite values.
Results may differ from the reference program's by a relative error of at most 0.0026.
Values may be sent and summed in bfloat16 or wider, within the bound.
No kernel may reach another device: no remote copies, remote signals or barrier semaphores. Data moves between devices by JAX's collectives and lax.ppermute only.
A program may use at most 128 MiB of HBM per device.

```python
import math
import jax
import jax.numpy as jnp
from jax import lax

QH = 32
KVH = 4
HD = 128
BLOCK = 128
CAP = 2
SUFFIX = 512
SESS = 8
MAXB = 16
SLOTS = 16
N_POOL = 8


def draw_queries(key, part):
    key = jax.random.fold_in(key, 11)
    total_rows = N_POOL * SUFFIX
    noise = 2.0 * jax.random.truncated_normal(key, -4.0, 4.0, (total_rows, QH, HD), jnp.float32)
    return noise.reshape(total_rows, QH * HD).astype(jnp.bfloat16)


def draw_suffix_kv(key, part):
    key = jax.random.fold_in(key, 12)
    total_rows = N_POOL * SUFFIX
    noise = jax.random.truncated_normal(key, -5.0, 5.0, (total_rows, 2, KVH, HD), jnp.float32)
    return noise.reshape(total_rows, 2 * KVH * HD).astype(jnp.bfloat16)


def draw_prefix_len(key, part):
    key = jax.random.fold_in(key, 21)
    first_key, second = jax.random.split(key)
    longest = MAXB * BLOCK
    raw_picks = jax.random.randint(first_key, (SESS,), 0, longest)
    lengths = 1 + raw_picks * raw_picks // longest
    chosen = jax.random.randint(second, (), 0, SESS)
    return jnp.where(jnp.arange(SESS) == chosen, longest, lengths).astype(jnp.int32)


def draw_suffix_len(key, part):
    key = jax.random.fold_in(key, 22)
    first_key, second = jax.random.split(key)
    lengths = jax.random.randint(first_key, (SESS,), SUFFIX // 2, SUFFIX + 1)
    chosen = jax.random.randint(second, (), 0, SESS)
    return jnp.where(jnp.arange(SESS) == chosen, SUFFIX, lengths).astype(jnp.int32)


def draw_block_table(key, part):
    key = jax.random.fold_in(key, 23)
    first_key, second = jax.random.split(key)
    run_keys = jax.random.split(first_key, SESS * CAP)
    holders = jax.vmap(lambda single: jax.random.permutation(single, N_POOL))(run_keys).astype(jnp.int32)
    slot_keys = jax.random.split(second, N_POOL)
    orders = jax.vmap(lambda single: jax.random.permutation(single, SLOTS))(slot_keys).astype(jnp.int32)
    run_index = jnp.arange(SESS * CAP, dtype=jnp.int32)[:, None]
    places = orders[holders, run_index]
    return (holders * SLOTS + places).reshape(SESS, MAXB).astype(jnp.int32)


def levels(own_key, extent, cuts, low, largest):
    def one(axis_at, parts):
        steps = jax.random.uniform(jax.random.fold_in(jax.random.fold_in(own_key, 6), axis_at), (parts,), jnp.float32, low / len(cuts), largest / len(cuts))
        return jnp.repeat(jnp.exp(steps), extent[axis_at] // parts).reshape((-1,) + (1,) * (len(extent) - axis_at - 1))

    level = one(*cuts[0])
    for cut in cuts[1:]:
        level = level * one(*cut)
    return level


def scatter_about(stream_key, shape, scale, reach, shards=(), kind=jnp.bfloat16):
    entries = scale * jax.random.normal(stream_key, shape, jnp.float32)
    if shards:
        entries = entries * levels(stream_key, shape, shards, -0.22, 0.18)
    return jnp.clip(entries, -reach, reach).astype(kind)


def setup_inputs(seed: int = 0) -> dict:
    arg_keys = jax.random.split(jax.random.key(seed), 9)
    return {
        "queries": draw_queries(jax.random.fold_in(arg_keys[8], 71), 0),
        "suffix_kv": draw_suffix_kv(jax.random.fold_in(arg_keys[8], 71), 0),
        "cache": scatter_about(arg_keys[2], (N_POOL * SLOTS, BLOCK, 2 * KVH * HD), 1.0, 6.0, ((0, 8),)),
        "cache_scale": jnp.clip(jnp.exp(math.log(2.0) - 1.3862944 * jax.random.uniform(arg_keys[3], (N_POOL * SLOTS, 2 * KVH), jnp.float32) ** levels(arg_keys[3], (N_POOL * SLOTS, 2 * KVH), ((0, 8),), -0.2, 0.2)), 0.5, 2.0).astype(jnp.bfloat16),
        "prefix_len": draw_prefix_len(jax.random.fold_in(arg_keys[8], 71), 0),
        "suffix_len": draw_suffix_len(jax.random.fold_in(arg_keys[8], 71), 0),
        "block_table": draw_block_table(jax.random.fold_in(arg_keys[8], 71), 0),
        "session_group": jax.random.permutation(arg_keys[7], N_POOL).astype(jnp.int32),
    }


masked_score = -1e+30

def head_attention(usable, operands):
    query_head, key_rows, value_rows, key_scale, value_scale = operands
    scores = jnp.einsum('rgd,nd->rgn', query_head.astype(jnp.float32), key_rows.astype(jnp.float32))
    scores = scores * key_scale[None, None, :]
    scores = jnp.where(usable[:, None, :], scores, masked_score)
    highest = lax.optimization_barrier(jnp.max(scores, axis=2, keepdims=True))
    weights = jnp.where(usable[:, None, :], jnp.exp(scores - highest), 0.0)
    weight_sum = lax.optimization_barrier(jnp.sum(weights, axis=2, keepdims=True))
    rounded = lax.optimization_barrier((weights * value_scale[None, None, :]).astype(jnp.bfloat16))
    weighted = jnp.einsum('rgn,nd->rgd', rounded.astype(jnp.float32), value_rows.astype(jnp.float32))
    return weighted / weight_sum

def reference(queries, suffix_kv, cache, cache_scale, prefix_len, suffix_len, block_table, session_group):
    per_group = QH // KVH
    prefix_tokens = MAXB * BLOCK
    inv_root = 1.0 / math.sqrt(HD)
    suffix_place = jnp.arange(SUFFIX, dtype=jnp.int32)
    prefix_place = jnp.arange(prefix_tokens, dtype=jnp.int32)

    def one_group(group_index):
        session = session_group[group_index]
        table_row = block_table[session]
        prefix_length = prefix_len[session]
        suffix_length = suffix_len[session]
        blocks = cache[table_row].reshape(prefix_tokens, 2, KVH, HD)
        scales = jnp.repeat(cache_scale[table_row].astype(jnp.float32), BLOCK, axis=0).reshape(prefix_tokens, 2, KVH)
        first_row = (group_index * SUFFIX).astype(jnp.int32)
        query_rows = lax.dynamic_slice_in_dim(queries, first_row, SUFFIX, 0).reshape(SUFFIX, KVH, per_group, HD)
        suffix_rows = lax.dynamic_slice_in_dim(suffix_kv, first_row, SUFFIX, 0).reshape(SUFFIX, 2, KVH, HD)
        prefix_usable = jnp.broadcast_to((prefix_place < prefix_length)[None, :], (SUFFIX, prefix_tokens))
        suffix_usable = (suffix_place[None, :] <= suffix_place[:, None]) & (suffix_place[None, :] < suffix_length)
        usable = jnp.concatenate([prefix_usable, suffix_usable], axis=1)
        unit_scale = jnp.ones((SUFFIX, KVH), jnp.float32)
        key_scale = jnp.transpose(jnp.concatenate([scales[:, 0], unit_scale], axis=0)) * inv_root
        value_scale = jnp.transpose(jnp.concatenate([scales[:, 1], unit_scale], axis=0))
        key_rows = jnp.transpose(jnp.concatenate([blocks[:, 0], suffix_rows[:, 0]], axis=0), (1, 0, 2))
        value_rows = jnp.transpose(jnp.concatenate([blocks[:, 1], suffix_rows[:, 1]], axis=0), (1, 0, 2))
        per_head = lax.map(lambda operands: head_attention(usable, operands), (jnp.transpose(query_rows, (1, 0, 2, 3)), key_rows, value_rows, key_scale, value_scale))
        attended = jnp.transpose(per_head, (1, 0, 2, 3)).reshape(SUFFIX, QH * HD)
        return jnp.where((suffix_place < suffix_length)[:, None], attended, 0.0).astype(jnp.bfloat16)
    outputs = lax.map(one_group, jnp.arange(N_POOL, dtype=jnp.int32))
    return outputs.reshape(N_POOL * SUFFIX, QH * HD)
```

```python
import functools
import math

import jax
import jax.numpy as jnp
from jax import lax
from jax.experimental import pallas as pl
from jax.experimental.pallas import tpu as pltpu
from jax.sharding import PartitionSpec as P

QH = 32
KVH = 4
HD = 128
PER = QH // KVH
LOG2E = math.log2(math.e)

masked_score = -1e30

RUNS = 2
BLK = 128
PAIR = RUNS * BLK
ROWS = 128
WIDE = PER * ROWS
POOL = 8
META_J = 0
META_SLOT = 2 * POOL
META_LEN = 4 * POOL
META_SUF = 4 * POOL + 1
META_M = 4 * POOL + 2
META_SIZE = 4 * POOL + 8
TILE = 512
NT = (((1,), (1,)), ((), ()))
VMEM_LIMIT = 32 << 20


def gather_kernel(ids, table, groups, lengths, suffixes, cache, queries, meta, *refs):
    far = refs[:4]
    near = refs[4:7]
    other_q = refs[7]
    sems = refs[8]
    p = ids[0]
    m = ids[1]
    slot_count = cache.shape[0]
    copies = []

    def copy(src, dst):
        c = pltpu.make_async_copy(src, dst, sems.at[len(copies)])
        c.start()
        copies.append(c)

    def find(session, run, holder):
        low = holder * slot_count
        place = jnp.int32(0)
        entry = jnp.int32(0)
        for jj in range(POOL):
            e = table[session, run * POOL + jj]
            hit = (e >= low) & (e < low + slot_count)
            place = jnp.where(hit, run * POOL + jj, place)
            entry = jnp.where(hit, e, entry)
        return place, entry

    def block(ref, dst, local, run, head):
        for half in range(2):
            column = pl.multiple_of((half * KVH + head) * HD, HD)
            copy(
                cache.at[local, :, pl.ds(column, HD)],
                dst.at[half, pl.ds(run * BLK, BLK), :],
            )

    for k in (4, 5, 6, 7, 1, 2, 3):
        to = p ^ k
        session = groups[to]
        for run in range(RUNS):
            _, entry = find(session, run, p)
            local = entry - p * slot_count
            if k >= 4:
                block(cache, far[k - 4], local, run, m)
            else:
                block(cache, near[k - 1].at[0], local, run, m)
                block(cache, near[k - 1].at[1], local, run, m ^ 2)
    for slot in range(2):
        column = pl.multiple_of((m ^ (1 + 2 * slot)) * WIDE, WIDE)
        copy(queries.at[:, pl.ds(column, WIDE)], other_q.at[slot])
    own = groups[p]
    for k in range(POOL):
        for run in range(RUNS):
            place, entry = find(own, run, p ^ k)
            meta[META_J + RUNS * k + run] = place
            meta[META_SLOT + RUNS * k + run] = entry
    meta[META_LEN] = lengths[own]
    meta[META_SUF] = suffixes[own]
    meta[META_M] = m
    for c in copies:
        c.wait()


def gather_call(ids, table, groups, lengths, suffixes, cache, queries):
    bf16 = jnp.bfloat16
    anywhere = pl.BlockSpec(memory_space=pl.ANY)
    smem = pl.BlockSpec(memory_space=pltpu.SMEM)
    outs = (
        [jax.ShapeDtypeStruct((META_SIZE,), jnp.int32)]
        + [jax.ShapeDtypeStruct((2, PAIR, HD), bf16)] * 4
        + [jax.ShapeDtypeStruct((2, 2, PAIR, HD), bf16)] * 3
        + [jax.ShapeDtypeStruct((2, ROWS, WIDE), bf16)]
    )
    return pl.pallas_call(
        gather_kernel,
        out_shape=outs,
        in_specs=[smem] * 5 + [anywhere] * 2,
        out_specs=[smem] + [anywhere] * 8,
        scratch_shapes=[pltpu.SemaphoreType.DMA((42,))],
        cost_estimate=pl.CostEstimate(flops=0, bytes_accessed=5 << 20, transcendentals=0),
    )(ids, table, groups, lengths, suffixes, cache, queries)


def fold(q, keys, values_t, state, scales, masks):
    m_ref, l_ref, a_ref = state
    blocks = len(scales)
    for t in range(WIDE // TILE):
        cols = pl.ds(t * TILE, TILE)
        heads = TILE // ROWS
        rows = jnp.concatenate(
            [q[:, (t * heads + i) * HD : (t * heads + i + 1) * HD] for i in range(heads)], axis=0
        )
        scores = lax.dot_general(keys, rows, NT, preferred_element_type=jnp.float32)
        parts = [scores[b * BLK : (b + 1) * BLK] for b in range(blocks)]
        usable = [None if masks[b] is None else masks[b](t) for b in range(blocks)]
        before = m_ref[0, :, cols]
        highest = before
        for b in range(blocks):
            if usable[b] is not None:
                parts[b] = jnp.where(usable[b], parts[b], masked_score)
            highest = jnp.maximum(highest, jnp.max(parts[b], axis=0, keepdims=True) * scales[b][0])
        factor = jnp.exp2(before - highest)
        total = l_ref[0, :, cols] * factor
        rounded = []
        for b in range(blocks):
            weights = jnp.exp2(parts[b] * scales[b][0] - (highest - scales[b][1]))
            if usable[b] is not None:
                weights = jnp.where(usable[b], weights, 0.0)
            total = total + jnp.sum(weights, axis=0, keepdims=True) * scales[b][2]
            rounded.append(weights.astype(jnp.bfloat16))
        rounded = jnp.concatenate(rounded, axis=0) if blocks > 1 else rounded[0]
        product = jnp.dot(values_t, rounded, preferred_element_type=jnp.float32)
        a_ref[0, :, cols] = a_ref[0, :, cols] * factor + product
        m_ref[0, :, cols] = highest
        l_ref[0, :, cols] = total


def attend_kernel(plan, meta, scale, *refs):
    refs = list(refs)
    qa, qb = refs.pop(0), refs.pop(0)
    state_in = [refs.pop(0) for _ in range(3)] if not plan["first"] else None
    sources = [refs.pop(0) for _ in range(plan["n_sources"])]
    state = [refs.pop(0) for _ in range(3)] if not plan["last"] else None
    out = refs.pop(0) if plan["last"] else None
    kv, sems = refs.pop(0), refs.pop(0)
    if plan["last"]:
        state = [refs.pop(0) for _ in range(3)]
    slots = plan["slots"]
    pairs = plan["pairs"]
    step = pl.program_id(0)
    m = meta[META_M]
    side = step % 2
    which = step // 2
    slot = which + slots[0]
    head = m ^ (2 * slot)
    member = m ^ side
    length = meta[META_LEN]
    suffix = meta[META_SUF]
    live = member * ROWS < suffix
    reach = jnp.where(live, length, 0)

    def copies(w):
        return plan["copies"](meta, m, slots[w], sources, kv.at[w], sems.at[w])

    @pl.when(step == 0)
    def _():
        for w in range(len(slots)):
            for c in copies(w):
                c.start()

    for w in range(len(slots)):

        @pl.when(step == 2 * w)
        def _():
            for c in copies(w):
                c.wait()

    if plan["first"]:
        state[0][...] = jnp.full(state[0].shape, masked_score, jnp.float32)
        state[1][...] = jnp.zeros(state[1].shape, jnp.float32)
        state[2][...] = jnp.zeros(state[2].shape, jnp.float32)
    else:
        for a, b in zip(state, state_in):
            a[...] = b[...]

    def query():
        return jnp.where(side == 1, qb[0], qa[...])

    def scales_of(k, run):
        at = meta[META_SLOT + RUNS * k + run] * KVH + head
        return (scale[at], scale[512 + at], scale[1024 + at])

    if pairs:
        count = [
            [jnp.clip(reach - meta[META_J + RUNS * k + r] * BLK, 0, BLK) for r in range(RUNS)]
            for k in pairs
        ]
        least = functools.reduce(jnp.minimum, [n for c in count for n in c])

        @pl.when(least == BLK)
        def _():
            n = len(pairs) * PAIR
            fold(
                query(),
                kv[which, 0, :n],
                kv[which, 1, :n].T,
                state,
                [scales_of(k, r) for k in pairs for r in range(RUNS)],
                [None] * (RUNS * len(pairs)),
            )

        for at, k in enumerate(pairs):

            @pl.when((least < BLK) & (count[at][0] + count[at][1] > 0))
            def _():
                place = lax.broadcasted_iota(jnp.int32, (BLK, TILE), 0)
                rows = pl.ds(at * PAIR, PAIR)
                fold(
                    query(),
                    kv[which, 0, rows],
                    kv[which, 1, rows].T,
                    state,
                    [scales_of(k, r) for r in range(RUNS)],
                    [lambda t, n=count[at][r]: place < n for r in range(RUNS)],
                )

    if plan["suffix"]:
        unit = (jnp.float32(LOG2E / math.sqrt(HD)), jnp.float32(0.0), jnp.float32(1.0))
        base = len(pairs) * PAIR
        for v in range(4):

            @pl.when(live & (member == v))
            def _():
                n = (v + 1) * BLK

                def causal(t):
                    key = lax.broadcasted_iota(jnp.int32, (BLK, TILE), 0)
                    row = lax.broadcasted_iota(jnp.int32, (BLK, TILE), 1) % ROWS
                    return key <= row

                fold(
                    query(),
                    kv[which, 0, base : base + n],
                    kv[which, 1, base : base + n].T,
                    state,
                    [unit] * (v + 1),
                    [None] * v + [causal],
                )

    if plan["last"]:
        row = lax.broadcasted_iota(jnp.int32, (ROWS, HD), 0) + member * ROWS
        for i in range(PER):
            cols = pl.ds(i * ROWS, ROWS)
            piece = (state[2][0, :, cols] / state[1][0, :, cols]).T
            piece = jnp.where(row < suffix, piece, 0.0)
            out[0, :, i * HD : (i + 1) * HD] = piece.astype(jnp.bfloat16)


def attend_call(meta, scale, qa, qb, state, sources, *, copies, slots, pairs, suffix, last, keys):
    plan = dict(
        first=state is None,
        last=last,
        n_sources=len(sources),
        slots=slots,
        pairs=pairs,
        suffix=suffix,
        copies=copies,
    )
    low = slots[0]
    stat = pl.BlockSpec((1, 1, WIDE), lambda i, *_: (2 * low + i, 0, 0))
    accu = pl.BlockSpec((1, HD, WIDE), lambda i, *_: (2 * low + i, 0, 0))
    states = [stat, stat, accu]
    f32 = jnp.float32
    state_shapes = [
        jax.ShapeDtypeStruct((4, 1, WIDE), f32),
        jax.ShapeDtypeStruct((4, 1, WIDE), f32),
        jax.ShapeDtypeStruct((4, HD, WIDE), f32),
    ]
    in_specs = [
        pl.BlockSpec((ROWS, WIDE), lambda i, meta, scale: (0, meta[META_M] ^ (2 * (i // 2 + low)))),
        pl.BlockSpec((1, ROWS, WIDE), lambda i, *_: (i // 2 + low, 0, 0)),
    ]
    args = [qa, qb]
    if state is not None:
        in_specs += states
        args += list(state)
    in_specs += [pl.BlockSpec(memory_space=pl.ANY)] * len(sources)
    args += list(sources)
    scratch = [
        pltpu.VMEM((len(slots), 2, keys, HD), jnp.bfloat16),
        pltpu.SemaphoreType.DMA((len(slots), 8)),
    ]
    aliases = {}
    if last:
        out_specs = [pl.BlockSpec((1, ROWS, WIDE), lambda i, *_: (i, 0, 0))]
        out_shape = [jax.ShapeDtypeStruct((2 * len(slots), ROWS, WIDE), jnp.bfloat16)]
        scratch += [
            pltpu.VMEM((1, 1, WIDE), f32),
            pltpu.VMEM((1, 1, WIDE), f32),
            pltpu.VMEM((1, HD, WIDE), f32),
        ]
    else:
        out_specs = states
        out_shape = state_shapes
        if state is not None:
            aliases = {4 + i: i for i in range(3)}
    flops = 4 * HD * keys * WIDE * 2 * len(slots)
    return pl.pallas_call(
        functools.partial(attend_kernel, plan),
        out_shape=out_shape,
        grid_spec=pltpu.PrefetchScalarGridSpec(
            num_scalar_prefetch=2,
            grid=(2 * len(slots),),
            in_specs=in_specs,
            out_specs=out_specs,
            scratch_shapes=scratch,
        ),
        input_output_aliases=aliases,
        compiler_params=pltpu.CompilerParams(
            vmem_limit_bytes=VMEM_LIMIT, dimension_semantics=("arbitrary",)
        ),
        cost_estimate=pl.CostEstimate(
            flops=flops, bytes_accessed=6 << 20, transcendentals=keys * WIDE * 2 * len(slots)
        ),
    )(meta, scale, *args)


def own_copies(meta, m, slot, sources, kv, sems):
    cache = sources[0]
    head = m ^ (2 * slot)
    made = []
    for run in range(RUNS):
        local = meta[META_SLOT + run] % cache.shape[0]
        for half in range(2):
            column = pl.multiple_of((half * KVH + head) * HD, HD)
            made.append(
                pltpu.make_async_copy(
                    cache.at[local, :, pl.ds(column, HD)],
                    kv.at[half, pl.ds(run * BLK, BLK), :],
                    sems.at[2 * run + half],
                )
            )
    return made


def suffix_copies(meta, m, slot, sources, kv, sems, at=0, sem=0):
    rows = sources[-1]
    head = m ^ (2 * slot)
    return [
        pltpu.make_async_copy(
            rows.at[:, pl.ds(pl.multiple_of((half * KVH + head) * HD, HD), HD)],
            kv.at[half, pl.ds(at, rows.shape[0]), :],
            sems.at[sem + half],
        )
        for half in range(2)
    ]


def near_copies(meta, m, slot, sources, kv, sems):
    return [
        pltpu.make_async_copy(s.at[slot], kv.at[:, pl.ds(i * PAIR, PAIR), :], sems.at[i])
        for i, s in enumerate(sources)
    ]


def far_copies(meta, m, slot, sources, kv, sems):
    return [
        pltpu.make_async_copy(s, kv.at[:, pl.ds(i * PAIR, PAIR), :], sems.at[i])
        for i, s in enumerate(sources)
    ]


def join_kernel(ids, a, b, c, d, out, sems):
    m = ids[1]
    made = []
    for i, (ref, head) in enumerate([(a.at[0], m), (b.at[0], m ^ 2), (c, m ^ 1), (d, m ^ 3)]):
        column = pl.multiple_of(head * WIDE, WIDE)
        made.append(pltpu.make_async_copy(ref, out.at[:, pl.ds(column, WIDE)], sems.at[i]))
    for x in made:
        x.start()
    for x in made:
        x.wait()


def join_call(ids, a, b, c, d):
    anywhere = pl.BlockSpec(memory_space=pl.ANY)
    return pl.pallas_call(
        join_kernel,
        out_shape=jax.ShapeDtypeStruct((ROWS, QH * HD), jnp.bfloat16),
        in_specs=[pl.BlockSpec(memory_space=pltpu.SMEM)] + [anywhere] * 4,
        out_specs=anywhere,
        scratch_shapes=[pltpu.SemaphoreType.DMA((4,))],
        cost_estimate=pl.CostEstimate(flops=0, bytes_accessed=2 << 20, transcendentals=0),
    )(ids, a, b, c, d)


def permute(x, axis, count, k):
    return lax.ppermute(x, axis, [(i, i ^ k) for i in range(count)])


def per_device_small(
    queries, suffix_kv, cache, cache_scale, prefix_len, suffix_len, block_table, session_group
):
    ids = jnp.stack([lax.axis_index("pool"), lax.axis_index("blk")]).astype(jnp.int32)
    all_scale = lax.all_gather(cache_scale, "pool", axis=0, tiled=True).astype(jnp.float32)
    key_scale = all_scale[:, :KVH] * jnp.float32(LOG2E / math.sqrt(HD))
    value_scale = all_scale[:, KVH:]
    scale = jnp.stack([key_scale, jnp.log2(value_scale), 1.0 / value_scale]).reshape(-1)
    suffix_rows = lax.all_gather(suffix_kv, "blk", axis=0, tiled=True)

    meta, *parts = gather_call(
        ids, block_table, session_group, prefix_len, suffix_len, cache, queries
    )
    far, near, other_q = parts[:4], parts[4:7], parts[7]
    far_in = [permute(far[k - 4], "pool", POOL, k) for k in (4, 5, 6, 7)]
    near_in = [permute(near[k - 1], "pool", POOL, k) for k in (1, 2, 3)]
    qb = permute(other_q, "blk", 4, 1)
    far_across = [permute(x, "blk", 4, 2) for x in far_in]

    call = functools.partial(attend_call, meta, scale, queries, qb)
    state = call(
        None,
        [cache],
        copies=own_copies,
        slots=(0, 1),
        pairs=(0,),
        suffix=False,
        last=False,
        keys=PAIR,
    )
    state = call(
        state,
        near_in,
        copies=near_copies,
        slots=(0, 1),
        pairs=(1, 2, 3),
        suffix=False,
        last=False,
        keys=3 * PAIR,
    )
    state = call(
        state,
        [suffix_rows],
        copies=suffix_copies,
        slots=(0, 1),
        pairs=(),
        suffix=True,
        last=False,
        keys=4 * BLK,
    )
    outs = []
    for slot, sources in ((0, far_in), (1, far_across)):
        (done,) = call(
            state,
            sources,
            copies=far_copies,
            slots=(slot,),
            pairs=(4, 5, 6, 7),
            suffix=False,
            last=True,
            keys=4 * PAIR,
        )
        outs.append((done, permute(done[1], "blk", 4, 1)))
    return join_call(ids, outs[0][0], outs[1][0], outs[0][1], outs[1][1])

def fold_keys(running, query_heads, key_rows, value_rows, key_scale, value_scale, usable):
    highest, weight_sum, weighted = running
    scores = jnp.einsum("kgrd,nkd->kgrn", query_heads, key_rows, preferred_element_type=jnp.float32)
    scores = scores * jnp.transpose(key_scale)[:, None, None, :]
    scores = jnp.where(usable[None, None], scores, masked_score)
    new_highest = jnp.maximum(highest, jnp.max(scores, axis=3))
    weights = jnp.where(usable[None, None], jnp.exp(scores - new_highest[..., None]), 0.0)
    factor = jnp.exp(highest - new_highest)
    weight_sum = weight_sum * factor + jnp.sum(weights, axis=3)
    rounded = (weights * jnp.transpose(value_scale)[:, None, None, :]).astype(jnp.bfloat16)
    weighted = weighted * factor[..., None] + jnp.einsum(
        "kgrn,nkd->kgrd", rounded, value_rows, preferred_element_type=jnp.float32
    )
    return (new_highest, weight_sum, weighted)


def per_device_any(
    queries, suffix_kv, cache, cache_scale, prefix_len, suffix_len, block_table, session_group
):
    local_rows = queries.shape[0]
    kv_heads = KVH
    per_group = QH // KVH
    head_size = HD
    pool_count = lax.axis_size("pool")
    member_count = lax.axis_size("blk")
    pool_index = lax.axis_index("pool")
    member_index = lax.axis_index("blk")
    slot_count = cache.shape[0]
    block_size = cache.shape[1]
    session_count = block_table.shape[0]
    block_count = block_table.shape[1]
    run_count = block_count // pool_count
    inv_root = 1.0 / math.sqrt(head_size)
    chooser = (
        session_group[:, None] == jnp.arange(session_count, dtype=jnp.int32)[None, :]
    ).astype(jnp.int32)
    tables = jnp.sum(chooser[:, :, None] * block_table[None], axis=1)
    holders = (tables // slot_count).reshape(pool_count, run_count, pool_count)
    places = (tables % slot_count).reshape(pool_count, run_count, pool_count)
    send_slots = jnp.sum(jnp.where(holders == pool_index, places, 0), axis=2)
    own_choice = lax.dynamic_index_in_dim(chooser, pool_index, 0, keepdims=False)
    prefix_length = jnp.sum(own_choice * prefix_len)
    suffix_length = jnp.sum(own_choice * suffix_len)
    own_holders = lax.dynamic_index_in_dim(holders, pool_index, 0, keepdims=False)
    positions = jnp.arange(block_count, dtype=jnp.int32).reshape(run_count, pool_count)
    matches = own_holders[None, :, :] == jnp.arange(pool_count, dtype=jnp.int32)[:, None, None]
    block_place = jnp.sum(jnp.where(matches, positions[None], 0), axis=2)
    scale_rows = cache_scale[send_slots]
    split_cache = cache.reshape(slot_count, block_size, 2 * kv_heads, head_size)
    share_size = 2 * kv_heads // member_count
    outgoing = lax.dynamic_slice_in_dim(
        split_cache[send_slots], member_index * share_size, share_size, 3
    )
    arrived_part, arrived_scale = (
        lax.all_to_all(outgoing, "pool", split_axis=0, concat_axis=0, tiled=True),
        lax.all_to_all(scale_rows, "pool", split_axis=0, concat_axis=0, tiled=True),
    )
    arrived = lax.all_gather(arrived_part, "blk", axis=3, tiled=True)
    prefix_tokens = pool_count * run_count * block_size
    step_tokens = min(1024, prefix_tokens)
    step_count = prefix_tokens // step_tokens
    prefix_stack = arrived.reshape(step_count, step_tokens, 2, kv_heads, head_size)
    token_scale = jnp.broadcast_to(
        arrived_scale.astype(jnp.float32).reshape(pool_count, run_count, 1, 2, kv_heads),
        (pool_count, run_count, block_size, 2, kv_heads),
    ).reshape(step_count, step_tokens, 2, kv_heads)
    token_place = (
        block_place[:, :, None] * block_size
        + jnp.arange(block_size, dtype=jnp.int32)[None, None, :]
    ).reshape(step_count, step_tokens)
    query_heads = jnp.transpose(
        queries.reshape(local_rows, kv_heads, per_group, head_size), (1, 2, 0, 3)
    )
    row_place = member_index * local_rows + jnp.arange(local_rows, dtype=jnp.int32)
    initial = (
        jnp.full((kv_heads, per_group, local_rows), masked_score, jnp.float32),
        jnp.zeros((kv_heads, per_group, local_rows), jnp.float32),
        jnp.zeros((kv_heads, per_group, local_rows, head_size), jnp.float32),
    )
    shard_rows = lax.all_gather(suffix_kv, "blk", axis=0, tiled=True)
    piece_count = shard_rows.shape[0]
    split_rows = shard_rows.reshape(piece_count, 2, kv_heads, head_size)
    key_place = jnp.arange(piece_count, dtype=jnp.int32)
    usable = (key_place[None, :] <= row_place[:, None]) & (key_place[None, :] < suffix_length)
    flat_scale = jnp.full((piece_count, kv_heads), inv_root, jnp.float32)
    unit_scale = jnp.ones((piece_count, kv_heads), jnp.float32)
    running = fold_keys(
        initial, query_heads, split_rows[:, 0], split_rows[:, 1], flat_scale, unit_scale, usable
    )

    def prefix_step(running, step_inputs):
        token_rows, scale_step, place_rows = step_inputs
        usable = (place_rows < prefix_length)[None, :]
        updated = fold_keys(
            running,
            query_heads,
            token_rows[:, 0],
            token_rows[:, 1],
            scale_step[:, 0] * inv_root,
            scale_step[:, 1],
            usable,
        )
        return (updated, None)

    running, unused = lax.scan(prefix_step, running, (prefix_stack, token_scale, token_place))
    highest, weight_sum, weighted = running
    result = weighted / weight_sum[..., None]
    result = jnp.transpose(result, (2, 0, 1, 3)).reshape(local_rows, QH * head_size)
    result = jnp.where((row_place < suffix_length)[:, None], result, 0.0)
    return result.astype(jnp.bfloat16)


def solution(mesh):
    small = dict(mesh.shape) == {"pool": POOL, "blk": 4}
    return jax.shard_map(
        per_device_small if small else per_device_any,
        mesh=mesh,
        in_specs=(
            P(("pool", "blk"), None),
            P(("pool", "blk"), None),
            P("pool", None, None),
            P("pool", None),
            P(),
            P(),
            P(),
            P(),
        ),
        out_specs=P(("pool", "blk"), None),
        check_vma=False,
    )
```

```python
import functools
import math

import jax
import jax.numpy as jnp
from jax import lax
from jax.experimental import pallas as pl
from jax.experimental.pallas import tpu as pltpu
from jax.sharding import PartitionSpec as P

QH = 32
KVH = 4
HD = 128
PER = QH // KVH
LOG2E = math.log2(math.e)
INV_ROOT = 1.0 / math.sqrt(HD)

masked_score = -1e30

RUNS = 2
BLK = 128
PAIR = RUNS * BLK
PIECE = 2 * PAIR + 16
ROWS = 128
WIDE = PER * ROWS
POOL = 8
META_J = 0
META_LEN = 2 * POOL
META_SUF = META_LEN + 1
META_M = META_LEN + 2
META_SIZE = 24
TILE = 512
TOO_LARGE = 2.0**100
NT = (((1,), (1,)), ((), ()))
VMEM_LIMIT = 24 << 20
BF16 = jnp.bfloat16
F32 = jnp.float32
IN_VMEM = pl.BlockSpec(memory_space=pltpu.VMEM)
IN_SMEM = pl.BlockSpec(memory_space=pltpu.SMEM)
IN_HBM = pl.BlockSpec(memory_space=pltpu.HBM)


def find(table, session, run, holder, slot_count):
    low = holder * slot_count
    place = jnp.int32(0)
    local = jnp.int32(0)
    for jj in range(POOL):
        at = table[session, run * POOL + jj] - low
        hit = (at >= 0) & (at < slot_count)
        place = jnp.where(hit, run * POOL + jj, place)
        local = jnp.where(hit, at, local)
    return place, local


def write_scales(scales, locals_, head, dst):
    slot_at = lax.broadcasted_iota(jnp.int32, scales.shape, 0)
    col_at = lax.broadcasted_iota(jnp.int32, scales.shape, 1)
    row = lax.broadcasted_iota(jnp.int32, (16, HD), 0)
    rows = jnp.zeros((16, HD), F32)
    for half in range(2):
        for run in range(RUNS):
            chosen = (slot_at == locals_[run]) & (col_at == half * KVH + head)
            one = jnp.sum(jnp.where(chosen, scales, 0.0), axis=(0, 1), keepdims=True)
            rows = jnp.where(row == half * RUNS + run, one, rows)
    dst[pl.ds(2 * PAIR, 16), :] = rows.astype(BF16)


def piece_copies(cache, locals_, head, dst, sems, first):
    made = []
    for half in range(2):
        column = pl.multiple_of((half * KVH + head) * HD, HD)
        for run in range(RUNS):
            made.append(
                pltpu.make_async_copy(
                    cache.at[locals_[run], :, pl.ds(column, HD)],
                    dst.at[pl.ds(half * PAIR + run * BLK, BLK), :],
                    sems.at[first + 2 * half + run],
                )
            )
    return made


def far_kernel(ids, table, groups, lengths, suffixes, cache, cache_scale, *refs):
    meta = refs[0]
    outs = refs[1:5]
    stage, sems, out_sems = refs[5:]
    p = ids[0]
    m = ids[1]
    slot_count = cache.shape[0]
    scales = cache_scale[...].astype(F32)
    pending = []
    for i in range(4):
        session = groups[p ^ (4 + i)]
        locals_ = [find(table, session, run, p, slot_count)[1] for run in range(RUNS)]
        made = piece_copies(cache, locals_, m, stage.at[i], sems, 4 * i)
        for c in made:
            c.start()
        pending.append((locals_, made))
    leaving = []
    for i in range(4):
        locals_, made = pending[i]
        write_scales(scales, locals_, m, stage.at[i])
        for c in made:
            c.wait()
        out = pltpu.make_async_copy(stage.at[i], outs[i], out_sems.at[i])
        out.start()
        leaving.append(out)
    own = groups[p]
    for k in range(POOL):
        for run in range(RUNS):
            meta[META_J + RUNS * k + run] = find(table, own, run, p ^ k, slot_count)[0]
    meta[META_LEN] = lengths[own]
    meta[META_SUF] = suffixes[own]
    meta[META_M] = m
    for out in leaving:
        out.wait()


def far_call(ids, table, groups, lengths, suffixes, cache, cache_scale):
    return pl.pallas_call(
        far_kernel,
        out_shape=[jax.ShapeDtypeStruct((META_SIZE,), jnp.int32)]
        + [jax.ShapeDtypeStruct((PIECE, HD), BF16)] * 4,
        in_specs=[IN_SMEM] * 5 + [IN_HBM, IN_VMEM],
        out_specs=[IN_SMEM] + [IN_HBM] * 4,
        scratch_shapes=[
            pltpu.VMEM((4, PIECE, HD), BF16),
            pltpu.SemaphoreType.DMA((16,)),
            pltpu.SemaphoreType.DMA((4,)),
        ],
        compiler_params=pltpu.CompilerParams(vmem_limit_bytes=VMEM_LIMIT),
        cost_estimate=pl.CostEstimate(flops=0, bytes_accessed=4 << 20, transcendentals=0),
    )(ids, table, groups, lengths, suffixes, cache, cache_scale)


SWAP = WIDE + 2 * HD


def near_kernel(ids, table, groups, cache, cache_scale, queries, suffix_kv, *refs):
    near = refs[:3]
    swap, own, own_q, own_kv = refs[3:7]
    stage, swap_stage, sems, out_sems = refs[7:]
    p = ids[0]
    m = ids[1]
    slot_count = cache.shape[0]
    scales = cache_scale[...].astype(F32)
    swaps = []
    local_copies = []
    count = 32
    for slot in range(2):
        mine = m ^ (2 * slot)
        theirs = mine ^ 1
        jobs = [
            (queries, theirs * WIDE, WIDE, swap_stage.at[slot, :, pl.ds(0, WIDE)], swaps),
            (suffix_kv, theirs * HD, HD, swap_stage.at[slot, :, pl.ds(WIDE, HD)], swaps),
            (suffix_kv, (KVH + theirs) * HD, HD, swap_stage.at[slot, :, pl.ds(WIDE + HD, HD)], swaps),
            (queries, mine * WIDE, WIDE, own_q.at[slot], local_copies),
            (suffix_kv, mine * HD, HD, own_kv.at[slot, pl.ds(0, ROWS), :], local_copies),
            (suffix_kv, (KVH + mine) * HD, HD, own_kv.at[slot, pl.ds(ROWS, ROWS), :], local_copies),
        ]
        for src, at, width, dst, group in jobs:
            c = pltpu.make_async_copy(
                src.at[:, pl.ds(pl.multiple_of(at, HD), width)], dst, sems.at[count]
            )
            count += 1
            c.start()
            group.append(c)
    pending = []
    for i, k in enumerate((1, 2, 3, 0)):
        session = groups[p ^ k]
        locals_ = [find(table, session, run, p, slot_count)[1] for run in range(RUNS)]
        made = []
        for slot in range(2):
            dst = own.at[slot] if k == 0 else stage.at[i, slot]
            made += piece_copies(cache, locals_, m ^ (2 * slot), dst, sems, 8 * i + 4 * slot)
        for c in made:
            c.start()
        pending.append((k, locals_, made))
    for c in swaps:
        c.wait()
    leaving = [pltpu.make_async_copy(swap_stage, swap, out_sems.at[3])]
    leaving[0].start()
    for i, (k, locals_, made) in enumerate(pending):
        for slot in range(2):
            dst = own.at[slot] if k == 0 else stage.at[i, slot]
            write_scales(scales, locals_, m ^ (2 * slot), dst)
        for c in made:
            c.wait()
        if k:
            out = pltpu.make_async_copy(stage.at[i], near[i], out_sems.at[i])
            out.start()
            leaving.append(out)
    for c in local_copies:
        c.wait()
    for out in leaving:
        out.wait()


def near_call(ids, table, groups, cache, cache_scale, queries, suffix_kv):
    return pl.pallas_call(
        near_kernel,
        out_shape=[jax.ShapeDtypeStruct((2, PIECE, HD), BF16)] * 3
        + [
            jax.ShapeDtypeStruct((2, ROWS, SWAP), BF16),
            pltpu.VMEM((2, PIECE, HD), BF16),
            pltpu.VMEM((2, ROWS, WIDE), BF16),
            pltpu.VMEM((2, 2 * ROWS, HD), BF16),
        ],
        in_specs=[IN_SMEM] * 3 + [IN_HBM, IN_VMEM, IN_HBM, IN_HBM],
        out_specs=[IN_HBM] * 4 + [IN_VMEM] * 3,
        scratch_shapes=[
            pltpu.VMEM((3, 2, PIECE, HD), BF16),
            pltpu.VMEM((2, ROWS, SWAP), BF16),
            pltpu.SemaphoreType.DMA((44,)),
            pltpu.SemaphoreType.DMA((4,)),
        ],
        compiler_params=pltpu.CompilerParams(vmem_limit_bytes=VMEM_LIMIT),
        cost_estimate=pl.CostEstimate(flops=0, bytes_accessed=6 << 20, transcendentals=0),
    )(ids, table, groups, cache, cache_scale, queries, suffix_kv)


def wide(row):
    return jnp.concatenate([row] * (TILE // HD), axis=1)


def terms(tile, run):
    key = tile[run : run + 1]
    value = tile[RUNS + run : RUNS + run + 1]
    return wide(key * (LOG2E * INV_ROOT)), wide(jnp.log2(value)), wide(1.0 / value)


UNIT = None


def fold(q, keys, values_t, before, after, side, blocks, exact):
    (m0, l0, a0), (m1, l1, a1) = before, after
    for t in range(WIDE // TILE):
        cols = pl.ds(t * TILE, TILE)
        scores = lax.dot_general(
            keys, q[pl.ds(t * TILE, TILE), :], NT, preferred_element_type=F32
        )
        reference = m0[side, :, cols]
        total = l0[side, :, cols]
        weighted = a0[side, :, cols]
        parts = []
        for b, (term, dead, mask) in enumerate(blocks):
            part = scores[b * BLK : (b + 1) * BLK]
            part = part * (LOG2E * INV_ROOT) if term is UNIT else part * term[0]
            if mask is not None:
                part = jnp.where(mask, part, masked_score)
            parts.append(part)
        if exact:
            old = reference
            for part, (term, dead, mask) in zip(parts, blocks):
                top = jnp.max(part, axis=0, keepdims=True)
                if dead is not None:
                    top = jnp.where(dead, masked_score, top)
                reference = jnp.maximum(reference, top)
            factor = jnp.exp2(old - reference)
            total = total * factor
            weighted = weighted * factor
        rounded = []
        for part, (term, dead, mask) in zip(parts, blocks):
            shift = reference if term is UNIT else reference - term[1]
            if dead is not None:
                shift = jnp.where(dead, -masked_score, shift)
            weights = jnp.exp2(part - shift)
            if mask is not None:
                weights = jnp.where(mask, weights, 0.0)
            summed = jnp.sum(weights, axis=0, keepdims=True)
            total = total + (summed if term is UNIT else summed * term[2])
            rounded.append(weights.astype(BF16))
        rounded = jnp.concatenate(rounded, axis=0) if len(rounded) > 1 else rounded[0]
        product = jnp.dot(values_t, rounded, preferred_element_type=F32)
        a1[side, :, cols] = weighted + product
        l1[side, :, cols] = total
        m1[side, :, cols] = reference


def add_pieces(q_all, slot, before, after, pieces, ks, meta, exact=True):
    m = meta[META_M]
    n = len(ks)

    def one_side(side):
        member = m ^ side
        reach = jnp.where(member * ROWS < meta[META_SUF], meta[META_LEN], 0)
        counts = [
            jnp.clip(reach - meta[META_J + RUNS * k + r] * BLK, 0, BLK)
            for k in ks
            for r in range(RUNS)
        ]
        most = functools.reduce(jnp.maximum, counts)
        q = q_all.at[2 * slot + side]
        own_before = before
        keep = [(a, b) for a, b in zip(before, after)]

        @pl.when(most < BLK)
        def _():
            for a, b in keep:
                b[side] = a[side]

        @pl.when(most == BLK)
        def _():
            blocks = []
            for i in range(n):
                tile = pieces[i, 2 * PAIR :, :].astype(F32)
                blocks += [(terms(tile, r), counts[RUNS * i + r] < BLK, None) for r in range(RUNS)]
            keys = [pieces[i, :PAIR, :] for i in range(n)]
            values = [pieces[i, PAIR : 2 * PAIR, :].T for i in range(n)]
            fold(
                q,
                jnp.concatenate(keys, axis=0) if n > 1 else keys[0],
                jnp.concatenate(values, axis=1) if n > 1 else values[0],
                own_before,
                after,
                side,
                blocks,
                exact,
            )

        def single(i, run, count, exact):
            tile = pieces[i, 2 * PAIR :, :].astype(F32)
            factor, shift, inverse = terms(tile, 0)
            factor1, shift1, inverse1 = terms(tile, 1)
            pick = lambda a, b: jnp.where(run == 1, b, a)
            term = (pick(factor, factor1), pick(shift, shift1), pick(inverse, inverse1))
            mask = lax.broadcasted_iota(jnp.int32, (BLK, TILE), 0) < count
            at = pl.multiple_of(run * BLK, BLK)
            fold(
                q,
                pieces[i, pl.ds(at, BLK), :],
                pieces[i, pl.ds(PAIR + at, BLK), :].T,
                after,
                after,
                side,
                [(term, None, mask)],
                exact,
            )

        part = jnp.int32(-1)
        part_count = jnp.int32(0)
        for at, count in enumerate(counts):
            hit = (count > 0) & (count < BLK)
            part = jnp.where(hit, at, part)
            part_count = jnp.where(hit, count, part_count)

        @pl.when(part >= 0)
        def _():
            single(part // RUNS, part % RUNS, part_count, exact)

        if exact:
            return
        fine = jnp.max(after[1][side]) < TOO_LARGE

        @pl.when(jnp.logical_not(fine))
        def _():
            for a, b in keep:
                b[side] = a[side]

            def body(at, carry):
                count = jnp.int32(0)
                for j, c in enumerate(counts):
                    count = jnp.where(at == j, c, count)

                @pl.when(count > 0)
                def _():
                    single(at // RUNS, at % RUNS, count, True)

                return carry

            lax.fori_loop(0, len(counts), body, 0)

    def body(side, carry):
        one_side(side)
        return carry

    lax.fori_loop(0, 2, body, 0)


def state_shapes(slots):
    one = [
        pltpu.VMEM((2, 1, WIDE), F32),
        pltpu.VMEM((2, 1, WIDE), F32),
        pltpu.VMEM((2, HD, WIDE), F32),
    ]
    return one * slots


def own_kernel(meta, swap, own, own_q, own_kv, *refs):
    q_all = refs[0]
    states = [refs[1:4], refs[4:7]]
    firsts = [refs[7:10], refs[10:13]]
    other, kv, sem = refs[13:]
    c = pltpu.make_async_copy(swap, other, sem)
    c.start()
    m = meta[META_M]
    for slot in range(2):
        for h in range(PER):
            q_all[2 * slot, h * ROWS : (h + 1) * ROWS, :] = own_q[slot, :, h * HD : (h + 1) * HD]
        kv[slot, 0] = own_kv[slot]
    c.wait()
    for slot in range(2):
        for h in range(PER):
            q_all[2 * slot + 1, h * ROWS : (h + 1) * ROWS, :] = other[
                slot, :, h * HD : (h + 1) * HD
            ]
        kv[slot, 1, :ROWS, :] = other[slot, :, WIDE : WIDE + HD]
        kv[slot, 1, ROWS:, :] = other[slot, :, WIDE + HD :]
    key = lax.broadcasted_iota(jnp.int32, (BLK, TILE), 0)
    row = lax.broadcasted_iota(jnp.int32, (BLK, TILE), 1) % ROWS
    for slot in range(2):
        first = firsts[slot]
        first[0][...] = jnp.full(first[0].shape, masked_score, F32)
        first[1][...] = jnp.zeros(first[1].shape, F32)
        first[2][...] = jnp.zeros(first[2].shape, F32)

        def body(side, carry):
            odd = ((m ^ side) % 2) == 1
            keys = jnp.concatenate([kv[slot, side, :ROWS], kv[slot, 1 - side, :ROWS]], axis=0)
            values = jnp.concatenate(
                [kv[slot, side, ROWS:].T, kv[slot, 1 - side, ROWS:].T], axis=1
            )
            fold(
                q_all.at[2 * slot + side],
                keys,
                values,
                first,
                first,
                side,
                [(UNIT, None, key <= row), (UNIT, jnp.logical_not(odd), None)],
                True,
            )
            return carry

        lax.fori_loop(0, 2, body, 0)
        add_pieces(q_all, slot, first, states[slot], own.at[pl.ds(slot, 1)], (0,), meta)


def own_call(meta, swap, own, own_q, own_kv):
    out = pl.pallas_call(
        own_kernel,
        out_shape=[pltpu.VMEM((4, WIDE, HD), BF16)] + state_shapes(2),
        in_specs=[IN_SMEM, IN_HBM, IN_VMEM, IN_VMEM, IN_VMEM],
        out_specs=[IN_VMEM] * 7,
        scratch_shapes=state_shapes(2)
        + [
            pltpu.VMEM((2, ROWS, SWAP), BF16),
            pltpu.VMEM((2, 2, 2 * ROWS, HD), BF16),
            pltpu.SemaphoreType.DMA,
        ],
        compiler_params=pltpu.CompilerParams(vmem_limit_bytes=VMEM_LIMIT),
        cost_estimate=pl.CostEstimate(
            flops=8 * HD * PAIR * WIDE * 2, bytes_accessed=1 << 20, transcendentals=8 * PAIR * WIDE
        ),
    )(meta, swap, own, own_q, own_kv)
    return out[0], [tuple(out[1:4]), tuple(out[4:7])]


def add_kernel(slots, ks, last, meta, q_all, *refs):
    refs = list(refs)
    take = lambda n: [refs.pop(0) for _ in range(n)]
    before = [take(3) for _ in slots]
    sources = take(len(ks))
    after = None if last else [take(3) for _ in slots]
    outs = take(2 * len(slots)) if last else None
    kv, sems = take(2)
    if last:
        after = [take(3) for _ in slots]
    copies = []
    for w, slot in enumerate(slots):
        made = []
        for i, s in enumerate(sources):
            src = s.at[slot] if len(s.shape) == 3 else s
            c = pltpu.make_async_copy(src, kv.at[w, i], sems.at[w, i])
            c.start()
            made.append(c)
        copies.append(made)
    for w, slot in enumerate(slots):
        for c in copies[w]:
            c.wait()
        add_pieces(q_all, slot, before[w], after[w], kv.at[w], ks, meta)
        if last:
            for side in range(2):
                member = meta[META_M] ^ side
                row = lax.broadcasted_iota(jnp.int32, (ROWS, HD), 0) + member * ROWS
                for i in range(PER):
                    cols = pl.ds(i * ROWS, ROWS)
                    piece = (after[w][2][side, :, cols] / after[w][1][side, :, cols]).T
                    piece = jnp.where(row < meta[META_SUF], piece, 0.0)
                    outs[2 * w + side][:, i * HD : (i + 1) * HD] = piece.astype(BF16)


def add_call(meta, q_all, states, sources, slots, ks, last=False):
    flat = [x for s in slots for x in states[s]]
    n = len(ks)
    scratch = [
        pltpu.VMEM((len(slots), n, PIECE, HD), BF16),
        pltpu.SemaphoreType.DMA((len(slots), n)),
    ]
    if last:
        out_shape = [
            pltpu.VMEM((ROWS, WIDE), BF16),
            jax.ShapeDtypeStruct((ROWS, WIDE), BF16),
        ] * len(slots)
        out_specs = [IN_VMEM] * (2 * len(slots))
        scratch += state_shapes(len(slots))
    else:
        out_shape = state_shapes(len(slots))
        out_specs = [IN_VMEM] * (3 * len(slots))
    work = len(slots) * 2 * n * PAIR * WIDE
    out = pl.pallas_call(
        functools.partial(add_kernel, slots, ks, last),
        out_shape=out_shape,
        in_specs=[IN_SMEM, IN_VMEM] + [IN_VMEM] * len(flat) + [IN_HBM] * n,
        out_specs=out_specs,
        scratch_shapes=scratch,
        compiler_params=pltpu.CompilerParams(vmem_limit_bytes=VMEM_LIMIT),
        cost_estimate=pl.CostEstimate(
            flops=4 * HD * work, bytes_accessed=1 << 20, transcendentals=work
        ),
    )(meta, q_all, *flat, *sources)
    if last:
        return out
    states = list(states)
    for w, slot in enumerate(slots):
        states[slot] = tuple(out[3 * w : 3 * w + 3])
    return states


def early_kernel(meta, q_all, *refs):
    before = [refs[0:3], refs[3:6]]
    rows = refs[6]
    after = [refs[7:10], refs[10:13]]
    kv, sems = refs[13:]
    m = meta[META_M]

    @pl.when(m < 2)
    def _():
        for a, b in zip(before[0] + before[1], after[0] + after[1]):
            b[...] = a[...]

    @pl.when(m >= 2)
    def _():
        copies = []
        for slot in range(2):
            for half in range(2):
                column = pl.multiple_of((half * KVH + (m ^ (2 * slot))) * HD, HD)
                c = pltpu.make_async_copy(
                    rows.at[pl.ds(0, PAIR), pl.ds(column, HD)], kv.at[slot, half], sems.at[slot, half]
                )
                c.start()
                copies.append(c)
        for c in copies:
            c.wait()
        for slot in range(2):

            def body(side, carry):
                blocks = [(UNIT, None, None)] * 2
                args = (q_all.at[2 * slot + side], kv[slot, 0], kv[slot, 1].T)
                fold(*args, before[slot], after[slot], side, blocks, True)
                return carry

            lax.fori_loop(0, 2, body, 0)


def early_call(meta, q_all, states, rows):
    work = 4 * PAIR * WIDE
    out = pl.pallas_call(
        early_kernel,
        out_shape=state_shapes(2),
        in_specs=[IN_SMEM] + [IN_VMEM] * 7 + [IN_HBM],
        out_specs=[IN_VMEM] * 6,
        scratch_shapes=[
            pltpu.VMEM((2, 2, PAIR, HD), BF16),
            pltpu.SemaphoreType.DMA((2, 2)),
        ],
        compiler_params=pltpu.CompilerParams(vmem_limit_bytes=VMEM_LIMIT),
        cost_estimate=pl.CostEstimate(
            flops=4 * HD * work, bytes_accessed=1 << 20, transcendentals=work
        ),
    )(meta, q_all, *states[0], *states[1], rows)
    return [tuple(out[:3]), tuple(out[3:])]


def join_kernel(ids, a, b, c, d, out, stage, sems, out_sems):
    m = ids[1]
    heads = [m, m ^ 2, m ^ 1, m ^ 3]
    incoming = [pltpu.make_async_copy(x, stage.at[i], sems.at[i]) for i, x in enumerate((c, d))]
    for x in incoming:
        x.start()
    leaving = []
    for i, src in enumerate((a, b, stage.at[0], stage.at[1])):
        if i >= 2:
            incoming[i - 2].wait()
        column = pl.multiple_of(heads[i] * WIDE, WIDE)
        x = pltpu.make_async_copy(src, out.at[:, pl.ds(column, WIDE)], out_sems.at[i])
        x.start()
        leaving.append(x)
    for x in leaving:
        x.wait()


def join_call(ids, a, b, c, d):
    return pl.pallas_call(
        join_kernel,
        out_shape=jax.ShapeDtypeStruct((ROWS, QH * HD), BF16),
        in_specs=[IN_SMEM, IN_VMEM, IN_VMEM, IN_HBM, IN_HBM],
        out_specs=IN_HBM,
        scratch_shapes=[
            pltpu.VMEM((2, ROWS, WIDE), BF16),
            pltpu.SemaphoreType.DMA((2,)),
            pltpu.SemaphoreType.DMA((4,)),
        ],
        cost_estimate=pl.CostEstimate(flops=0, bytes_accessed=2 << 20, transcendentals=0),
    )(ids, a, b, c, d)


def permute(x, axis, count, k):
    return lax.ppermute(x, axis, [(i, i ^ k) for i in range(count)])


def per_device_small(
    queries, suffix_kv, cache, cache_scale, prefix_len, suffix_len, block_table, session_group
):
    ids = jnp.stack([lax.axis_index("pool"), lax.axis_index("blk")]).astype(jnp.int32)
    suffix_rows = lax.all_gather(suffix_kv, "blk", axis=0, tiled=True)
    meta, *far = far_call(
        ids, block_table, session_group, prefix_len, suffix_len, cache, cache_scale
    )
    far_in = {k: permute(far[k - 4], "pool", POOL, k) for k in (4, 5, 6, 7)}
    *near, swap, own, own_q, own_kv = near_call(
        ids, block_table, session_group, cache, cache_scale, queries, suffix_kv
    )
    swap_in = permute(swap, "blk", 4, 1)
    near_in = [permute(near[k - 1], "pool", POOL, k) for k in (1, 2, 3)]
    across = {k: permute(far_in[k], "blk", 4, 2) for k in (4, 5, 6, 7)}

    q_all, states = own_call(meta, swap_in, own, own_q, own_kv)
    states = add_call(meta, q_all, states, near_in, (0, 1), (1, 2, 3))
    states = early_call(meta, q_all, states, suffix_rows)
    states = add_call(meta, q_all, states, [far_in[4], far_in[5]], (0,), (4, 5))
    states = add_call(meta, q_all, states, [across[4], across[5]], (1,), (4, 5))
    mine, yours = [], []
    for slot, source in ((0, far_in), (1, across)):
        a, b = add_call(meta, q_all, states, [source[6], source[7]], (slot,), (6, 7), last=True)
        mine.append(a)
        yours.append(permute(b, "blk", 4, 1))
    return join_call(ids, mine[0], mine[1], yours[0], yours[1])


def fold_keys(running, query_heads, key_rows, value_rows, key_scale, value_scale, usable):
    highest, weight_sum, weighted = running
    scores = jnp.einsum("kgrd,nkd->kgrn", query_heads, key_rows, preferred_element_type=jnp.float32)
    scores = scores * jnp.transpose(key_scale)[:, None, None, :]
    scores = jnp.where(usable[None, None], scores, masked_score)
    new_highest = jnp.maximum(highest, jnp.max(scores, axis=3))
    weights = jnp.where(usable[None, None], jnp.exp(scores - new_highest[..., None]), 0.0)
    factor = jnp.exp(highest - new_highest)
    weight_sum = weight_sum * factor + jnp.sum(weights, axis=3)
    rounded = (weights * jnp.transpose(value_scale)[:, None, None, :]).astype(jnp.bfloat16)
    weighted = weighted * factor[..., None] + jnp.einsum(
        "kgrn,nkd->kgrd", rounded, value_rows, preferred_element_type=jnp.float32
    )
    return (new_highest, weight_sum, weighted)


def per_device_any(
    queries, suffix_kv, cache, cache_scale, prefix_len, suffix_len, block_table, session_group
):
    local_rows = queries.shape[0]
    kv_heads = KVH
    per_group = QH // KVH
    head_size = HD
    pool_count = lax.axis_size("pool")
    member_count = lax.axis_size("blk")
    pool_index = lax.axis_index("pool")
    member_index = lax.axis_index("blk")
    slot_count = cache.shape[0]
    block_size = cache.shape[1]
    session_count = block_table.shape[0]
    block_count = block_table.shape[1]
    run_count = block_count // pool_count
    inv_root = 1.0 / math.sqrt(head_size)
    chooser = (
        session_group[:, None] == jnp.arange(session_count, dtype=jnp.int32)[None, :]
    ).astype(jnp.int32)
    tables = jnp.sum(chooser[:, :, None] * block_table[None], axis=1)
    holders = (tables // slot_count).reshape(pool_count, run_count, pool_count)
    places = (tables % slot_count).reshape(pool_count, run_count, pool_count)
    send_slots = jnp.sum(jnp.where(holders == pool_index, places, 0), axis=2)
    own_choice = lax.dynamic_index_in_dim(chooser, pool_index, 0, keepdims=False)
    prefix_length = jnp.sum(own_choice * prefix_len)
    suffix_length = jnp.sum(own_choice * suffix_len)
    own_holders = lax.dynamic_index_in_dim(holders, pool_index, 0, keepdims=False)
    positions = jnp.arange(block_count, dtype=jnp.int32).reshape(run_count, pool_count)
    matches = own_holders[None, :, :] == jnp.arange(pool_count, dtype=jnp.int32)[:, None, None]
    block_place = jnp.sum(jnp.where(matches, positions[None], 0), axis=2)
    scale_rows = cache_scale[send_slots]
    split_cache = cache.reshape(slot_count, block_size, 2 * kv_heads, head_size)
    share_size = 2 * kv_heads // member_count
    outgoing = lax.dynamic_slice_in_dim(
        split_cache[send_slots], member_index * share_size, share_size, 3
    )
    arrived_part, arrived_scale = (
        lax.all_to_all(outgoing, "pool", split_axis=0, concat_axis=0, tiled=True),
        lax.all_to_all(scale_rows, "pool", split_axis=0, concat_axis=0, tiled=True),
    )
    arrived = lax.all_gather(arrived_part, "blk", axis=3, tiled=True)
    prefix_tokens = pool_count * run_count * block_size
    step_tokens = min(1024, prefix_tokens)
    step_count = prefix_tokens // step_tokens
    prefix_stack = arrived.reshape(step_count, step_tokens, 2, kv_heads, head_size)
    token_scale = jnp.broadcast_to(
        arrived_scale.astype(jnp.float32).reshape(pool_count, run_count, 1, 2, kv_heads),
        (pool_count, run_count, block_size, 2, kv_heads),
    ).reshape(step_count, step_tokens, 2, kv_heads)
    token_place = (
        block_place[:, :, None] * block_size
        + jnp.arange(block_size, dtype=jnp.int32)[None, None, :]
    ).reshape(step_count, step_tokens)
    query_heads = jnp.transpose(
        queries.reshape(local_rows, kv_heads, per_group, head_size), (1, 2, 0, 3)
    )
    row_place = member_index * local_rows + jnp.arange(local_rows, dtype=jnp.int32)
    initial = (
        jnp.full((kv_heads, per_group, local_rows), masked_score, jnp.float32),
        jnp.zeros((kv_heads, per_group, local_rows), jnp.float32),
        jnp.zeros((kv_heads, per_group, local_rows, head_size), jnp.float32),
    )
    shard_rows = lax.all_gather(suffix_kv, "blk", axis=0, tiled=True)
    piece_count = shard_rows.shape[0]
    split_rows = shard_rows.reshape(piece_count, 2, kv_heads, head_size)
    key_place = jnp.arange(piece_count, dtype=jnp.int32)
    usable = (key_place[None, :] <= row_place[:, None]) & (key_place[None, :] < suffix_length)
    flat_scale = jnp.full((piece_count, kv_heads), inv_root, jnp.float32)
    unit_scale = jnp.ones((piece_count, kv_heads), jnp.float32)
    running = fold_keys(
        initial, query_heads, split_rows[:, 0], split_rows[:, 1], flat_scale, unit_scale, usable
    )

    def prefix_step(running, step_inputs):
        token_rows, scale_step, place_rows = step_inputs
        usable = (place_rows < prefix_length)[None, :]
        updated = fold_keys(
            running,
            query_heads,
            token_rows[:, 0],
            token_rows[:, 1],
            scale_step[:, 0] * inv_root,
            scale_step[:, 1],
            usable,
        )
        return (updated, None)

    running, unused = lax.scan(prefix_step, running, (prefix_stack, token_scale, token_place))
    highest, weight_sum, weighted = running
    result = weighted / weight_sum[..., None]
    result = jnp.transpose(result, (2, 0, 1, 3)).reshape(local_rows, QH * head_size)
    result = jnp.where((row_place < suffix_length)[:, None], result, 0.0)
    return result.astype(jnp.bfloat16)


def solution(mesh):
    small = dict(mesh.shape) == {"pool": POOL, "blk": 4}
    return jax.shard_map(
        per_device_small if small else per_device_any,
        mesh=mesh,
        in_specs=(
            P(("pool", "blk"), None),
            P(("pool", "blk"), None),
            P("pool", None, None),
            P("pool", None),
            P(),
            P(),
            P(),
            P(),
        ),
        out_specs=P(("pool", "blk"), None),
        check_vma=False,
    )
```

```python
import functools
import math

import jax
import jax.numpy as jnp
from jax import lax
from jax.experimental import pallas as pl
from jax.experimental.pallas import tpu as pltpu
from jax.sharding import PartitionSpec as P

QH = 32
KVH = 4
HD = 128
PER = QH // KVH
LOG2E = math.log2(math.e)
INV_ROOT = 1.0 / math.sqrt(HD)

masked_score = -1e30

RUNS = 2
BLK = 128
PAIR = RUNS * BLK
PIECE = 2 * PAIR + 16
ROWS = 128
WIDE = PER * ROWS
BOTH = 2 * WIDE
REF_ROW = HD
SUM_ROW = HD + 8
STATE = HD + 16
POOL = 8
META_J = 0
META_LEN = 2 * POOL
META_SUF = META_LEN + 1
META_M = META_LEN + 2
META_SEND = 24
META_SIZE = META_SEND + 2 * POOL
TILE = 512
NT = (((1,), (1,)), ((), ()))
VMEM_LIMIT = 24 << 20
BF16 = jnp.bfloat16
F32 = jnp.float32
IN_VMEM = pl.BlockSpec(memory_space=pltpu.VMEM)
IN_SMEM = pl.BlockSpec(memory_space=pltpu.SMEM)
IN_HBM = pl.BlockSpec(memory_space=pltpu.HBM)


COST = pl.CostEstimate(flops=1 << 10, bytes_accessed=1 << 10, transcendentals=0)


def write_scales(scales, locals_, head, dst):
    col_at = lax.broadcasted_iota(jnp.int32, scales.shape, 0)
    slot_at = lax.broadcasted_iota(jnp.int32, scales.shape, 1)
    row = lax.broadcasted_iota(jnp.int32, (16, HD), 0)
    rows = jnp.zeros((16, HD), F32)
    for half in range(2):
        for run in range(RUNS):
            chosen = (slot_at == locals_[run]) & (col_at == half * KVH + head)
            one = jnp.sum(jnp.where(chosen, scales, 0.0), axis=(0, 1), keepdims=True)
            rows = jnp.where(row == half * RUNS + run, one, rows)
    dst[pl.ds(2 * PAIR, 16), :] = rows.astype(BF16)


def piece_copies(cache, locals_, head, dst, sems, first):
    made = []
    for half in range(2):
        column = pl.multiple_of((half * KVH + head) * HD, HD)
        for run in range(RUNS):
            made.append(
                pltpu.make_async_copy(
                    cache.at[locals_[run], :, pl.ds(column, HD)],
                    dst.at[pl.ds(half * PAIR + run * BLK, BLK), :],
                    sems.at[first + 2 * half + run],
                )
            )
    return made


def gather_pieces(meta, cache, cache_scale, jobs, sems):
    m = meta[META_M]
    pending = []
    count = 0
    for k, slots, refs in jobs:
        locals_ = [meta[META_SEND + RUNS * k + run] for run in range(RUNS)]
        made = []
        for slot, ref in zip(slots, refs):
            made += piece_copies(cache, locals_, m ^ (2 * slot), ref, sems, count)
            count += 4
        for c in made:
            c.start()
        pending.append((slots, refs, locals_, made))
    scales = cache_scale[...].astype(F32)
    for slots, refs, locals_, _ in pending:
        for slot, ref in zip(slots, refs):
            write_scales(scales, locals_, m ^ (2 * slot), ref)
    return [made for _, _, _, made in pending]


def leave(stages, outs, waits, sems):
    made = []
    for i, (stage, out) in enumerate(zip(stages, outs)):
        for c in waits[i]:
            c.wait()
        c = pltpu.make_async_copy(stage, out, sems.at[i])
        c.start()
        made.append(c)
    return made


def far_kernel(ids, table_, groups_, lengths_, suffixes_, cache, cache_scale, *refs):
    meta, out4, out5, stage, table, groups, lengths, suffixes, table_sems, sems, out_sems = refs
    loads = [
        pltpu.make_async_copy(a, b, table_sems.at[i])
        for i, (a, b) in enumerate(
            [(table_, table), (groups_, groups), (lengths_, lengths), (suffixes_, suffixes)]
        )
    ]
    for c in loads:
        c.start()
    for c in loads:
        c.wait()
    p = ids[0]
    meta[META_M] = ids[1]
    slot_count = cache.shape[0]
    low = p * slot_count

    def send_slots(k):
        session = groups[p ^ k]
        for run in range(RUNS):
            local = jnp.int32(0)
            for jj in range(POOL):
                at = table[session, run * POOL + jj] - low
                local = jnp.where((at >= 0) & (at < slot_count), at, local)
            meta[META_SEND + RUNS * k + run] = local

    send_slots(4)
    send_slots(5)
    jobs = [(4, (0,), (stage.at[0],)), (5, (0,), (stage.at[1],))]
    waits = gather_pieces(meta, cache, cache_scale, jobs, sems)
    own = groups[p]
    for run in range(RUNS):
        for jj in range(POOL):
            at = run * POOL + jj
            meta[META_J + RUNS * ((table[own, at] // slot_count) ^ p) + run] = at
    meta[META_LEN] = lengths[own]
    meta[META_SUF] = suffixes[own]
    leaving = leave([stage.at[0], stage.at[1]], [out4, out5], waits, out_sems)
    for k in (0, 1, 2, 3, 6, 7):
        send_slots(k)
    for out in leaving:
        out.wait()


PIECE_1 = jax.ShapeDtypeStruct((PIECE, HD), BF16)
PIECE_2 = jax.ShapeDtypeStruct((2, PIECE, HD), BF16)


def far_call(ids, table, groups, lengths, suffixes, cache, cache_scale):
    return pl.pallas_call(
        far_kernel,
        out_shape=[jax.ShapeDtypeStruct((META_SIZE,), jnp.int32), PIECE_1, PIECE_1],
        in_specs=[IN_SMEM] + [IN_HBM] * 5 + [IN_VMEM],
        out_specs=[IN_SMEM] + [IN_HBM] * 2,
        scratch_shapes=[
            pltpu.VMEM((2, PIECE, HD), BF16),
            pltpu.SMEM(table.shape, jnp.int32),
            pltpu.SMEM(groups.shape, jnp.int32),
            pltpu.SMEM(lengths.shape, jnp.int32),
            pltpu.SMEM(suffixes.shape, jnp.int32),
            pltpu.SemaphoreType.DMA((4,)),
            pltpu.SemaphoreType.DMA((8,)),
            pltpu.SemaphoreType.DMA((2,)),
        ],
        compiler_params=pltpu.CompilerParams(vmem_limit_bytes=VMEM_LIMIT),
        cost_estimate=COST,
    )(ids, table, groups, lengths, suffixes, cache, cache_scale)


SWAP = WIDE + 2 * HD


def near_kernel(meta, cache, cache_scale, queries, suffix_kv, *refs):
    out6, out1, swap, own, own_q, own_kv = refs[:6]
    stage6, stage1, swap_stage, sems, swap_sems, own_sems, out_sems = refs[6:]
    m = meta[META_M]
    swaps = []
    mine_copies = []
    for slot in range(2):
        mine = m ^ (2 * slot)
        theirs = mine ^ 1
        jobs = [
            (queries, theirs * WIDE, WIDE, swap_stage.at[slot, :, pl.ds(0, WIDE)]),
            (suffix_kv, theirs * HD, HD, swap_stage.at[slot, :, pl.ds(WIDE, HD)]),
            (suffix_kv, (KVH + theirs) * HD, HD, swap_stage.at[slot, :, pl.ds(WIDE + HD, HD)]),
            (queries, mine * WIDE, WIDE, own_q.at[slot]),
            (suffix_kv, mine * HD, HD, own_kv.at[slot, pl.ds(0, ROWS), :]),
            (suffix_kv, (KVH + mine) * HD, HD, own_kv.at[slot, pl.ds(ROWS, ROWS), :]),
        ]
        for i, (src, at, width, dst) in enumerate(jobs):
            sem = (swap_sems if i < 3 else own_sems).at[3 * slot + i % 3]
            c = pltpu.make_async_copy(src.at[:, pl.ds(pl.multiple_of(at, HD), width)], dst, sem)
            c.start()
            (swaps if i < 3 else mine_copies).append(c)
    jobs = [
        (6, (0,), (stage6,)),
        (1, (0, 1), (stage1.at[0], stage1.at[1])),
        (0, (0, 1), (own.at[0], own.at[1])),
    ]
    waits = gather_pieces(meta, cache, cache_scale, jobs, sems)
    leaving = leave(
        [swap_stage, stage6, stage1], [swap, out6, out1], [swaps, waits[0], waits[1]], out_sems
    )
    for c in mine_copies + waits[2] + leaving:
        c.wait()


def near_call(meta, cache, cache_scale, queries, suffix_kv):
    return pl.pallas_call(
        near_kernel,
        out_shape=[
            PIECE_1,
            PIECE_2,
            jax.ShapeDtypeStruct((2, ROWS, SWAP), BF16),
            pltpu.VMEM((2, PIECE, HD), BF16),
            pltpu.VMEM((2, ROWS, WIDE), BF16),
            pltpu.VMEM((2, 2 * ROWS, HD), BF16),
        ],
        in_specs=[IN_SMEM, IN_HBM, IN_VMEM, IN_HBM, IN_HBM],
        out_specs=[IN_HBM] * 3 + [IN_VMEM] * 3,
        scratch_shapes=[
            pltpu.VMEM((PIECE, HD), BF16),
            pltpu.VMEM((2, PIECE, HD), BF16),
            pltpu.VMEM((2, ROWS, SWAP), BF16),
            pltpu.SemaphoreType.DMA((20,)),
            pltpu.SemaphoreType.DMA((6,)),
            pltpu.SemaphoreType.DMA((6,)),
            pltpu.SemaphoreType.DMA((3,)),
        ],
        compiler_params=pltpu.CompilerParams(vmem_limit_bytes=VMEM_LIMIT),
        cost_estimate=COST,
    )(meta, cache, cache_scale, queries, suffix_kv)


def wide(row):
    return jnp.concatenate([row] * (TILE // HD), axis=1)


def terms(tile, run):
    key = tile[run : run + 1]
    value = tile[RUNS + run : RUNS + run + 1]
    return wide(key * (LOG2E * INV_ROOT)), wide(jnp.log2(value)), wide(1.0 / value)


UNIT = None


def fold(q, keys, values_t, before, after, blocks_of):
    tiles = BOTH // TILE

    def score(t):
        return lax.dot_general(
            keys, q[pl.ds(t * TILE, TILE), :], NT, preferred_element_type=F32
        )

    following = score(0)
    for t in range(tiles):
        scores = following
        if t + 1 < tiles:
            following = score(t + 1)
        cols = pl.ds(t * TILE, TILE)
        blocks = blocks_of(t)
        old = before[REF_ROW : REF_ROW + 1, cols]
        parts = []
        reference = old
        for b, (term, dead, mask) in enumerate(blocks):
            part = scores[b * BLK : (b + 1) * BLK]
            part = part if mask is None else jnp.where(mask, part, masked_score)
            parts.append(part)
            top = jnp.max(part, axis=0, keepdims=True)
            top = top * (LOG2E * INV_ROOT) if term is UNIT else top * term[0]
            if dead is not None:
                top = jnp.where(dead, masked_score, top)
            reference = jnp.maximum(reference, top)
        factor = jnp.exp2(old - reference)
        total = before[SUM_ROW : SUM_ROW + 1, cols] * factor
        rounded = []
        for part, (term, dead, mask) in zip(parts, blocks):
            shift = reference if term is UNIT else reference - term[1]
            if dead is not None:
                shift = jnp.where(dead, -masked_score, shift)
            scaled = part * (LOG2E * INV_ROOT) if term is UNIT else part * term[0]
            weights = jnp.exp2(scaled - shift)
            if mask is not None:
                weights = jnp.where(mask, weights, 0.0)
            summed = jnp.sum(weights, axis=0, keepdims=True)
            total = total + (summed if term is UNIT else summed * term[2])
            rounded.append(weights.astype(BF16))
        rounded = jnp.concatenate(rounded, axis=0) if len(rounded) > 1 else rounded[0]
        product = jnp.dot(values_t, rounded, preferred_element_type=F32)
        after[:HD, cols] = before[:HD, cols] * factor + product
        after[REF_ROW : REF_ROW + 1, cols] = reference
        after[SUM_ROW : SUM_ROW + 1, cols] = total


def add_pieces(q, before, after, pieces, ks, meta):
    m = meta[META_M]
    n = len(ks)
    reach = jnp.where(((m // 2) * 2) * ROWS < meta[META_SUF], meta[META_LEN], 0)
    counts = [
        jnp.clip(reach - meta[META_J + RUNS * k + r] * BLK, 0, BLK) for k in ks for r in range(RUNS)
    ]
    most = functools.reduce(jnp.maximum, counts)

    @pl.when(most < BLK)
    def _():
        after[...] = before[...]

    @pl.when(most == BLK)
    def _():
        blocks = []
        for i in range(n):
            tile = pieces[i, 2 * PAIR :, :].astype(F32)
            blocks += [(terms(tile, r), counts[RUNS * i + r] < BLK, None) for r in range(RUNS)]
        keys = [pieces[i, :PAIR, :] for i in range(n)]
        values = [pieces[i, PAIR : 2 * PAIR, :].T for i in range(n)]
        fold(
            q,
            jnp.concatenate(keys, axis=0) if n > 1 else keys[0],
            jnp.concatenate(values, axis=1) if n > 1 else values[0],
            before,
            after,
            lambda t: blocks,
        )

    part = jnp.int32(-1)
    count = jnp.int32(0)
    for at, c in enumerate(counts):
        hit = (c > 0) & (c < BLK)
        part = jnp.where(hit, at, part)
        count = jnp.where(hit, c, count)

    @pl.when(part >= 0)
    def _():
        i = part // RUNS
        run = part % RUNS
        tile = pieces[i, 2 * PAIR :, :].astype(F32)
        term = [jnp.where(run == 1, b, a) for a, b in zip(terms(tile, 0), terms(tile, 1))]
        mask = lax.broadcasted_iota(jnp.int32, (BLK, TILE), 0) < count
        at = pl.multiple_of(run * BLK, BLK)
        fold(
            q,
            pieces[i, pl.ds(at, BLK), :],
            pieces[i, pl.ds(PAIR + at, BLK), :].T,
            after,
            after,
            lambda t: [(term, None, mask)],
        )


def state_shapes(slots):
    return [pltpu.VMEM((STATE, BOTH), F32)] * slots


def own_kernel(meta, cache, cache_scale, swap, own, own_q, own_kv, *refs):
    out7, out2, out3, kv, q_all = refs[:5]
    states = refs[5:7]
    firsts = refs[7:9]
    other, sem, stage7, stage2, stage3, sems, out_sems = refs[9:]
    c = pltpu.make_async_copy(swap, other, sem)
    c.start()
    jobs = [
        (7, (0,), (stage7,)),
        (2, (0, 1), (stage2.at[0], stage2.at[1])),
        (3, (0, 1), (stage3.at[0], stage3.at[1])),
    ]
    waits = gather_pieces(meta, cache, cache_scale, jobs, sems)
    leaving = leave([stage7, stage2, stage3], [out7, out2, out3], waits, out_sems)
    m = meta[META_M]
    for slot in range(2):
        for h in range(PER):
            q_all[slot, h * ROWS : (h + 1) * ROWS, :] = own_q[slot, :, h * HD : (h + 1) * HD]
        kv[slot, 0] = own_kv[slot]
    c.wait()
    for slot in range(2):
        for h in range(PER):
            q_all[slot, WIDE + h * ROWS : WIDE + (h + 1) * ROWS, :] = other[
                slot, :, h * HD : (h + 1) * HD
            ]
        kv[slot, 1, :ROWS, :] = other[slot, :, WIDE : WIDE + HD]
        kv[slot, 1, ROWS:, :] = other[slot, :, WIDE + HD :]
    key = lax.broadcasted_iota(jnp.int32, (BLK, TILE), 0)
    row = lax.broadcasted_iota(jnp.int32, (BLK, TILE), 1) % ROWS
    causal = key <= row
    odd = (m % 2) == 1

    def blocks_of(t):
        if t * TILE < WIDE:
            return [(UNIT, None, causal), (UNIT, jnp.logical_not(odd), None)]
        return [(UNIT, odd, None), (UNIT, None, causal)]

    for slot in range(2):
        first = firsts[slot]
        first[:HD, :] = jnp.zeros((HD, BOTH), F32)
        first[REF_ROW : REF_ROW + 8, :] = jnp.full((8, BOTH), masked_score, F32)
        first[SUM_ROW : SUM_ROW + 8, :] = jnp.zeros((8, BOTH), F32)
        keys = jnp.concatenate([kv[slot, 0, :ROWS], kv[slot, 1, :ROWS]], axis=0)
        values = jnp.concatenate([kv[slot, 0, ROWS:].T, kv[slot, 1, ROWS:].T], axis=1)
        fold(q_all.at[slot], keys, values, first, first, blocks_of)
        add_pieces(q_all.at[slot], first, states[slot], own.at[pl.ds(slot, 1)], (0,), meta)
    for c in leaving:
        c.wait()


def own_call(meta, cache, cache_scale, swap, own, own_q, own_kv):
    out = pl.pallas_call(
        own_kernel,
        out_shape=[
            PIECE_1,
            PIECE_2,
            PIECE_2,
            jax.ShapeDtypeStruct((2, 2, 2 * ROWS, HD), BF16),
            pltpu.VMEM((2, BOTH, HD), BF16),
        ]
        + state_shapes(2),
        in_specs=[IN_SMEM, IN_HBM, IN_VMEM, IN_HBM, IN_VMEM, IN_VMEM, IN_VMEM],
        out_specs=[IN_HBM] * 3 + [IN_VMEM] * 4,
        scratch_shapes=state_shapes(2)
        + [
            pltpu.VMEM((2, ROWS, SWAP), BF16),
            pltpu.SemaphoreType.DMA,
            pltpu.VMEM((PIECE, HD), BF16),
            pltpu.VMEM((2, PIECE, HD), BF16),
            pltpu.VMEM((2, PIECE, HD), BF16),
            pltpu.SemaphoreType.DMA((20,)),
            pltpu.SemaphoreType.DMA((3,)),
        ],
        compiler_params=pltpu.CompilerParams(vmem_limit_bytes=VMEM_LIMIT),
        cost_estimate=COST,
    )(meta, cache, cache_scale, swap, own, own_q, own_kv)
    return out[:4], out[4], out[5:]


def add_kernel(slots, ks, last, meta, q_all, *refs):
    refs = list(refs)
    take = lambda n: [refs.pop(0) for _ in range(n)]
    before = take(len(slots))
    sources = take(len(ks))
    if last:
        whole = take(1)[0] if slots[0] == 0 else take(2)[1]
        other, state, mine, sem = take(4)
        after = [state]
    else:
        after = take(len(slots))
    kv = take(1)[0]
    for w, slot in enumerate(slots):
        for i, s in enumerate(sources):
            kv[w, i] = s[slot] if len(s.shape) == 3 else s[...]
        add_pieces(q_all.at[slot], before[w], after[w], kv.at[w], ks, meta)
    if last:
        for side, ref in enumerate((mine, other)):
            member = meta[META_M] ^ side
            row = lax.broadcasted_iota(jnp.int32, (ROWS, HD), 0) + member * ROWS
            for i in range(PER):
                cols = pl.ds(side * WIDE + i * ROWS, ROWS)
                piece = (state[:HD, cols] / state[SUM_ROW : SUM_ROW + 1, cols]).T
                piece = jnp.where(row < meta[META_SUF], piece, 0.0)
                ref[:, i * HD : (i + 1) * HD] = piece.astype(BF16)
        column = pl.multiple_of((meta[META_M] ^ (2 * slots[0])) * WIDE, WIDE)
        c = pltpu.make_async_copy(mine, whole.at[:, pl.ds(column, WIDE)], sem)
        c.start()
        c.wait()


def add_call(meta, q_all, states, sources, slots, ks, last=False, whole=None):
    flat = [states[s] for s in slots]
    n = len(ks)
    args = [meta, q_all, *flat, *sources]
    in_specs = [IN_SMEM] + [IN_VMEM] * (len(args) - 1)
    scratch = [pltpu.VMEM((len(slots), n, PIECE, HD), BF16)]
    aliases = {}
    if last:
        out_shape = [
            jax.ShapeDtypeStruct((ROWS, QH * HD), BF16),
            jax.ShapeDtypeStruct((ROWS, WIDE), BF16),
        ]
        out_specs = [IN_HBM, IN_VMEM]
        scratch = (
            state_shapes(1) + [pltpu.VMEM((ROWS, WIDE), BF16), pltpu.SemaphoreType.DMA] + scratch
        )
        if whole is not None:
            aliases = {len(args): 0}
            args.append(whole)
            in_specs.append(IN_HBM)
    else:
        out_shape = state_shapes(len(slots))
        out_specs = [IN_VMEM] * len(slots)
    out = pl.pallas_call(
        functools.partial(add_kernel, slots, ks, last),
        out_shape=out_shape,
        in_specs=in_specs,
        out_specs=out_specs,
        scratch_shapes=scratch,
        input_output_aliases=aliases,
        compiler_params=pltpu.CompilerParams(vmem_limit_bytes=VMEM_LIMIT),
        cost_estimate=COST,
    )(*args)
    if last:
        return out
    states = list(states)
    for w, slot in enumerate(slots):
        states[slot] = out[w]
    return states


def early_kernel(meta, q_all, *refs):
    before = refs[0:2]
    kv = refs[2]
    after = refs[3:5]
    m = meta[META_M]

    @pl.when(m < 2)
    def _():
        for a, b in zip(before, after):
            b[...] = a[...]

    @pl.when(m >= 2)
    def _():
        for slot in range(2):
            fold(
                q_all.at[slot],
                jnp.concatenate([kv[1 - slot, side, :ROWS] for side in range(2)], axis=0),
                jnp.concatenate([kv[1 - slot, side, ROWS:].T for side in range(2)], axis=1),
                before[slot],
                after[slot],
                lambda t: [(UNIT, None, None)] * 2,
            )


def early_call(meta, q_all, states, kv):
    return pl.pallas_call(
        early_kernel,
        out_shape=state_shapes(2),
        in_specs=[IN_SMEM] + [IN_VMEM] * 4,
        out_specs=[IN_VMEM] * 2,
        compiler_params=pltpu.CompilerParams(vmem_limit_bytes=VMEM_LIMIT),
        cost_estimate=COST,
    )(meta, q_all, *states, kv)


def join_kernel(meta, c, d, _, out, sems):
    made = []
    for i, src in enumerate((c, d)):
        column = pl.multiple_of((meta[META_M] ^ (1 + 2 * i)) * WIDE, WIDE)
        made.append(pltpu.make_async_copy(src, out.at[:, pl.ds(column, WIDE)], sems.at[i]))
        made[-1].start()
    for x in made:
        x.wait()


def join_call(meta, c, d, whole):
    return pl.pallas_call(
        join_kernel,
        out_shape=jax.ShapeDtypeStruct((ROWS, QH * HD), BF16),
        in_specs=[IN_SMEM, IN_VMEM, IN_VMEM, IN_HBM],
        out_specs=IN_HBM,
        scratch_shapes=[pltpu.SemaphoreType.DMA((2,))],
        input_output_aliases={3: 0},
        cost_estimate=COST,
    )(meta, c, d, whole)


def permute(x, axis, count, k):
    return lax.ppermute(x, axis, [(i, i ^ k) for i in range(count)])


def per_device_small(
    queries, suffix_kv, cache, cache_scale, prefix_len, suffix_len, block_table, session_group
):
    ids = jnp.stack([lax.axis_index("pool"), lax.axis_index("blk")]).astype(jnp.int32)
    tables = [block_table, session_group, prefix_len, suffix_len]
    queries, suffix_kv, cache, *tables = [
        pltpu.with_memory_space_constraint(x, pltpu.HBM)
        for x in (queries, suffix_kv, cache, *tables)
    ]
    blocks = (cache, cache_scale.T)
    far_in, near_in = {}, {}
    meta, far4, far5 = far_call(ids, *tables, *blocks)
    far_in[4] = permute(far4, "pool", POOL, 4)
    far_in[5] = permute(far5, "pool", POOL, 5)
    far6, near1, swap, own, own_q, own_kv = near_call(meta, *blocks, queries, suffix_kv)
    swap_in = permute(swap, "blk", 4, 1)
    far_in[6] = permute(far6, "pool", POOL, 6)
    near_in[1] = permute(near1, "pool", POOL, 1)
    (far7, near2, near3, kv), q_all, states = own_call(
        meta, *blocks, swap_in, own, own_q, own_kv
    )
    far_in[7] = permute(far7, "pool", POOL, 7)
    near_in[2] = permute(near2, "pool", POOL, 2)
    near_in[3] = permute(near3, "pool", POOL, 3)
    early = permute(kv, "blk", 4, 2)
    across = {k: permute(far_in[k], "blk", 4, 2) for k in (4, 5, 6, 7)}

    states = add_call(meta, q_all, states, [near_in[1]], (0, 1), (1,))
    states = early_call(meta, q_all, states, early)
    states = add_call(meta, q_all, states, [near_in[2], near_in[3]], (0, 1), (2, 3))
    states = add_call(meta, q_all, states, [far_in[4], far_in[5]], (0,), (4, 5))
    states = add_call(meta, q_all, states, [across[4], across[5]], (1,), (4, 5))
    whole = None
    yours = []
    for slot, source in ((0, far_in), (1, across)):
        whole, other = add_call(
            meta, q_all, states, [source[6], source[7]], (slot,), (6, 7), last=True, whole=whole
        )
        yours.append(permute(other, "blk", 4, 1))
    return join_call(meta, *yours, whole)


def fold_keys(running, query_heads, key_rows, value_rows, key_scale, value_scale, usable):
    highest, weight_sum, weighted = running
    scores = jnp.einsum("kgrd,nkd->kgrn", query_heads, key_rows, preferred_element_type=jnp.float32)
    scores = scores * jnp.transpose(key_scale)[:, None, None, :]
    scores = jnp.where(usable[None, None], scores, masked_score)
    new_highest = jnp.maximum(highest, jnp.max(scores, axis=3))
    weights = jnp.where(usable[None, None], jnp.exp(scores - new_highest[..., None]), 0.0)
    factor = jnp.exp(highest - new_highest)
    weight_sum = weight_sum * factor + jnp.sum(weights, axis=3)
    rounded = (weights * jnp.transpose(value_scale)[:, None, None, :]).astype(jnp.bfloat16)
    weighted = weighted * factor[..., None] + jnp.einsum(
        "kgrn,nkd->kgrd", rounded, value_rows, preferred_element_type=jnp.float32
    )
    return (new_highest, weight_sum, weighted)


def per_device_any(
    queries, suffix_kv, cache, cache_scale, prefix_len, suffix_len, block_table, session_group
):
    local_rows = queries.shape[0]
    kv_heads = KVH
    per_group = QH // KVH
    head_size = HD
    pool_count = lax.axis_size("pool")
    member_count = lax.axis_size("blk")
    pool_index = lax.axis_index("pool")
    member_index = lax.axis_index("blk")
    slot_count = cache.shape[0]
    block_size = cache.shape[1]
    session_count = block_table.shape[0]
    block_count = block_table.shape[1]
    run_count = block_count // pool_count
    inv_root = 1.0 / math.sqrt(head_size)
    chooser = (
        session_group[:, None] == jnp.arange(session_count, dtype=jnp.int32)[None, :]
    ).astype(jnp.int32)
    tables = jnp.sum(chooser[:, :, None] * block_table[None], axis=1)
    holders = (tables // slot_count).reshape(pool_count, run_count, pool_count)
    places = (tables % slot_count).reshape(pool_count, run_count, pool_count)
    send_slots = jnp.sum(jnp.where(holders == pool_index, places, 0), axis=2)
    own_choice = lax.dynamic_index_in_dim(chooser, pool_index, 0, keepdims=False)
    prefix_length = jnp.sum(own_choice * prefix_len)
    suffix_length = jnp.sum(own_choice * suffix_len)
    own_holders = lax.dynamic_index_in_dim(holders, pool_index, 0, keepdims=False)
    positions = jnp.arange(block_count, dtype=jnp.int32).reshape(run_count, pool_count)
    matches = own_holders[None, :, :] == jnp.arange(pool_count, dtype=jnp.int32)[:, None, None]
    block_place = jnp.sum(jnp.where(matches, positions[None], 0), axis=2)
    scale_rows = cache_scale[send_slots]
    split_cache = cache.reshape(slot_count, block_size, 2 * kv_heads, head_size)
    share_size = 2 * kv_heads // member_count
    outgoing = lax.dynamic_slice_in_dim(
        split_cache[send_slots], member_index * share_size, share_size, 3
    )
    arrived_part, arrived_scale = (
        lax.all_to_all(outgoing, "pool", split_axis=0, concat_axis=0, tiled=True),
        lax.all_to_all(scale_rows, "pool", split_axis=0, concat_axis=0, tiled=True),
    )
    arrived = lax.all_gather(arrived_part, "blk", axis=3, tiled=True)
    prefix_tokens = pool_count * run_count * block_size
    step_tokens = min(1024, prefix_tokens)
    step_count = prefix_tokens // step_tokens
    prefix_stack = arrived.reshape(step_count, step_tokens, 2, kv_heads, head_size)
    token_scale = jnp.broadcast_to(
        arrived_scale.astype(jnp.float32).reshape(pool_count, run_count, 1, 2, kv_heads),
        (pool_count, run_count, block_size, 2, kv_heads),
    ).reshape(step_count, step_tokens, 2, kv_heads)
    token_place = (
        block_place[:, :, None] * block_size
        + jnp.arange(block_size, dtype=jnp.int32)[None, None, :]
    ).reshape(step_count, step_tokens)
    query_heads = jnp.transpose(
        queries.reshape(local_rows, kv_heads, per_group, head_size), (1, 2, 0, 3)
    )
    row_place = member_index * local_rows + jnp.arange(local_rows, dtype=jnp.int32)
    initial = (
        jnp.full((kv_heads, per_group, local_rows), masked_score, jnp.float32),
        jnp.zeros((kv_heads, per_group, local_rows), jnp.float32),
        jnp.zeros((kv_heads, per_group, local_rows, head_size), jnp.float32),
    )
    shard_rows = lax.all_gather(suffix_kv, "blk", axis=0, tiled=True)
    piece_count = shard_rows.shape[0]
    split_rows = shard_rows.reshape(piece_count, 2, kv_heads, head_size)
    key_place = jnp.arange(piece_count, dtype=jnp.int32)
    usable = (key_place[None, :] <= row_place[:, None]) & (key_place[None, :] < suffix_length)
    flat_scale = jnp.full((piece_count, kv_heads), inv_root, jnp.float32)
    unit_scale = jnp.ones((piece_count, kv_heads), jnp.float32)
    running = fold_keys(
        initial, query_heads, split_rows[:, 0], split_rows[:, 1], flat_scale, unit_scale, usable
    )

    def prefix_step(running, step_inputs):
        token_rows, scale_step, place_rows = step_inputs
        usable = (place_rows < prefix_length)[None, :]
        updated = fold_keys(
            running,
            query_heads,
            token_rows[:, 0],
            token_rows[:, 1],
            scale_step[:, 0] * inv_root,
            scale_step[:, 1],
            usable,
        )
        return (updated, None)

    running, unused = lax.scan(prefix_step, running, (prefix_stack, token_scale, token_place))
    highest, weight_sum, weighted = running
    result = weighted / weight_sum[..., None]
    result = jnp.transpose(result, (2, 0, 1, 3)).reshape(local_rows, QH * head_size)
    result = jnp.where((row_place < suffix_length)[:, None], result, 0.0)
    return result.astype(jnp.bfloat16)


def solution(mesh):
    small = dict(mesh.shape) == {"pool": POOL, "blk": 4}
    return jax.shard_map(
        per_device_small if small else per_device_any,
        mesh=mesh,
        in_specs=(
            P(("pool", "blk"), None),
            P(("pool", "blk"), None),
            P("pool", None, None),
            P("pool", None),
            P(),
            P(),
            P(),
            P(),
        ),
        out_specs=P(("pool", "blk"), None),
        check_vma=False,
    )
```

```python
import functools
import math

import jax
import jax.numpy as jnp
from jax import lax
from jax.experimental import pallas as pl
from jax.experimental.pallas import tpu as pltpu
from jax.sharding import PartitionSpec as P

QH = 32
KVH = 4
HD = 128
PER = QH // KVH
LOG2E = math.log2(math.e)
INV_ROOT = 1.0 / math.sqrt(HD)

masked_score = -1e30

RUNS = 2
BLK = 128
PAIR = RUNS * BLK
PIECE = 2 * PAIR + 16
ROWS = 128
WIDE = PER * ROWS
BOTH = 2 * WIDE
REF_ROW = HD
SUM_ROW = HD + 8
STATE = HD + 16
POOL = 8
META_J = 0
META_LEN = 2 * POOL
META_SUF = META_LEN + 1
META_M = META_LEN + 2
META_SIZE = 24
TILE = 512
NT = (((1,), (1,)), ((), ()))
VMEM_LIMIT = 24 << 20
BF16 = jnp.bfloat16
F32 = jnp.float32
IN_VMEM = pl.BlockSpec(memory_space=pltpu.VMEM)
IN_SMEM = pl.BlockSpec(memory_space=pltpu.SMEM)
IN_HBM = pl.BlockSpec(memory_space=pltpu.HBM)


COST = pl.CostEstimate(flops=1 << 10, bytes_accessed=1 << 10, transcendentals=0)


def write_scales(scales, locals_, head, dst):
    col_at = lax.broadcasted_iota(jnp.int32, scales.shape, 0)
    slot_at = lax.broadcasted_iota(jnp.int32, scales.shape, 1)
    row = lax.broadcasted_iota(jnp.int32, (16, HD), 0)
    rows = jnp.zeros((16, HD), F32)
    for half in range(2):
        for run in range(RUNS):
            chosen = (slot_at == locals_[run]) & (col_at == half * KVH + head)
            one = jnp.sum(jnp.where(chosen, scales, 0.0), axis=(0, 1), keepdims=True)
            rows = jnp.where(row == half * RUNS + run, one, rows)
    dst[pl.ds(2 * PAIR, 16), :] = rows.astype(BF16)


def piece_copies(cache, locals_, head, dst, sems, first):
    made = []
    for half in range(2):
        column = pl.multiple_of((half * KVH + head) * HD, HD)
        for run in range(RUNS):
            made.append(
                pltpu.make_async_copy(
                    cache.at[locals_[run], :, pl.ds(column, HD)],
                    dst.at[pl.ds(half * PAIR + run * BLK, BLK), :],
                    sems.at[first + 2 * half + run],
                )
            )
    return made


PIECE_1 = pltpu.VMEM((PIECE, HD), BF16)
PIECE_2 = pltpu.VMEM((2, PIECE, HD), BF16)
SWAP = WIDE + 2 * HD


def gather_kernel(ids, queries, suffix_kv, cache, *refs):
    loads = list(zip(refs[:5], refs[17:22]))
    meta, swap = refs[5:7]
    far, near, own = refs[7:11], refs[11:14], refs[14]
    own_q, own_kv = refs[15:17]
    table, groups, lengths, suffixes, cache_scale = refs[17:22]
    table_sems, more_sems, sems = refs[22:]
    p = ids[0]
    m = ids[1]
    loads = [
        pltpu.make_async_copy(a, b, table_sems.at[i]) for i, (a, b) in enumerate(loads)
    ]
    for c in loads:
        c.start()
    made = []
    for slot in range(2):
        mine = m ^ (2 * slot)
        theirs = mine ^ 1
        jobs = [
            (queries, theirs * WIDE, WIDE, swap.at[slot, :, pl.ds(0, WIDE)]),
            (suffix_kv, theirs * HD, HD, swap.at[slot, :, pl.ds(WIDE, HD)]),
            (suffix_kv, (KVH + theirs) * HD, HD, swap.at[slot, :, pl.ds(WIDE + HD, HD)]),
            (queries, mine * WIDE, WIDE, own_q.at[slot]),
            (suffix_kv, mine * HD, HD, own_kv.at[slot, pl.ds(0, ROWS), :]),
            (suffix_kv, (KVH + mine) * HD, HD, own_kv.at[slot, pl.ds(ROWS, ROWS), :]),
        ]
        for src, at, width, dst in jobs:
            src = src.at[:, pl.ds(pl.multiple_of(at, HD), width)]
            c = pltpu.make_async_copy(src, dst, more_sems.at[len(made)])
            c.start()
            made.append(c)
    for c in loads:
        c.wait()
    meta[META_M] = m
    slot_count = cache.shape[0]
    low = p * slot_count
    jobs = [(4 + i, (0,), (ref,)) for i, ref in enumerate(far)]
    jobs += [(1 + i, (0, 1), (ref.at[0], ref.at[1])) for i, ref in enumerate(near)]
    jobs += [(0, (0, 1), (own.at[0], own.at[1]))]
    pending = []
    count = 0
    for k, slots, outs in jobs:
        session = groups[p ^ k]
        locals_ = []
        for run in range(RUNS):
            local = jnp.int32(0)
            for jj in range(POOL):
                at = table[session, run * POOL + jj] - low
                local = jnp.where((at >= 0) & (at < slot_count), at, local)
            locals_.append(local)
        for slot, out in zip(slots, outs):
            group = piece_copies(cache, locals_, m ^ (2 * slot), out, sems, count)
            count += 4
            for c in group:
                c.start()
            made += group
            pending.append((locals_, m ^ (2 * slot), out))
    mine = groups[p]
    for run in range(RUNS):
        for jj in range(POOL):
            at = run * POOL + jj
            meta[META_J + RUNS * ((table[mine, at] // slot_count) ^ p) + run] = at
    meta[META_LEN] = lengths[mine]
    meta[META_SUF] = suffixes[mine]
    scales = cache_scale[...].astype(F32)
    for locals_, head, out in pending:
        write_scales(scales, locals_, head, out)
    for c in made:
        c.wait()


def gather_call(ids, queries, suffix_kv, cache, tables, cache_scale):
    return pl.pallas_call(
        gather_kernel,
        out_shape=[
            jax.ShapeDtypeStruct((META_SIZE,), jnp.int32),
            pltpu.VMEM((2, ROWS, SWAP), BF16),
        ]
        + [PIECE_1] * 4
        + [PIECE_2] * 4
        + [pltpu.VMEM((2, ROWS, WIDE), BF16), pltpu.VMEM((2, 2 * ROWS, HD), BF16)],
        in_specs=[IN_SMEM] + [IN_HBM] * 8,
        out_specs=[IN_SMEM] + [IN_VMEM] * 11,
        scratch_shapes=[pltpu.SMEM(x.shape, jnp.int32) for x in tables]
        + [
            pltpu.VMEM(cache_scale.shape, cache_scale.dtype),
            pltpu.SemaphoreType.DMA((5,)),
            pltpu.SemaphoreType.DMA((12,)),
            pltpu.SemaphoreType.DMA((48,)),
        ],
        compiler_params=pltpu.CompilerParams(vmem_limit_bytes=VMEM_LIMIT),
        cost_estimate=COST,
    )(ids, queries, suffix_kv, cache, *tables, cache_scale)


def wide(row):
    return jnp.concatenate([row] * (TILE // HD), axis=1)


def terms(tile, run):
    key = tile[run : run + 1]
    value = tile[RUNS + run : RUNS + run + 1]
    return wide(key * (LOG2E * INV_ROOT)), wide(jnp.log2(value)), wide(1.0 / value)


UNIT = None


def fold(q, keys, values_t, before, after, blocks_of):
    tiles = BOTH // TILE

    def score(t):
        return lax.dot_general(
            keys, q[pl.ds(t * TILE, TILE), :], NT, preferred_element_type=F32
        )

    following = score(0)
    for t in range(tiles):
        scores = following
        if t + 1 < tiles:
            following = score(t + 1)
        cols = pl.ds(t * TILE, TILE)
        blocks = blocks_of(t)
        old = jnp.full((1, TILE), masked_score, F32) if before is None else before[REF_ROW : REF_ROW + 1, cols]
        parts = []
        reference = old
        for b, (term, dead, mask) in enumerate(blocks):
            part = scores[b * BLK : (b + 1) * BLK]
            part = part if mask is None else jnp.where(mask, part, masked_score)
            parts.append(part)
            top = jnp.max(part, axis=0, keepdims=True)
            top = top * (LOG2E * INV_ROOT) if term is UNIT else top * term[0]
            if dead is not None:
                top = jnp.where(dead, masked_score, top)
            reference = jnp.maximum(reference, top)
        if before is None:
            total = jnp.zeros((1, TILE), F32)
        else:
            factor = jnp.exp2(old - reference)
            total = before[SUM_ROW : SUM_ROW + 1, cols] * factor
        rounded = []
        for part, (term, dead, mask) in zip(parts, blocks):
            shift = reference if term is UNIT else reference - term[1]
            if dead is not None:
                shift = jnp.where(dead, -masked_score, shift)
            scaled = part * (LOG2E * INV_ROOT) if term is UNIT else part * term[0]
            weights = jnp.exp2(scaled - shift)
            if mask is not None:
                weights = jnp.where(mask, weights, 0.0)
            summed = jnp.sum(weights, axis=0, keepdims=True)
            total = total + (summed if term is UNIT else summed * term[2])
            rounded.append(weights.astype(BF16))
        rounded = jnp.concatenate(rounded, axis=0) if len(rounded) > 1 else rounded[0]
        product = jnp.dot(values_t, rounded, preferred_element_type=F32)
        after[:HD, cols] = product if before is None else before[:HD, cols] * factor + product
        after[REF_ROW : REF_ROW + 1, cols] = reference
        after[SUM_ROW : SUM_ROW + 1, cols] = total


def add_pieces(q, before, after, pieces, ks, meta, extra=None):
    m = meta[META_M]
    n = len(ks)
    reach = jnp.where(((m // 2) * 2) * ROWS < meta[META_SUF], meta[META_LEN], 0)
    counts = [
        jnp.clip(reach - meta[META_J + RUNS * k + r] * BLK, 0, BLK) for k in ks for r in range(RUNS)
    ]
    most = functools.reduce(jnp.maximum, counts)

    def whole():
        blocks = []
        for i in range(n):
            tile = pieces[i, 2 * PAIR :, :].astype(F32)
            blocks += [(terms(tile, r), counts[RUNS * i + r] < BLK, None) for r in range(RUNS)]
        keys = [pieces[i, :PAIR, :] for i in range(n)]
        values = [pieces[i, PAIR : 2 * PAIR, :].T for i in range(n)]
        blocks_of = lambda t: blocks
        if extra is not None:
            keys = [extra[0]] + keys
            values = [extra[1]] + values
            blocks_of = lambda t: extra[2](t) + blocks
        keys = jnp.concatenate(keys, axis=0) if len(keys) > 1 else keys[0]
        values = jnp.concatenate(values, axis=1) if len(values) > 1 else values[0]
        fold(q, keys, values, before, after, blocks_of)

    if extra is not None:
        whole()
    else:

        @pl.when(most < BLK)
        def _():
            after[...] = before[...]

        pl.when(most == BLK)(whole)

    part = jnp.int32(-1)
    count = jnp.int32(0)
    for at, c in enumerate(counts):
        hit = (c > 0) & (c < BLK)
        part = jnp.where(hit, at, part)
        count = jnp.where(hit, c, count)

    @pl.when(part >= 0)
    def _():
        i = part // RUNS
        run = part % RUNS
        tile = pieces[i, 2 * PAIR :, :].astype(F32)
        term = [jnp.where(run == 1, b, a) for a, b in zip(terms(tile, 0), terms(tile, 1))]
        mask = lax.broadcasted_iota(jnp.int32, (BLK, TILE), 0) < count
        at = pl.multiple_of(run * BLK, BLK)
        fold(
            q,
            pieces[i, pl.ds(at, BLK), :],
            pieces[i, pl.ds(PAIR + at, BLK), :].T,
            after,
            after,
            lambda t: [(term, None, mask)],
        )


def state_shapes(slots):
    return [pltpu.VMEM((STATE, BOTH), F32)] * slots


def own_kernel(meta, swap, own, own_q, own_kv, kv, q_all, *states):
    m = meta[META_M]
    for slot in range(2):
        for h in range(PER):
            rows = pl.ds(h * ROWS, ROWS)
            others = pl.ds(WIDE + h * ROWS, ROWS)
            q_all[slot, rows, :] = own_q[slot, :, h * HD : (h + 1) * HD]
            q_all[slot, others, :] = swap[slot, :, h * HD : (h + 1) * HD]
        kv[slot, 0] = own_kv[slot]
        kv[slot, 1, :ROWS, :] = swap[slot, :, WIDE : WIDE + HD]
        kv[slot, 1, ROWS:, :] = swap[slot, :, WIDE + HD :]
    key = lax.broadcasted_iota(jnp.int32, (BLK, TILE), 0)
    row = lax.broadcasted_iota(jnp.int32, (BLK, TILE), 1) % ROWS
    causal = key <= row
    odd = (m % 2) == 1

    def blocks_of(t):
        if t * TILE < WIDE:
            return [(UNIT, None, causal), (UNIT, jnp.logical_not(odd), None)]
        return [(UNIT, odd, None), (UNIT, None, causal)]

    for slot in range(2):
        keys = jnp.concatenate([kv[slot, side, :ROWS] for side in range(2)], axis=0)
        values = jnp.concatenate([kv[slot, side, ROWS:].T for side in range(2)], axis=1)
        add_pieces(
            q_all.at[slot],
            None,
            states[slot],
            own.at[pl.ds(slot, 1)],
            (0,),
            meta,
            (keys, values, blocks_of),
        )


def own_call(meta, swap, own, own_q, own_kv):
    out = pl.pallas_call(
        own_kernel,
        out_shape=[pltpu.VMEM((2, 2, 2 * ROWS, HD), BF16), pltpu.VMEM((2, BOTH, HD), BF16)]
        + state_shapes(2),
        in_specs=[IN_SMEM] + [IN_VMEM] * 4,
        out_specs=[IN_VMEM] * 4,
        compiler_params=pltpu.CompilerParams(vmem_limit_bytes=VMEM_LIMIT),
        cost_estimate=COST,
    )(meta, swap, own, own_q, own_kv)
    return out[0], out[1], out[2:]


def add_kernel(slots, ks, early, last, meta, q_all, *refs):
    refs = list(refs)
    take = lambda n: [refs.pop(0) for _ in range(n)]
    before = take(len(slots))
    sources = take(len(ks))
    kv_early = take(1)[0] if early else None
    outs = take(2) if last else None
    after = take(len(slots))
    kv = take(1)[0]
    for w, slot in enumerate(slots):
        for i, s in enumerate(sources):
            kv[w, i] = s[slot] if len(s.shape) == 3 else s[...]
        extra = None
        if early:
            unused = meta[META_M] < 2
            extra = (
                jnp.concatenate([kv_early[1 - slot, side, :ROWS] for side in range(2)], axis=0),
                jnp.concatenate([kv_early[1 - slot, side, ROWS:].T for side in range(2)], axis=1),
                lambda t: [(UNIT, unused, None)] * 2,
            )
        add_pieces(q_all.at[slot], before[w], after[w], kv.at[w], ks, meta, extra)
    if last:
        state = after[0]
        for side, out in enumerate(outs):
            member = meta[META_M] ^ side
            row = lax.broadcasted_iota(jnp.int32, (HD, ROWS), 1) + member * ROWS
            for i in range(PER):
                cols = pl.ds(side * WIDE + i * ROWS, ROWS)
                piece = state[:HD, cols] * (1.0 / state[SUM_ROW : SUM_ROW + 1, cols])
                piece = jnp.where(row < meta[META_SUF], piece, 0.0).astype(BF16)
                out[:, i * HD : (i + 1) * HD] = piece.T


def add_call(meta, q_all, states, sources, slots, ks, early=None, last=False):
    flat = [states[s] for s in slots]
    n = len(ks)
    args = [meta, q_all, *flat, *sources] + ([] if early is None else [early])
    scratch = [pltpu.VMEM((len(slots), n, PIECE, HD), BF16)]
    if last:
        out_shape = [pltpu.VMEM((ROWS, WIDE), BF16)] * 2
        scratch = state_shapes(1) + scratch
    else:
        out_shape = state_shapes(len(slots))
    out = pl.pallas_call(
        functools.partial(add_kernel, slots, ks, early is not None, last),
        out_shape=out_shape,
        in_specs=[IN_SMEM] + [IN_VMEM] * (len(args) - 1),
        out_specs=[IN_VMEM] * len(out_shape),
        scratch_shapes=scratch,
        compiler_params=pltpu.CompilerParams(vmem_limit_bytes=VMEM_LIMIT),
        cost_estimate=COST,
    )(*args)
    if last:
        return out
    states = list(states)
    for w, slot in enumerate(slots):
        states[slot] = out[w]
    return states


def join_kernel(meta, *refs):
    out, sems = refs[4:]
    made = []
    for i, src in enumerate(refs[:4]):
        head = meta[META_M] ^ (2 * (i % 2) + i // 2)
        column = pl.multiple_of(head * WIDE, WIDE)
        made.append(pltpu.make_async_copy(src, out.at[:, pl.ds(column, WIDE)], sems.at[i]))
        made[-1].start()
    for x in made:
        x.wait()


def join_call(meta, mine, yours):
    return pl.pallas_call(
        join_kernel,
        out_shape=jax.ShapeDtypeStruct((ROWS, QH * HD), BF16),
        in_specs=[IN_SMEM] + [IN_VMEM] * 4,
        out_specs=IN_HBM,
        scratch_shapes=[pltpu.SemaphoreType.DMA((4,))],
        cost_estimate=COST,
    )(meta, *mine, *yours)


def permute(x, axis, count, k):
    return lax.ppermute(x, axis, [(i, i ^ k) for i in range(count)])


def per_device_small(
    queries, suffix_kv, cache, cache_scale, prefix_len, suffix_len, block_table, session_group
):
    ids = jnp.stack([lax.axis_index("pool"), lax.axis_index("blk")]).astype(jnp.int32)
    tables = [block_table, session_group, prefix_len, suffix_len]
    queries, suffix_kv, cache, scale, *tables = [
        pltpu.with_memory_space_constraint(x, pltpu.HBM)
        for x in (queries, suffix_kv, cache, cache_scale.T, *tables)
    ]
    meta, swap, *parts = gather_call(ids, queries, suffix_kv, cache, tables, scale)
    far, near = parts[:4], parts[4:7]
    own, own_q, own_kv = parts[7:]
    far_in, near_in, across = {}, {}, {}
    swap_in = permute(swap, "blk", 4, 1)
    for k in (4, 5):
        far_in[k] = permute(far[k - 4], "pool", POOL, k)
    for k in (1, 2):
        near_in[k] = permute(near[k - 1], "pool", POOL, k)
    kv, q_all, states = own_call(meta, swap_in, own, own_q, own_kv)
    far[2], near[2], kv, states = lax.optimization_barrier((far[2], near[2], kv, states))
    far_in[6] = permute(far[2], "pool", POOL, 6)
    near_in[3] = permute(near[2], "pool", POOL, 3)
    early = permute(kv, "blk", 4, 2)
    states = add_call(meta, q_all, states, [near_in[1], near_in[2]], (0, 1), (1, 2))
    far[3], far_in[4], far_in[5], states = lax.optimization_barrier(
        (far[3], far_in[4], far_in[5], states)
    )
    far_in[7] = permute(far[3], "pool", POOL, 7)
    for k in (4, 5):
        across[k] = permute(far_in[k], "blk", 4, 2)
    states = add_call(meta, q_all, states, [near_in[3]], (0, 1), (3,), early=early)
    far_in[6], far_in[7], states = lax.optimization_barrier((far_in[6], far_in[7], states))
    for k in (6, 7):
        across[k] = permute(far_in[k], "blk", 4, 2)
    states = add_call(meta, q_all, states, [far_in[4], far_in[5]], (0,), (4, 5))
    states = add_call(meta, q_all, states, [across[4], across[5]], (1,), (4, 5))
    mine, yours = [], []
    for slot, source in ((0, far_in), (1, across)):
        a, b = add_call(meta, q_all, states, [source[6], source[7]], (slot,), (6, 7), last=True)
        mine.append(a)
        yours.append(
            pltpu.with_memory_space_constraint(permute(b, "blk", 4, 1), pltpu.VMEM)
        )
    return join_call(meta, mine, yours)


def fold_keys(running, query_heads, key_rows, value_rows, key_scale, value_scale, usable):
    highest, weight_sum, weighted = running
    scores = jnp.einsum("kgrd,nkd->kgrn", query_heads, key_rows, preferred_element_type=jnp.float32)
    scores = scores * jnp.transpose(key_scale)[:, None, None, :]
    scores = jnp.where(usable[None, None], scores, masked_score)
    new_highest = jnp.maximum(highest, jnp.max(scores, axis=3))
    weights = jnp.where(usable[None, None], jnp.exp(scores - new_highest[..., None]), 0.0)
    factor = jnp.exp(highest - new_highest)
    weight_sum = weight_sum * factor + jnp.sum(weights, axis=3)
    rounded = (weights * jnp.transpose(value_scale)[:, None, None, :]).astype(jnp.bfloat16)
    weighted = weighted * factor[..., None] + jnp.einsum(
        "kgrn,nkd->kgrd", rounded, value_rows, preferred_element_type=jnp.float32
    )
    return (new_highest, weight_sum, weighted)


def per_device_any(
    queries, suffix_kv, cache, cache_scale, prefix_len, suffix_len, block_table, session_group
):
    local_rows = queries.shape[0]
    kv_heads = KVH
    per_group = QH // KVH
    head_size = HD
    pool_count = lax.axis_size("pool")
    member_count = lax.axis_size("blk")
    pool_index = lax.axis_index("pool")
    member_index = lax.axis_index("blk")
    slot_count = cache.shape[0]
    block_size = cache.shape[1]
    session_count = block_table.shape[0]
    block_count = block_table.shape[1]
    run_count = block_count // pool_count
    inv_root = 1.0 / math.sqrt(head_size)
    chooser = (
        session_group[:, None] == jnp.arange(session_count, dtype=jnp.int32)[None, :]
    ).astype(jnp.int32)
    tables = jnp.sum(chooser[:, :, None] * block_table[None], axis=1)
    holders = (tables // slot_count).reshape(pool_count, run_count, pool_count)
    places = (tables % slot_count).reshape(pool_count, run_count, pool_count)
    send_slots = jnp.sum(jnp.where(holders == pool_index, places, 0), axis=2)
    own_choice = lax.dynamic_index_in_dim(chooser, pool_index, 0, keepdims=False)
    prefix_length = jnp.sum(own_choice * prefix_len)
    suffix_length = jnp.sum(own_choice * suffix_len)
    own_holders = lax.dynamic_index_in_dim(holders, pool_index, 0, keepdims=False)
    positions = jnp.arange(block_count, dtype=jnp.int32).reshape(run_count, pool_count)
    matches = own_holders[None, :, :] == jnp.arange(pool_count, dtype=jnp.int32)[:, None, None]
    block_place = jnp.sum(jnp.where(matches, positions[None], 0), axis=2)
    scale_rows = cache_scale[send_slots]
    split_cache = cache.reshape(slot_count, block_size, 2 * kv_heads, head_size)
    share_size = 2 * kv_heads // member_count
    outgoing = lax.dynamic_slice_in_dim(
        split_cache[send_slots], member_index * share_size, share_size, 3
    )
    arrived_part, arrived_scale = (
        lax.all_to_all(outgoing, "pool", split_axis=0, concat_axis=0, tiled=True),
        lax.all_to_all(scale_rows, "pool", split_axis=0, concat_axis=0, tiled=True),
    )
    arrived = lax.all_gather(arrived_part, "blk", axis=3, tiled=True)
    prefix_tokens = pool_count * run_count * block_size
    step_tokens = min(1024, prefix_tokens)
    step_count = prefix_tokens // step_tokens
    prefix_stack = arrived.reshape(step_count, step_tokens, 2, kv_heads, head_size)
    token_scale = jnp.broadcast_to(
        arrived_scale.astype(jnp.float32).reshape(pool_count, run_count, 1, 2, kv_heads),
        (pool_count, run_count, block_size, 2, kv_heads),
    ).reshape(step_count, step_tokens, 2, kv_heads)
    token_place = (
        block_place[:, :, None] * block_size
        + jnp.arange(block_size, dtype=jnp.int32)[None, None, :]
    ).reshape(step_count, step_tokens)
    query_heads = jnp.transpose(
        queries.reshape(local_rows, kv_heads, per_group, head_size), (1, 2, 0, 3)
    )
    row_place = member_index * local_rows + jnp.arange(local_rows, dtype=jnp.int32)
    initial = (
        jnp.full((kv_heads, per_group, local_rows), masked_score, jnp.float32),
        jnp.zeros((kv_heads, per_group, local_rows), jnp.float32),
        jnp.zeros((kv_heads, per_group, local_rows, head_size), jnp.float32),
    )
    shard_rows = lax.all_gather(suffix_kv, "blk", axis=0, tiled=True)
    piece_count = shard_rows.shape[0]
    split_rows = shard_rows.reshape(piece_count, 2, kv_heads, head_size)
    key_place = jnp.arange(piece_count, dtype=jnp.int32)
    usable = (key_place[None, :] <= row_place[:, None]) & (key_place[None, :] < suffix_length)
    flat_scale = jnp.full((piece_count, kv_heads), inv_root, jnp.float32)
    unit_scale = jnp.ones((piece_count, kv_heads), jnp.float32)
    running = fold_keys(
        initial, query_heads, split_rows[:, 0], split_rows[:, 1], flat_scale, unit_scale, usable
    )

    def prefix_step(running, step_inputs):
        token_rows, scale_step, place_rows = step_inputs
        usable = (place_rows < prefix_length)[None, :]
        updated = fold_keys(
            running,
            query_heads,
            token_rows[:, 0],
            token_rows[:, 1],
            scale_step[:, 0] * inv_root,
            scale_step[:, 1],
            usable,
        )
        return (updated, None)

    running, unused = lax.scan(prefix_step, running, (prefix_stack, token_scale, token_place))
    highest, weight_sum, weighted = running
    result = weighted / weight_sum[..., None]
    result = jnp.transpose(result, (2, 0, 1, 3)).reshape(local_rows, QH * head_size)
    result = jnp.where((row_place < suffix_length)[:, None], result, 0.0)
    return result.astype(jnp.bfloat16)


def solution(mesh):
    small = dict(mesh.shape) == {"pool": POOL, "blk": 4}
    return jax.shard_map(
        per_device_small if small else per_device_any,
        mesh=mesh,
        in_specs=(
            P(("pool", "blk"), None),
            P(("pool", "blk"), None),
            P("pool", None, None),
            P("pool", None),
            P(),
            P(),
            P(),
            P(),
        ),
        out_specs=P(("pool", "blk"), None),
        check_vma=False,
    )
```

```python
import functools
import math

import jax
import jax.numpy as jnp
from jax import lax
from jax.experimental import pallas as pl
from jax.experimental.pallas import tpu as pltpu
from jax.sharding import PartitionSpec as P

QH = 32
KVH = 4
HD = 128
PER = QH // KVH
LOG2E = math.log2(math.e)
INV_ROOT = 1.0 / math.sqrt(HD)

masked_score = -1e30

RUNS = 2
BLK = 128
PAIR = RUNS * BLK
PIECE = 2 * PAIR + 16
ROWS = 128
WIDE = PER * ROWS
BOTH = 2 * WIDE
REF_ROW = HD
SUM_ROW = HD + 8
STATE = HD + 16
POOL = 8
META_J = 0
META_LEN = 2 * POOL
META_SUF = META_LEN + 1
META_M = META_LEN + 2
META_SIZE = 24
TILE = 1024
VMEM_LIMIT = 24 << 20
BF16 = jnp.bfloat16
F32 = jnp.float32
IN_VMEM = pl.BlockSpec(memory_space=pltpu.VMEM)
IN_SMEM = pl.BlockSpec(memory_space=pltpu.SMEM)
IN_HBM = pl.BlockSpec(memory_space=pltpu.HBM)


COST = pl.CostEstimate(flops=1 << 10, bytes_accessed=1 << 10, transcendentals=0)


def spread_scales(cache_scale, m, spread):
    scales = cache_scale[...].astype(F32).T
    column = lax.broadcasted_iota(jnp.int32, scales.shape, 1)
    for slot in range(2):
        for half in range(2):
            chosen = jnp.where(column == half * KVH + (m ^ (2 * slot)), scales, 0.0)
            one = jnp.sum(chosen, axis=1, keepdims=True)
            spread[2 * slot + half] = jnp.broadcast_to(one, (scales.shape[0], HD))


def write_scales(spread, locals_, slot, dst):
    row = lax.broadcasted_iota(jnp.int32, (16, HD), 0)
    rows = jnp.ones((16, HD), F32)
    for half in range(2):
        for run in range(RUNS):
            one = spread[2 * slot + half, pl.ds(locals_[run], 1), :]
            rows = jnp.where(row == half * RUNS + run, one, rows)
    dst[pl.ds(2 * PAIR, 16), :] = rows.astype(BF16)


def piece_copies(cache, locals_, head, dst, sems, first):
    made = []
    for half in range(2):
        column = pl.multiple_of((half * KVH + head) * HD, HD)
        for run in range(RUNS):
            made.append(
                pltpu.make_async_copy(
                    cache.at[locals_[run], :, pl.ds(column, HD)],
                    dst.at[pl.ds(half * PAIR + run * BLK, BLK), :],
                    sems.at[first + 2 * half + run],
                )
            )
    return made


PIECE_1 = pltpu.VMEM((PIECE, HD), BF16)
PIECE_2 = pltpu.VMEM((2, PIECE, HD), BF16)
SWAP = WIDE + 2 * HD


def gather_kernel(ids, queries, suffix_kv, cache, *refs):
    loads = list(zip(refs[:5], refs[17:22]))
    meta, swap = refs[5:7]
    far, near, own = refs[7:11], refs[11:14], refs[14]
    own_q, own_kv = refs[15:17]
    table, groups, lengths, suffixes, cache_scale = refs[17:22]
    spread, table_sems, more_sems, sems = refs[22:]
    p = ids[0]
    m = ids[1]
    loads = [
        pltpu.make_async_copy(a, b, table_sems.at[i]) for i, (a, b) in enumerate(loads)
    ]
    for c in loads:
        c.start()
    made = []
    for slot in range(2):
        mine = m ^ (2 * slot)
        theirs = mine ^ 1
        jobs = [
            (queries, theirs * WIDE, WIDE, swap.at[slot, :, pl.ds(0, WIDE)]),
            (suffix_kv, theirs * HD, HD, swap.at[slot, :, pl.ds(WIDE, HD)]),
            (suffix_kv, (KVH + theirs) * HD, HD, swap.at[slot, :, pl.ds(WIDE + HD, HD)]),
            (queries, mine * WIDE, WIDE, own_q.at[slot]),
            (suffix_kv, mine * HD, HD, own_kv.at[slot, pl.ds(0, ROWS), :]),
            (suffix_kv, (KVH + mine) * HD, HD, own_kv.at[slot, pl.ds(ROWS, ROWS), :]),
        ]
        for src, at, width, dst in jobs:
            src = src.at[:, pl.ds(pl.multiple_of(at, HD), width)]
            c = pltpu.make_async_copy(src, dst, more_sems.at[len(made)])
            c.start()
            made.append(c)
    for c in loads:
        c.wait()
    meta[META_M] = m
    slot_count = cache.shape[0]
    low = p * slot_count
    jobs = [(4 + i, (0,), (ref,)) for i, ref in enumerate(far)]
    jobs += [(1 + i, (0, 1), (ref.at[0], ref.at[1])) for i, ref in enumerate(near)]
    jobs += [(0, (0, 1), (own.at[0], own.at[1]))]
    pending = []
    count = 0
    for k, slots, outs in jobs:
        session = groups[p ^ k]
        locals_ = []
        for run in range(RUNS):
            local = jnp.int32(0)
            for jj in range(POOL):
                at = table[session, run * POOL + jj] - low
                local = jnp.where((at >= 0) & (at < slot_count), at, local)
            locals_.append(local)
        for slot, out in zip(slots, outs):
            group = piece_copies(cache, locals_, m ^ (2 * slot), out, sems, count)
            count += 4
            for c in group:
                c.start()
            made += group
            pending.append((locals_, slot, out))
    mine = groups[p]
    for run in range(RUNS):
        for jj in range(POOL):
            at = run * POOL + jj
            meta[META_J + RUNS * ((table[mine, at] // slot_count) ^ p) + run] = at
    meta[META_LEN] = lengths[mine]
    meta[META_SUF] = suffixes[mine]
    spread_scales(cache_scale, m, spread)
    for locals_, slot, out in pending:
        write_scales(spread, locals_, slot, out)
    for c in made:
        c.wait()


def gather_call(ids, queries, suffix_kv, cache, tables, cache_scale):
    return pl.pallas_call(
        gather_kernel,
        out_shape=[
            jax.ShapeDtypeStruct((META_SIZE,), jnp.int32),
            pltpu.VMEM((2, ROWS, SWAP), BF16),
        ]
        + [PIECE_1] * 4
        + [PIECE_2] * 4
        + [pltpu.VMEM((2, ROWS, WIDE), BF16), pltpu.VMEM((2, 2 * ROWS, HD), BF16)],
        in_specs=[IN_SMEM] + [IN_HBM] * 8,
        out_specs=[IN_SMEM] + [IN_VMEM] * 11,
        scratch_shapes=[pltpu.SMEM(x.shape, jnp.int32) for x in tables]
        + [
            pltpu.VMEM(cache_scale.shape, cache_scale.dtype),
            pltpu.VMEM((4, cache.shape[0], HD), F32),
            pltpu.SemaphoreType.DMA((5,)),
            pltpu.SemaphoreType.DMA((12,)),
            pltpu.SemaphoreType.DMA((48,)),
        ],
        compiler_params=pltpu.CompilerParams(vmem_limit_bytes=VMEM_LIMIT),
        cost_estimate=COST,
    )(ids, queries, suffix_kv, cache, *tables, cache_scale)


def wide(row):
    return jnp.broadcast_to(jnp.concatenate([row] * (TILE // HD), axis=1), (8, TILE))


def terms(tile, run):
    key = tile[run : run + 1]
    value = tile[RUNS + run : RUNS + run + 1]
    return wide(key * (LOG2E * INV_ROOT)), wide(jnp.log2(value)), wide(1.0 / value)


UNIT = None


def fold(q, keys, values_t, before, after, blocks_of):
    tiles = BOTH // TILE

    def score(t):
        return jnp.dot(keys, q[:, pl.ds(t * TILE, TILE)], preferred_element_type=F32)

    following = score(0)
    for t in range(tiles):
        scores = following
        if t + 1 < tiles:
            following = score(t + 1)
        cols = pl.ds(t * TILE, TILE)
        blocks = blocks_of(t)
        if before is None:
            old = jnp.full((8, TILE), masked_score, F32)
        else:
            old = before[REF_ROW : REF_ROW + 8, cols]
        parts = []
        highest = old
        for b, (term, dead, mask) in enumerate(blocks):
            part = scores[b * BLK : (b + 1) * BLK]
            part = part if mask is None else jnp.where(mask, part, masked_score)
            part = part.reshape(BLK // 8, 8, TILE)
            parts.append(part)
            top = jnp.max(part, axis=0) * (LOG2E * INV_ROOT if term is UNIT else term[0])
            if dead is not None:
                top = jnp.where(dead, masked_score, top)
            highest = jnp.maximum(highest, top)
        reference = jnp.broadcast_to(jnp.max(highest, axis=0, keepdims=True), (8, TILE))
        if before is None:
            total = jnp.zeros((8, TILE), F32)
        else:
            factor = jnp.exp2(old - reference)
            total = before[SUM_ROW : SUM_ROW + 8, cols] * factor
        rounded = []
        for part, (term, dead, mask) in zip(parts, blocks):
            shift = reference if term is UNIT else reference - term[1]
            if dead is not None:
                shift = jnp.where(dead, -masked_score, shift)
            scaled = part * (LOG2E * INV_ROOT if term is UNIT else term[0])
            weights = jnp.exp2(scaled - shift)
            summed = jnp.sum(weights, axis=0)
            total = total + (summed if term is UNIT else summed * term[2])
            rounded.append(weights.reshape(BLK, TILE).astype(BF16))
        rounded = jnp.concatenate(rounded, axis=0) if len(rounded) > 1 else rounded[0]
        product = jnp.dot(values_t, rounded, preferred_element_type=F32)
        if before is not None:
            held = before[:HD, cols].reshape(HD // 8, 8, TILE) * factor
            product = held.reshape(HD, TILE) + product
        after[:HD, cols] = product
        after[REF_ROW : REF_ROW + 8, cols] = reference
        after[SUM_ROW : SUM_ROW + 8, cols] = total


def add_pieces(q, before, after, pieces, ks, meta, extra=None):
    m = meta[META_M]
    n = len(ks)
    reach = jnp.where(((m // 2) * 2) * ROWS < meta[META_SUF], meta[META_LEN], 0)
    counts = [
        jnp.clip(reach - meta[META_J + RUNS * k + r] * BLK, 0, BLK) for k in ks for r in range(RUNS)
    ]
    most = functools.reduce(jnp.maximum, counts)
    ragged = functools.reduce(jnp.logical_or, [(c > 0) & (c < BLK) for c in counts])

    def whole(masked):
        blocks = []
        place = lax.broadcasted_iota(jnp.int32, (BLK, TILE), 0) if masked else None
        for i in range(n):
            tile = pieces[i][2 * PAIR :, :].astype(F32)
            for r in range(RUNS):
                c = counts[RUNS * i + r]
                blocks.append((terms(tile, r),) + ((None, place < c) if masked else (c < BLK, None)))
        keys = [pieces[i][:PAIR, :] for i in range(n)]
        values = [pieces[i][PAIR : 2 * PAIR, :].T for i in range(n)]
        blocks_of = lambda t: blocks
        if extra is not None:
            keys = [extra[0]] + keys
            values = [extra[1]] + values
            blocks_of = lambda t: extra[2](t) + blocks
        keys = jnp.concatenate(keys, axis=0) if len(keys) > 1 else keys[0]
        values = jnp.concatenate(values, axis=1) if len(values) > 1 else values[0]
        fold(q, keys, values, before, after, blocks_of)

    if extra is None:

        @pl.when(most == 0)
        def _():
            after[...] = before[...]

    some = jnp.bool_(True) if extra is not None else most > 0
    pl.when(some & jnp.logical_not(ragged))(functools.partial(whole, False))
    pl.when(some & ragged)(functools.partial(whole, True))


def state_shapes(slots):
    return [pltpu.VMEM((STATE, BOTH), F32)] * slots


def prepare_kernel(swap, own_q, own_kv, kv, q_all):
    for slot in range(2):
        kv[slot, 0] = own_kv[slot]
        kv[slot, 1, :ROWS, :] = swap[slot, :, WIDE : WIDE + HD]
        kv[slot, 1, ROWS:, :] = swap[slot, :, WIDE + HD :]
        for h in range(PER):
            rows = pl.ds(h * ROWS, ROWS)
            others = pl.ds(WIDE + h * ROWS, ROWS)
            q_all[slot, :, rows] = own_q[slot, :, h * HD : (h + 1) * HD].T
            q_all[slot, :, others] = swap[slot, :, h * HD : (h + 1) * HD].T


def prepare_call(swap, own_q, own_kv):
    return pl.pallas_call(
        prepare_kernel,
        out_shape=[pltpu.VMEM((2, 2, 2 * ROWS, HD), BF16), pltpu.VMEM((2, HD, BOTH), BF16)],
        in_specs=[IN_VMEM] * 3,
        out_specs=[IN_VMEM] * 2,
        compiler_params=pltpu.CompilerParams(vmem_limit_bytes=VMEM_LIMIT),
        cost_estimate=COST,
    )(swap, own_q, own_kv)


def own_kernel(meta, q_all, kv, own, *states):
    m = meta[META_M]
    key = lax.broadcasted_iota(jnp.int32, (BLK, TILE), 0)
    row = lax.broadcasted_iota(jnp.int32, (BLK, TILE), 1) % ROWS
    causal = key <= row
    odd = (m % 2) == 1

    def blocks_of(t):
        if t * TILE < WIDE:
            return [(UNIT, None, causal), (UNIT, jnp.logical_not(odd), None)]
        return [(UNIT, odd, None), (UNIT, None, causal)]

    for slot in range(2):
        keys = jnp.concatenate([kv[slot, side, :ROWS] for side in range(2)], axis=0)
        values = jnp.concatenate([kv[slot, side, ROWS:].T for side in range(2)], axis=1)
        add_pieces(
            q_all.at[slot],
            None,
            states[slot],
            [own.at[slot]],
            (0,),
            meta,
            (keys, values, blocks_of),
        )


def own_call(meta, q_all, kv, own):
    return pl.pallas_call(
        own_kernel,
        out_shape=state_shapes(2),
        in_specs=[IN_SMEM] + [IN_VMEM] * 3,
        out_specs=[IN_VMEM] * 2,
        compiler_params=pltpu.CompilerParams(vmem_limit_bytes=VMEM_LIMIT),
        cost_estimate=COST,
    )(meta, q_all, kv, own)


def add_kernel(slots, ks, early, last, meta, q_all, *refs):
    refs = list(refs)
    take = lambda n: [refs.pop(0) for _ in range(n)]
    before = take(len(slots))
    sources = take(len(ks))
    kv_early = take(1)[0] if early else None
    outs = take(2) if last else None
    after = take(len(slots))
    for w, slot in enumerate(slots):
        pieces = [s.at[slot] if len(s.shape) == 3 else s for s in sources]
        extra = None
        if early:
            unused = meta[META_M] < 2
            extra = (
                jnp.concatenate([kv_early[1 - slot, side, :ROWS] for side in range(2)], axis=0),
                jnp.concatenate([kv_early[1 - slot, side, ROWS:].T for side in range(2)], axis=1),
                lambda t: [(UNIT, unused, None)] * 2,
            )
        add_pieces(q_all.at[slot], before[w], after[w], pieces, ks, meta, extra)
    if last:
        state = after[0]
        for side, out in enumerate(outs):
            member = meta[META_M] ^ side
            row = lax.broadcasted_iota(jnp.int32, (HD, ROWS), 1) + member * ROWS
            for i in range(PER):
                cols = pl.ds(side * WIDE + i * ROWS, ROWS)
                piece = state[:HD, cols] * (1.0 / jnp.sum(state[SUM_ROW : SUM_ROW + 8, cols], axis=0, keepdims=True))
                piece = jnp.where(row < meta[META_SUF], piece, 0.0).astype(BF16)
                out[:, i * HD : (i + 1) * HD] = piece.T


def add_call(meta, q_all, states, sources, slots, ks, early=None, last=False):
    flat = [states[s] for s in slots]
    args = [meta, q_all, *flat, *sources] + ([] if early is None else [early])
    scratch = []
    if last:
        out_shape = [pltpu.VMEM((ROWS, WIDE), BF16)] * 2
        scratch = state_shapes(1)
    else:
        out_shape = state_shapes(len(slots))
    out = pl.pallas_call(
        functools.partial(add_kernel, slots, ks, early is not None, last),
        out_shape=out_shape,
        in_specs=[IN_SMEM] + [IN_VMEM] * (len(args) - 1),
        out_specs=[IN_VMEM] * len(out_shape),
        scratch_shapes=scratch,
        compiler_params=pltpu.CompilerParams(vmem_limit_bytes=VMEM_LIMIT),
        cost_estimate=COST,
    )(*args)
    if last:
        return out
    states = list(states)
    for w, slot in enumerate(slots):
        states[slot] = out[w]
    return states


def join_kernel(meta, *refs):
    out, sems = refs[4:]
    made = []
    for i, src in enumerate(refs[:4]):
        head = meta[META_M] ^ (2 * (i % 2) + i // 2)
        column = pl.multiple_of(head * WIDE, WIDE)
        made.append(pltpu.make_async_copy(src, out.at[:, pl.ds(column, WIDE)], sems.at[i]))
        made[-1].start()
    for x in made:
        x.wait()


def join_call(meta, mine, yours):
    return pl.pallas_call(
        join_kernel,
        out_shape=jax.ShapeDtypeStruct((ROWS, QH * HD), BF16),
        in_specs=[IN_SMEM] + [IN_VMEM] * 4,
        out_specs=IN_HBM,
        scratch_shapes=[pltpu.SemaphoreType.DMA((4,))],
        cost_estimate=COST,
    )(meta, *mine, *yours)


def permute(x, axis, count, k):
    return lax.ppermute(x, axis, [(i, i ^ k) for i in range(count)])


def per_device_small(
    queries, suffix_kv, cache, cache_scale, prefix_len, suffix_len, block_table, session_group
):
    ids = jnp.stack([lax.axis_index("pool"), lax.axis_index("blk")]).astype(jnp.int32)
    tables = [block_table, session_group, prefix_len, suffix_len]
    queries, suffix_kv, cache, scale, *tables = [
        pltpu.with_memory_space_constraint(x, pltpu.HBM)
        for x in (queries, suffix_kv, cache, cache_scale.T, *tables)
    ]
    meta, swap, *parts = gather_call(ids, queries, suffix_kv, cache, tables, scale)
    far, near = parts[:4], parts[4:7]
    own, own_q, own_kv = parts[7:]
    far_in, near_in, across = {}, {}, {}
    swap_in = permute(swap, "blk", 4, 1)
    for k in (4, 5):
        far_in[k] = permute(far[k - 4], "pool", POOL, k)
    for k in (1, 2):
        near_in[k] = permute(near[k - 1], "pool", POOL, k)
    kv, q_all = prepare_call(swap_in, own_q, own_kv)
    early = permute(kv, "blk", 4, 2)
    states = own_call(meta, q_all, kv, own)
    near[2], states = lax.optimization_barrier((near[2], states))
    near_in[3] = permute(near[2], "pool", POOL, 3)
    states = add_call(meta, q_all, states, [near_in[1]], (0, 1), (1,), early=early)
    far[2], far[3], near_in[2], far_in[4], far_in[5], states = lax.optimization_barrier(
        (far[2], far[3], near_in[2], far_in[4], far_in[5], states)
    )
    for k in (6, 7):
        far_in[k] = permute(far[k - 4], "pool", POOL, k)
    for k in (4, 5):
        across[k] = permute(far_in[k], "blk", 4, 2)
    states = add_call(meta, q_all, states, [far_in[4], far_in[5]], (0,), (4, 5))
    near_in[3], states = lax.optimization_barrier((near_in[3], states))
    states = add_call(meta, q_all, states, [near_in[2], near_in[3]], (0, 1), (2, 3))
    far_in[6], far_in[7], states = lax.optimization_barrier((far_in[6], far_in[7], states))
    for k in (6, 7):
        across[k] = permute(far_in[k], "blk", 4, 2)
    states = add_call(meta, q_all, states, [across[4], across[5]], (1,), (4, 5))
    mine, yours = [], []
    for slot, source in ((0, far_in), (1, across)):
        a, b = add_call(meta, q_all, states, [source[6], source[7]], (slot,), (6, 7), last=True)
        mine.append(pltpu.with_memory_space_constraint(a, pltpu.VMEM))
        yours.append(
            pltpu.with_memory_space_constraint(permute(b, "blk", 4, 1), pltpu.VMEM)
        )
    return join_call(meta, mine, yours)


def fold_keys(running, query_heads, key_rows, value_rows, key_scale, value_scale, usable):
    highest, weight_sum, weighted = running
    scores = jnp.einsum("kgrd,nkd->kgrn", query_heads, key_rows, preferred_element_type=jnp.float32)
    scores = scores * jnp.transpose(key_scale)[:, None, None, :]
    scores = jnp.where(usable[None, None], scores, masked_score)
    new_highest = jnp.maximum(highest, jnp.max(scores, axis=3))
    weights = jnp.where(usable[None, None], jnp.exp(scores - new_highest[..., None]), 0.0)
    factor = jnp.exp(highest - new_highest)
    weight_sum = weight_sum * factor + jnp.sum(weights, axis=3)
    rounded = (weights * jnp.transpose(value_scale)[:, None, None, :]).astype(jnp.bfloat16)
    weighted = weighted * factor[..., None] + jnp.einsum(
        "kgrn,nkd->kgrd", rounded, value_rows, preferred_element_type=jnp.float32
    )
    return (new_highest, weight_sum, weighted)


def per_device_any(
    queries, suffix_kv, cache, cache_scale, prefix_len, suffix_len, block_table, session_group
):
    local_rows = queries.shape[0]
    kv_heads = KVH
    per_group = QH // KVH
    head_size = HD
    pool_count = lax.axis_size("pool")
    member_count = lax.axis_size("blk")
    pool_index = lax.axis_index("pool")
    member_index = lax.axis_index("blk")
    slot_count = cache.shape[0]
    block_size = cache.shape[1]
    session_count = block_table.shape[0]
    block_count = block_table.shape[1]
    run_count = block_count // pool_count
    inv_root = 1.0 / math.sqrt(head_size)
    chooser = (
        session_group[:, None] == jnp.arange(session_count, dtype=jnp.int32)[None, :]
    ).astype(jnp.int32)
    tables = jnp.sum(chooser[:, :, None] * block_table[None], axis=1)
    holders = (tables // slot_count).reshape(pool_count, run_count, pool_count)
    places = (tables % slot_count).reshape(pool_count, run_count, pool_count)
    send_slots = jnp.sum(jnp.where(holders == pool_index, places, 0), axis=2)
    own_choice = lax.dynamic_index_in_dim(chooser, pool_index, 0, keepdims=False)
    prefix_length = jnp.sum(own_choice * prefix_len)
    suffix_length = jnp.sum(own_choice * suffix_len)
    own_holders = lax.dynamic_index_in_dim(holders, pool_index, 0, keepdims=False)
    positions = jnp.arange(block_count, dtype=jnp.int32).reshape(run_count, pool_count)
    matches = own_holders[None, :, :] == jnp.arange(pool_count, dtype=jnp.int32)[:, None, None]
    block_place = jnp.sum(jnp.where(matches, positions[None], 0), axis=2)
    scale_rows = cache_scale[send_slots]
    split_cache = cache.reshape(slot_count, block_size, 2 * kv_heads, head_size)
    share_size = 2 * kv_heads // member_count
    outgoing = lax.dynamic_slice_in_dim(
        split_cache[send_slots], member_index * share_size, share_size, 3
    )
    arrived_part, arrived_scale = (
        lax.all_to_all(outgoing, "pool", split_axis=0, concat_axis=0, tiled=True),
        lax.all_to_all(scale_rows, "pool", split_axis=0, concat_axis=0, tiled=True),
    )
    arrived = lax.all_gather(arrived_part, "blk", axis=3, tiled=True)
    prefix_tokens = pool_count * run_count * block_size
    step_tokens = min(1024, prefix_tokens)
    step_count = prefix_tokens // step_tokens
    prefix_stack = arrived.reshape(step_count, step_tokens, 2, kv_heads, head_size)
    token_scale = jnp.broadcast_to(
        arrived_scale.astype(jnp.float32).reshape(pool_count, run_count, 1, 2, kv_heads),
        (pool_count, run_count, block_size, 2, kv_heads),
    ).reshape(step_count, step_tokens, 2, kv_heads)
    token_place = (
        block_place[:, :, None] * block_size
        + jnp.arange(block_size, dtype=jnp.int32)[None, None, :]
    ).reshape(step_count, step_tokens)
    query_heads = jnp.transpose(
        queries.reshape(local_rows, kv_heads, per_group, head_size), (1, 2, 0, 3)
    )
    row_place = member_index * local_rows + jnp.arange(local_rows, dtype=jnp.int32)
    initial = (
        jnp.full((kv_heads, per_group, local_rows), masked_score, jnp.float32),
        jnp.zeros((kv_heads, per_group, local_rows), jnp.float32),
        jnp.zeros((kv_heads, per_group, local_rows, head_size), jnp.float32),
    )
    shard_rows = lax.all_gather(suffix_kv, "blk", axis=0, tiled=True)
    piece_count = shard_rows.shape[0]
    split_rows = shard_rows.reshape(piece_count, 2, kv_heads, head_size)
    key_place = jnp.arange(piece_count, dtype=jnp.int32)
    usable = (key_place[None, :] <= row_place[:, None]) & (key_place[None, :] < suffix_length)
    flat_scale = jnp.full((piece_count, kv_heads), inv_root, jnp.float32)
    unit_scale = jnp.ones((piece_count, kv_heads), jnp.float32)
    running = fold_keys(
        initial, query_heads, split_rows[:, 0], split_rows[:, 1], flat_scale, unit_scale, usable
    )

    def prefix_step(running, step_inputs):
        token_rows, scale_step, place_rows = step_inputs
        usable = (place_rows < prefix_length)[None, :]
        updated = fold_keys(
            running,
            query_heads,
            token_rows[:, 0],
            token_rows[:, 1],
            scale_step[:, 0] * inv_root,
            scale_step[:, 1],
            usable,
        )
        return (updated, None)

    running, unused = lax.scan(prefix_step, running, (prefix_stack, token_scale, token_place))
    highest, weight_sum, weighted = running
    result = weighted / weight_sum[..., None]
    result = jnp.transpose(result, (2, 0, 1, 3)).reshape(local_rows, QH * head_size)
    result = jnp.where((row_place < suffix_length)[:, None], result, 0.0)
    return result.astype(jnp.bfloat16)


def solution(mesh):
    small = dict(mesh.shape) == {"pool": POOL, "blk": 4}
    return jax.shard_map(
        per_device_small if small else per_device_any,
        mesh=mesh,
        in_specs=(
            P(("pool", "blk"), None),
            P(("pool", "blk"), None),
            P("pool", None, None),
            P("pool", None),
            P(),
            P(),
            P(),
            P(),
        ),
        out_specs=P(("pool", "blk"), None),
        check_vma=False,
    )
```

```python
import functools
import math

import jax
import jax.numpy as jnp
from jax import lax
from jax.experimental import pallas as pl
from jax.experimental.pallas import tpu as pltpu
from jax.sharding import PartitionSpec as P

QH = 32
KVH = 4
HD = 128
PER = QH // KVH
LOG2E = math.log2(math.e)
INV_ROOT = 1.0 / math.sqrt(HD)

masked_score = -1e30

RUNS = 2
BLK = 128
PAIR = RUNS * BLK
PIECE = 2 * PAIR + 16
ROWS = 128
WIDE = PER * ROWS
BOTH = 2 * WIDE
REF_ROW = HD
SUM_ROW = HD + 8
STATE = HD + 16
POOL = 8
META_J = 0
META_LEN = 2 * POOL
META_SUF = META_LEN + 1
META_M = META_LEN + 2
META_SIZE = 24
TILE = 1024
VMEM_LIMIT = 24 << 20
BF16 = jnp.bfloat16
F32 = jnp.float32
IN_VMEM = pl.BlockSpec(memory_space=pltpu.VMEM)
IN_SMEM = pl.BlockSpec(memory_space=pltpu.SMEM)
IN_HBM = pl.BlockSpec(memory_space=pltpu.HBM)


COST = pl.CostEstimate(flops=1 << 10, bytes_accessed=1 << 10, transcendentals=0)


def spread_scales(cache_scale, m, spread):
    scales = cache_scale[...].astype(F32).T
    column = lax.broadcasted_iota(jnp.int32, scales.shape, 1)
    for slot in range(2):
        for half in range(2):
            chosen = jnp.where(column == half * KVH + (m ^ (2 * slot)), scales, 0.0)
            one = jnp.sum(chosen, axis=1, keepdims=True)
            spread[2 * slot + half] = jnp.broadcast_to(one, (scales.shape[0], HD))


def write_scales(spread, locals_, slot, dst):
    row = lax.broadcasted_iota(jnp.int32, (16, HD), 0)
    rows = jnp.ones((16, HD), F32)
    for half in range(2):
        for run in range(RUNS):
            one = spread[2 * slot + half, pl.ds(locals_[run], 1), :]
            rows = jnp.where(row == half * RUNS + run, one, rows)
    dst[pl.ds(2 * PAIR, 16), :] = rows.astype(BF16)


def piece_copies(cache, locals_, head, dst, sems, first):
    made = []
    for half in range(2):
        column = pl.multiple_of((half * KVH + head) * HD, HD)
        for run in range(RUNS):
            made.append(
                pltpu.make_async_copy(
                    cache.at[locals_[run], :, pl.ds(column, HD)],
                    dst.at[pl.ds(half * PAIR + run * BLK, BLK), :],
                    sems.at[first + 2 * half + run],
                )
            )
    return made


PIECE_1 = pltpu.VMEM((PIECE, HD), BF16)
PIECE_2 = pltpu.VMEM((2, PIECE, HD), BF16)
SWAP = WIDE + 2 * HD


def gather_kernel(ids, queries, suffix_kv, cache, *refs):
    loads = list(zip(refs[:5], refs[17:22]))
    meta, swap = refs[5:7]
    far, near, own = refs[7:11], refs[11:14], refs[14]
    own_q, own_kv = refs[15:17]
    table, groups, lengths, suffixes, cache_scale = refs[17:22]
    spread, table_sems, more_sems, sems = refs[22:]
    p = ids[0]
    m = ids[1]
    loads = [
        pltpu.make_async_copy(a, b, table_sems.at[i]) for i, (a, b) in enumerate(loads)
    ]
    for c in loads:
        c.start()
    made = []
    for slot in range(2):
        mine = m ^ (2 * slot)
        theirs = mine ^ 1
        jobs = [
            (queries, theirs * WIDE, WIDE, swap.at[slot, :, pl.ds(0, WIDE)]),
            (suffix_kv, theirs * HD, HD, swap.at[slot, :, pl.ds(WIDE, HD)]),
            (suffix_kv, (KVH + theirs) * HD, HD, swap.at[slot, :, pl.ds(WIDE + HD, HD)]),
            (queries, mine * WIDE, WIDE, own_q.at[slot]),
            (suffix_kv, mine * HD, HD, own_kv.at[slot, pl.ds(0, ROWS), :]),
            (suffix_kv, (KVH + mine) * HD, HD, own_kv.at[slot, pl.ds(ROWS, ROWS), :]),
        ]
        for src, at, width, dst in jobs:
            src = src.at[:, pl.ds(pl.multiple_of(at, HD), width)]
            c = pltpu.make_async_copy(src, dst, more_sems.at[len(made)])
            c.start()
            made.append(c)
    for c in loads:
        c.wait()
    meta[META_M] = m
    slot_count = cache.shape[0]
    low = p * slot_count
    jobs = [(4 + i, (0,), (ref,)) for i, ref in enumerate(far)]
    jobs += [(1 + i, (0, 1), (ref.at[0], ref.at[1])) for i, ref in enumerate(near)]
    jobs += [(0, (0, 1), (own.at[0], own.at[1]))]
    pending = []
    count = 0
    for k, slots, outs in jobs:
        session = groups[p ^ k]
        locals_ = []
        for run in range(RUNS):
            local = jnp.int32(0)
            for jj in range(POOL):
                at = table[session, run * POOL + jj] - low
                local = jnp.where((at >= 0) & (at < slot_count), at, local)
            locals_.append(local)
        for slot, out in zip(slots, outs):
            group = piece_copies(cache, locals_, m ^ (2 * slot), out, sems, count)
            count += 4
            for c in group:
                c.start()
            made += group
            pending.append((locals_, slot, out))
    mine = groups[p]
    for run in range(RUNS):
        for jj in range(POOL):
            at = run * POOL + jj
            meta[META_J + RUNS * ((table[mine, at] // slot_count) ^ p) + run] = at
    meta[META_LEN] = lengths[mine]
    meta[META_SUF] = suffixes[mine]
    spread_scales(cache_scale, m, spread)
    for locals_, slot, out in pending:
        write_scales(spread, locals_, slot, out)
    for c in made:
        c.wait()


def gather_call(ids, queries, suffix_kv, cache, tables, cache_scale):
    return pl.pallas_call(
        gather_kernel,
        out_shape=[
            jax.ShapeDtypeStruct((META_SIZE,), jnp.int32),
            pltpu.VMEM((2, ROWS, SWAP), BF16),
        ]
        + [PIECE_1] * 4
        + [PIECE_2] * 4
        + [pltpu.VMEM((2, ROWS, WIDE), BF16), pltpu.VMEM((2, 2 * ROWS, HD), BF16)],
        in_specs=[IN_SMEM] + [IN_HBM] * 8,
        out_specs=[IN_SMEM] + [IN_VMEM] * 11,
        scratch_shapes=[pltpu.SMEM(x.shape, jnp.int32) for x in tables]
        + [
            pltpu.VMEM(cache_scale.shape, cache_scale.dtype),
            pltpu.VMEM((4, cache.shape[0], HD), F32),
            pltpu.SemaphoreType.DMA((5,)),
            pltpu.SemaphoreType.DMA((12,)),
            pltpu.SemaphoreType.DMA((48,)),
        ],
        compiler_params=pltpu.CompilerParams(vmem_limit_bytes=VMEM_LIMIT),
        cost_estimate=COST,
    )(ids, queries, suffix_kv, cache, *tables, cache_scale)


def wide(row):
    return jnp.broadcast_to(jnp.concatenate([row] * (TILE // HD), axis=1), (8, TILE))


def terms(tile, run):
    value = tile[RUNS + run : RUNS + run + 1]
    return wide(jnp.log2(value)), wide(1.0 / value)


def scaled_keys(keys, scale):
    whole = keys.astype(F32) * (scale * (LOG2E * INV_ROOT))
    high = whole.astype(BF16)
    return jnp.concatenate([high, (whole - high.astype(F32)).astype(BF16)], axis=1)


UNIT = None


def fold(q, keys, values_t, before, after, blocks_of):
    tiles = BOTH // TILE

    def score(t):
        return jnp.dot(keys, q[:, pl.ds(t * TILE, TILE)], preferred_element_type=F32)

    following = score(0)
    for t in range(tiles):
        scores = following
        if t + 1 < tiles:
            following = score(t + 1)
        cols = pl.ds(t * TILE, TILE)
        blocks = blocks_of(t)
        if before is None:
            old = jnp.full((8, TILE), masked_score, F32)
        else:
            old = before[REF_ROW : REF_ROW + 8, cols]
        parts = []
        highest = old
        for b, (term, dead, mask) in enumerate(blocks):
            part = scores[b * BLK : (b + 1) * BLK]
            part = part if mask is None else jnp.where(mask, part, masked_score)
            part = part.reshape(BLK // 8, 8, TILE)
            parts.append(part)
            top = jnp.max(part, axis=0)
            if dead is not None:
                top = jnp.where(dead, masked_score, top)
            highest = jnp.maximum(highest, top)
        reference = jnp.broadcast_to(jnp.max(highest, axis=0, keepdims=True), (8, TILE))
        if before is None:
            total = jnp.zeros((8, TILE), F32)
        else:
            factor = jnp.exp2(old - reference)
            total = before[SUM_ROW : SUM_ROW + 8, cols] * factor
        rounded = []
        for part, (term, dead, mask) in zip(parts, blocks):
            shift = reference if term is UNIT else reference - term[0]
            if dead is not None:
                shift = jnp.where(dead, -masked_score, shift)
            weights = jnp.exp2(part - shift)
            summed = jnp.sum(weights, axis=0)
            total = total + (summed if term is UNIT else summed * term[1])
            rounded.append(weights.reshape(BLK, TILE).astype(BF16))
        rounded = jnp.concatenate(rounded, axis=0) if len(rounded) > 1 else rounded[0]
        product = jnp.dot(values_t, rounded, preferred_element_type=F32)
        if before is not None:
            held = before[:HD, cols].reshape(HD // 8, 8, TILE) * factor
            product = held.reshape(HD, TILE) + product
        after[:HD, cols] = product
        after[REF_ROW : REF_ROW + 8, cols] = reference
        after[SUM_ROW : SUM_ROW + 8, cols] = total


def add_pieces(q, before, after, pieces, ks, meta, extra=None):
    m = meta[META_M]
    n = len(ks)
    reach = jnp.where(((m // 2) * 2) * ROWS < meta[META_SUF], meta[META_LEN], 0)
    counts = [
        jnp.clip(reach - meta[META_J + RUNS * k + r] * BLK, 0, BLK) for k in ks for r in range(RUNS)
    ]
    most = functools.reduce(jnp.maximum, counts)
    ragged = functools.reduce(jnp.logical_or, [(c > 0) & (c < BLK) for c in counts])

    def whole(masked):
        blocks = []
        place = lax.broadcasted_iota(jnp.int32, (BLK, TILE), 0) if masked else None
        for i in range(n):
            tile = pieces[i][2 * PAIR :, :].astype(F32)
            for r in range(RUNS):
                c = counts[RUNS * i + r]
                blocks.append((terms(tile, r),) + ((None, place < c) if masked else (c < BLK, None)))
        keys = []
        for i in range(n):
            tile = pieces[i][2 * PAIR :, :].astype(F32)
            for r in range(RUNS):
                block = pieces[i][r * BLK : (r + 1) * BLK, :]
                keys.append(scaled_keys(block, tile[r : r + 1]))
        values = [pieces[i][PAIR : 2 * PAIR, :].T for i in range(n)]
        blocks_of = lambda t: blocks
        if extra is not None:
            keys = [scaled_keys(extra[0], 1.0)] + keys
            values = [extra[1]] + values
            blocks_of = lambda t: extra[2](t) + blocks
        keys = jnp.concatenate(keys, axis=0)
        values = jnp.concatenate(values, axis=1) if len(values) > 1 else values[0]
        fold(q, keys, values, before, after, blocks_of)

    if extra is None:

        @pl.when(most == 0)
        def _():
            after[...] = before[...]

    some = jnp.bool_(True) if extra is not None else most > 0
    pl.when(some & jnp.logical_not(ragged))(functools.partial(whole, False))
    pl.when(some & ragged)(functools.partial(whole, True))


def state_shapes(slots):
    return [pltpu.VMEM((STATE, BOTH), F32)] * slots


def prepare_kernel(swap, own_q, own_kv, kv, q_all):
    for slot in range(2):
        kv[slot, 0] = own_kv[slot]
        kv[slot, 1, :ROWS, :] = swap[slot, :, WIDE : WIDE + HD]
        kv[slot, 1, ROWS:, :] = swap[slot, :, WIDE + HD :]
        for h in range(PER):
            rows = pl.ds(h * ROWS, ROWS)
            others = pl.ds(WIDE + h * ROWS, ROWS)
            mine = own_q[slot, :, h * HD : (h + 1) * HD].T
            theirs = swap[slot, :, h * HD : (h + 1) * HD].T
            for copy in range(2):
                q_all[slot, copy * HD : (copy + 1) * HD, rows] = mine
                q_all[slot, copy * HD : (copy + 1) * HD, others] = theirs


def prepare_call(swap, own_q, own_kv):
    return pl.pallas_call(
        prepare_kernel,
        out_shape=[pltpu.VMEM((2, 2, 2 * ROWS, HD), BF16), pltpu.VMEM((2, 2 * HD, BOTH), BF16)],
        in_specs=[IN_VMEM] * 3,
        out_specs=[IN_VMEM] * 2,
        compiler_params=pltpu.CompilerParams(vmem_limit_bytes=VMEM_LIMIT),
        cost_estimate=COST,
    )(swap, own_q, own_kv)


def own_kernel(meta, q_all, kv, own, *states):
    m = meta[META_M]
    key = lax.broadcasted_iota(jnp.int32, (BLK, TILE), 0)
    row = lax.broadcasted_iota(jnp.int32, (BLK, TILE), 1) % ROWS
    causal = key <= row
    odd = (m % 2) == 1

    def blocks_of(t):
        if t * TILE < WIDE:
            return [(UNIT, None, causal), (UNIT, jnp.logical_not(odd), None)]
        return [(UNIT, odd, None), (UNIT, None, causal)]

    for slot in range(2):
        keys = jnp.concatenate([kv[slot, side, :ROWS] for side in range(2)], axis=0)
        values = jnp.concatenate([kv[slot, side, ROWS:].T for side in range(2)], axis=1)
        add_pieces(
            q_all.at[slot],
            None,
            states[slot],
            [own.at[slot]],
            (0,),
            meta,
            (keys, values, blocks_of),
        )


def own_call(meta, q_all, kv, own):
    return pl.pallas_call(
        own_kernel,
        out_shape=state_shapes(2),
        in_specs=[IN_SMEM] + [IN_VMEM] * 3,
        out_specs=[IN_VMEM] * 2,
        compiler_params=pltpu.CompilerParams(vmem_limit_bytes=VMEM_LIMIT),
        cost_estimate=COST,
    )(meta, q_all, kv, own)


def add_kernel(slots, ks, early, last, meta, q_all, *refs):
    refs = list(refs)
    take = lambda n: [refs.pop(0) for _ in range(n)]
    before = take(len(slots))
    sources = take(len(ks))
    kv_early = take(1)[0] if early else None
    outs = take(2) if last else None
    after = take(len(slots))
    for w, slot in enumerate(slots):
        pieces = [s.at[slot] if len(s.shape) == 3 else s for s in sources]
        extra = None
        if early:
            unused = meta[META_M] < 2
            extra = (
                jnp.concatenate([kv_early[1 - slot, side, :ROWS] for side in range(2)], axis=0),
                jnp.concatenate([kv_early[1 - slot, side, ROWS:].T for side in range(2)], axis=1),
                lambda t: [(UNIT, unused, None)] * 2,
            )
        add_pieces(q_all.at[slot], before[w], after[w], pieces, ks, meta, extra)
    if last:
        state = after[0]
        for side, out in enumerate(outs):
            member = meta[META_M] ^ side
            row = lax.broadcasted_iota(jnp.int32, (HD, ROWS), 1) + member * ROWS
            for i in range(PER):
                cols = pl.ds(side * WIDE + i * ROWS, ROWS)
                piece = state[:HD, cols] * (1.0 / jnp.sum(state[SUM_ROW : SUM_ROW + 8, cols], axis=0, keepdims=True))
                piece = jnp.where(row < meta[META_SUF], piece, 0.0).astype(BF16)
                out[:, i * HD : (i + 1) * HD] = piece.T


def add_call(meta, q_all, states, sources, slots, ks, early=None, last=False):
    flat = [states[s] for s in slots]
    args = [meta, q_all, *flat, *sources] + ([] if early is None else [early])
    scratch = []
    if last:
        out_shape = [pltpu.VMEM((ROWS, WIDE), BF16)] * 2
        scratch = state_shapes(1)
    else:
        out_shape = state_shapes(len(slots))
    out = pl.pallas_call(
        functools.partial(add_kernel, slots, ks, early is not None, last),
        out_shape=out_shape,
        in_specs=[IN_SMEM] + [IN_VMEM] * (len(args) - 1),
        out_specs=[IN_VMEM] * len(out_shape),
        scratch_shapes=scratch,
        compiler_params=pltpu.CompilerParams(vmem_limit_bytes=VMEM_LIMIT),
        cost_estimate=COST,
    )(*args)
    if last:
        return out
    states = list(states)
    for w, slot in enumerate(slots):
        states[slot] = out[w]
    return states


def join_kernel(meta, *refs):
    out, sems = refs[4:]
    made = []
    for i, src in enumerate(refs[:4]):
        head = meta[META_M] ^ (2 * (i % 2) + i // 2)
        column = pl.multiple_of(head * WIDE, WIDE)
        made.append(pltpu.make_async_copy(src, out.at[:, pl.ds(column, WIDE)], sems.at[i]))
        made[-1].start()
    for x in made:
        x.wait()


def join_call(meta, mine, yours):
    return pl.pallas_call(
        join_kernel,
        out_shape=jax.ShapeDtypeStruct((ROWS, QH * HD), BF16),
        in_specs=[IN_SMEM] + [IN_VMEM] * 4,
        out_specs=IN_HBM,
        scratch_shapes=[pltpu.SemaphoreType.DMA((4,))],
        cost_estimate=COST,
    )(meta, *mine, *yours)


def permute(x, axis, count, k):
    return lax.ppermute(x, axis, [(i, i ^ k) for i in range(count)])


def per_device_small(
    queries, suffix_kv, cache, cache_scale, prefix_len, suffix_len, block_table, session_group
):
    ids = jnp.stack([lax.axis_index("pool"), lax.axis_index("blk")]).astype(jnp.int32)
    tables = [block_table, session_group, prefix_len, suffix_len]
    queries, suffix_kv, cache, scale, *tables = [
        pltpu.with_memory_space_constraint(x, pltpu.HBM)
        for x in (queries, suffix_kv, cache, cache_scale.T, *tables)
    ]
    meta, swap, *parts = gather_call(ids, queries, suffix_kv, cache, tables, scale)
    far, near = parts[:4], parts[4:7]
    own, own_q, own_kv = parts[7:]
    far_in, near_in, across = {}, {}, {}
    swap_in = permute(swap, "blk", 4, 1)
    for k in (4, 5):
        far_in[k] = permute(far[k - 4], "pool", POOL, k)
    for k in (1, 2):
        near_in[k] = permute(near[k - 1], "pool", POOL, k)
    kv, q_all = prepare_call(swap_in, own_q, own_kv)
    early = permute(kv, "blk", 4, 2)
    states = own_call(meta, q_all, kv, own)
    near[2], states = lax.optimization_barrier((near[2], states))
    near_in[3] = permute(near[2], "pool", POOL, 3)
    states = add_call(meta, q_all, states, [near_in[1], near_in[2]], (0, 1), (1, 2), early=early)
    far[2], far[3], far_in[4], far_in[5], states = lax.optimization_barrier(
        (far[2], far[3], far_in[4], far_in[5], states)
    )
    for k in (6, 7):
        far_in[k] = permute(far[k - 4], "pool", POOL, k)
    for k in (4, 5):
        across[k] = permute(far_in[k], "blk", 4, 2)
    states = add_call(meta, q_all, states, [far_in[4], far_in[5]], (0,), (4, 5))
    near_in[3], states = lax.optimization_barrier((near_in[3], states))
    states = add_call(meta, q_all, states, [near_in[3]], (0, 1), (3,))
    far_in[6], far_in[7], states = lax.optimization_barrier((far_in[6], far_in[7], states))
    for k in (6, 7):
        across[k] = permute(far_in[k], "blk", 4, 2)
    states = add_call(meta, q_all, states, [across[4], across[5]], (1,), (4, 5))
    mine, yours = [], []
    for slot, source in ((0, far_in), (1, across)):
        a, b = add_call(meta, q_all, states, [source[6], source[7]], (slot,), (6, 7), last=True)
        mine.append(pltpu.with_memory_space_constraint(a, pltpu.VMEM))
        yours.append(
            pltpu.with_memory_space_constraint(permute(b, "blk", 4, 1), pltpu.VMEM)
        )
    return join_call(meta, mine, yours)


def fold_keys(running, query_heads, key_rows, value_rows, key_scale, value_scale, usable):
    highest, weight_sum, weighted = running
    scores = jnp.einsum("kgrd,nkd->kgrn", query_heads, key_rows, preferred_element_type=jnp.float32)
    scores = scores * jnp.transpose(key_scale)[:, None, None, :]
    scores = jnp.where(usable[None, None], scores, masked_score)
    new_highest = jnp.maximum(highest, jnp.max(scores, axis=3))
    weights = jnp.where(usable[None, None], jnp.exp(scores - new_highest[..., None]), 0.0)
    factor = jnp.exp(highest - new_highest)
    weight_sum = weight_sum * factor + jnp.sum(weights, axis=3)
    rounded = (weights * jnp.transpose(value_scale)[:, None, None, :]).astype(jnp.bfloat16)
    weighted = weighted * factor[..., None] + jnp.einsum(
        "kgrn,nkd->kgrd", rounded, value_rows, preferred_element_type=jnp.float32
    )
    return (new_highest, weight_sum, weighted)


def per_device_any(
    queries, suffix_kv, cache, cache_scale, prefix_len, suffix_len, block_table, session_group
):
    local_rows = queries.shape[0]
    kv_heads = KVH
    per_group = QH // KVH
    head_size = HD
    pool_count = lax.axis_size("pool")
    member_count = lax.axis_size("blk")
    pool_index = lax.axis_index("pool")
    member_index = lax.axis_index("blk")
    slot_count = cache.shape[0]
    block_size = cache.shape[1]
    session_count = block_table.shape[0]
    block_count = block_table.shape[1]
    run_count = block_count // pool_count
    inv_root = 1.0 / math.sqrt(head_size)
    chooser = (
        session_group[:, None] == jnp.arange(session_count, dtype=jnp.int32)[None, :]
    ).astype(jnp.int32)
    tables = jnp.sum(chooser[:, :, None] * block_table[None], axis=1)
    holders = (tables // slot_count).reshape(pool_count, run_count, pool_count)
    places = (tables % slot_count).reshape(pool_count, run_count, pool_count)
    send_slots = jnp.sum(jnp.where(holders == pool_index, places, 0), axis=2)
    own_choice = lax.dynamic_index_in_dim(chooser, pool_index, 0, keepdims=False)
    prefix_length = jnp.sum(own_choice * prefix_len)
    suffix_length = jnp.sum(own_choice * suffix_len)
    own_holders = lax.dynamic_index_in_dim(holders, pool_index, 0, keepdims=False)
    positions = jnp.arange(block_count, dtype=jnp.int32).reshape(run_count, pool_count)
    matches = own_holders[None, :, :] == jnp.arange(pool_count, dtype=jnp.int32)[:, None, None]
    block_place = jnp.sum(jnp.where(matches, positions[None], 0), axis=2)
    scale_rows = cache_scale[send_slots]
    split_cache = cache.reshape(slot_count, block_size, 2 * kv_heads, head_size)
    share_size = 2 * kv_heads // member_count
    outgoing = lax.dynamic_slice_in_dim(
        split_cache[send_slots], member_index * share_size, share_size, 3
    )
    arrived_part, arrived_scale = (
        lax.all_to_all(outgoing, "pool", split_axis=0, concat_axis=0, tiled=True),
        lax.all_to_all(scale_rows, "pool", split_axis=0, concat_axis=0, tiled=True),
    )
    arrived = lax.all_gather(arrived_part, "blk", axis=3, tiled=True)
    prefix_tokens = pool_count * run_count * block_size
    step_tokens = min(1024, prefix_tokens)
    step_count = prefix_tokens // step_tokens
    prefix_stack = arrived.reshape(step_count, step_tokens, 2, kv_heads, head_size)
    token_scale = jnp.broadcast_to(
        arrived_scale.astype(jnp.float32).reshape(pool_count, run_count, 1, 2, kv_heads),
        (pool_count, run_count, block_size, 2, kv_heads),
    ).reshape(step_count, step_tokens, 2, kv_heads)
    token_place = (
        block_place[:, :, None] * block_size
        + jnp.arange(block_size, dtype=jnp.int32)[None, None, :]
    ).reshape(step_count, step_tokens)
    query_heads = jnp.transpose(
        queries.reshape(local_rows, kv_heads, per_group, head_size), (1, 2, 0, 3)
    )
    row_place = member_index * local_rows + jnp.arange(local_rows, dtype=jnp.int32)
    initial = (
        jnp.full((kv_heads, per_group, local_rows), masked_score, jnp.float32),
        jnp.zeros((kv_heads, per_group, local_rows), jnp.float32),
        jnp.zeros((kv_heads, per_group, local_rows, head_size), jnp.float32),
    )
    shard_rows = lax.all_gather(suffix_kv, "blk", axis=0, tiled=True)
    piece_count = shard_rows.shape[0]
    split_rows = shard_rows.reshape(piece_count, 2, kv_heads, head_size)
    key_place = jnp.arange(piece_count, dtype=jnp.int32)
    usable = (key_place[None, :] <= row_place[:, None]) & (key_place[None, :] < suffix_length)
    flat_scale = jnp.full((piece_count, kv_heads), inv_root, jnp.float32)
    unit_scale = jnp.ones((piece_count, kv_heads), jnp.float32)
    running = fold_keys(
        initial, query_heads, split_rows[:, 0], split_rows[:, 1], flat_scale, unit_scale, usable
    )

    def prefix_step(running, step_inputs):
        token_rows, scale_step, place_rows = step_inputs
        usable = (place_rows < prefix_length)[None, :]
        updated = fold_keys(
            running,
            query_heads,
            token_rows[:, 0],
            token_rows[:, 1],
            scale_step[:, 0] * inv_root,
            scale_step[:, 1],
            usable,
        )
        return (updated, None)

    running, unused = lax.scan(prefix_step, running, (prefix_stack, token_scale, token_place))
    highest, weight_sum, weighted = running
    result = weighted / weight_sum[..., None]
    result = jnp.transpose(result, (2, 0, 1, 3)).reshape(local_rows, QH * head_size)
    result = jnp.where((row_place < suffix_length)[:, None], result, 0.0)
    return result.astype(jnp.bfloat16)


def solution(mesh):
    small = dict(mesh.shape) == {"pool": POOL, "blk": 4}
    return jax.shard_map(
        per_device_small if small else per_device_any,
        mesh=mesh,
        in_specs=(
            P(("pool", "blk"), None),
            P(("pool", "blk"), None),
            P("pool", None, None),
            P("pool", None),
            P(),
            P(),
            P(),
            P(),
        ),
        out_specs=P(("pool", "blk"), None),
        check_vma=False,
    )
```

```python
import functools
import math

import jax
import jax.numpy as jnp
from jax import lax
from jax.experimental import pallas as pl
from jax.experimental.pallas import tpu as pltpu
from jax.sharding import PartitionSpec as P

QH = 32
KVH = 4
HD = 128
PER = QH // KVH
LOG2E = math.log2(math.e)
INV_ROOT = 1.0 / math.sqrt(HD)

masked_score = -1e30

RUNS = 2
BLK = 128
PAIR = RUNS * BLK
PIECE = 2 * PAIR + 16
ROWS = 128
WIDE = PER * ROWS
BOTH = 2 * WIDE
REF_ROW = HD
SUM_ROW = HD + 8
STATE = HD + 16
POOL = 8
META_J = 0
META_LEN = 2 * POOL
META_SUF = META_LEN + 1
META_M = META_LEN + 2
META_SIZE = 24
TILE = 1024
VMEM_LIMIT = 24 << 20
BF16 = jnp.bfloat16
F32 = jnp.float32
IN_VMEM = pl.BlockSpec(memory_space=pltpu.VMEM)
IN_SMEM = pl.BlockSpec(memory_space=pltpu.SMEM)
IN_HBM = pl.BlockSpec(memory_space=pltpu.HBM)


COST = pl.CostEstimate(flops=1 << 10, bytes_accessed=1 << 10, transcendentals=0)


def spread_scales(cache_scale, m, spread):
    scales = cache_scale[...].astype(F32).T
    column = lax.broadcasted_iota(jnp.int32, scales.shape, 1)
    for slot in range(2):
        for half in range(2):
            chosen = jnp.where(column == half * KVH + (m ^ (2 * slot)), scales, 0.0)
            one = jnp.sum(chosen, axis=1, keepdims=True)
            spread[2 * slot + half] = jnp.broadcast_to(one, (scales.shape[0], HD))


def write_scales(spread, locals_, slot, dst):
    row = lax.broadcasted_iota(jnp.int32, (16, HD), 0)
    rows = jnp.ones((16, HD), F32)
    for half in range(2):
        for run in range(RUNS):
            one = spread[2 * slot + half, pl.ds(locals_[run], 1), :]
            rows = jnp.where(row == half * RUNS + run, one, rows)
    dst[pl.ds(2 * PAIR, 16), :] = rows.astype(BF16)


PIECE_1 = pltpu.VMEM((PIECE, HD), BF16)
PIECE_2 = pltpu.VMEM((2, PIECE, HD), BF16)
SWAP = WIDE + 2 * HD


def gather_kernel(ids, queries, suffix_kv, cache, *refs):
    loads = list(zip(refs[:5], refs[17:22]))
    meta, swap = refs[5:7]
    far, near, own = refs[7:11], refs[11:14], refs[14]
    own_q, own_kv = refs[15:17]
    table, groups, lengths, suffixes, cache_scale = refs[17:22]
    spread, stage, table_sems, more_sems, stage_sems = refs[22:]
    p = ids[0]
    m = ids[1]
    loads = [
        pltpu.make_async_copy(a, b, table_sems.at[i]) for i, (a, b) in enumerate(loads)
    ]
    for c in loads:
        c.start()
    staged = []
    for i in range(4):
        column = pl.multiple_of((i % 2 * KVH + (m ^ (2 * (i // 2)))) * HD, HD)
        c = pltpu.make_async_copy(
            cache.at[:, :, pl.ds(column, HD)], stage.at[i], stage_sems.at[i]
        )
        c.start()
        staged.append(c)
    made = []
    for slot in range(2):
        mine = m ^ (2 * slot)
        theirs = mine ^ 1
        jobs = [
            (queries, theirs * WIDE, WIDE, swap.at[slot, :, pl.ds(0, WIDE)]),
            (suffix_kv, theirs * HD, HD, swap.at[slot, :, pl.ds(WIDE, HD)]),
            (suffix_kv, (KVH + theirs) * HD, HD, swap.at[slot, :, pl.ds(WIDE + HD, HD)]),
            (queries, mine * WIDE, WIDE, own_q.at[slot]),
            (suffix_kv, mine * HD, HD, own_kv.at[slot, pl.ds(0, ROWS), :]),
            (suffix_kv, (KVH + mine) * HD, HD, own_kv.at[slot, pl.ds(ROWS, ROWS), :]),
        ]
        for src, at, width, dst in jobs:
            src = src.at[:, pl.ds(pl.multiple_of(at, HD), width)]
            c = pltpu.make_async_copy(src, dst, more_sems.at[len(made)])
            c.start()
            made.append(c)
    for c in loads:
        c.wait()
    meta[META_M] = m
    slot_count = cache.shape[0]
    low = p * slot_count
    jobs = [(4 + i, (0,), (ref,)) for i, ref in enumerate(far)]
    jobs += [(1 + i, (0, 1), (ref.at[0], ref.at[1])) for i, ref in enumerate(near)]
    jobs += [(0, (0, 1), (own.at[0], own.at[1]))]
    pending = []
    for k, slots, outs in jobs:
        session = groups[p ^ k]
        locals_ = []
        for run in range(RUNS):
            local = jnp.int32(0)
            for jj in range(POOL):
                at = table[session, run * POOL + jj] - low
                local = jnp.where((at >= 0) & (at < slot_count), at, local)
            locals_.append(local)
        for slot, out in zip(slots, outs):
            pending.append((locals_, slot, out))
    mine = groups[p]
    for run in range(RUNS):
        for jj in range(POOL):
            at = run * POOL + jj
            meta[META_J + RUNS * ((table[mine, at] // slot_count) ^ p) + run] = at
    meta[META_LEN] = lengths[mine]
    meta[META_SUF] = suffixes[mine]
    spread_scales(cache_scale, m, spread)
    for locals_, slot, out in pending:
        write_scales(spread, locals_, slot, out)
    for c in staged:
        c.wait()
    for locals_, slot, out in pending:
        for half in range(2):
            for run in range(RUNS):
                rows = pl.ds(half * PAIR + run * BLK, BLK)
                out[rows, :] = stage[2 * slot + half, locals_[run]]
    for c in made:
        c.wait()


def gather_call(ids, queries, suffix_kv, cache, tables, cache_scale):
    return pl.pallas_call(
        gather_kernel,
        out_shape=[
            jax.ShapeDtypeStruct((META_SIZE,), jnp.int32),
            pltpu.VMEM((2, ROWS, SWAP), BF16),
        ]
        + [PIECE_1] * 4
        + [PIECE_2] * 4
        + [pltpu.VMEM((2, ROWS, WIDE), BF16), pltpu.VMEM((2, 2 * ROWS, HD), BF16)],
        in_specs=[IN_SMEM] + [IN_HBM] * 8,
        out_specs=[IN_SMEM] + [IN_VMEM] * 11,
        scratch_shapes=[pltpu.SMEM(x.shape, jnp.int32) for x in tables]
        + [
            pltpu.VMEM(cache_scale.shape, cache_scale.dtype),
            pltpu.VMEM((4, cache.shape[0], HD), F32),
            pltpu.VMEM((4, cache.shape[0], BLK, HD), BF16),
            pltpu.SemaphoreType.DMA((5,)),
            pltpu.SemaphoreType.DMA((12,)),
            pltpu.SemaphoreType.DMA((4,)),
        ],
        compiler_params=pltpu.CompilerParams(vmem_limit_bytes=VMEM_LIMIT),
        cost_estimate=COST,
    )(ids, queries, suffix_kv, cache, *tables, cache_scale)


def wide(row):
    return jnp.broadcast_to(jnp.concatenate([row] * (TILE // HD), axis=1), (8, TILE))


def terms(tile, run):
    value = tile[RUNS + run : RUNS + run + 1]
    return wide(jnp.log2(value)), wide(1.0 / value)


def scaled_keys(keys, scale):
    whole = keys.astype(F32) * (scale * (LOG2E * INV_ROOT))
    high = whole.astype(BF16)
    return jnp.concatenate([high, (whole - high.astype(F32)).astype(BF16)], axis=1)


UNIT = None


def fold(q, keys, values_t, before, after, blocks_of):
    tiles = BOTH // TILE

    def score(t):
        return jnp.dot(keys, q[:, pl.ds(t * TILE, TILE)], preferred_element_type=F32)

    following = score(0)
    for t in range(tiles):
        scores = following
        if t + 1 < tiles:
            following = score(t + 1)
        cols = pl.ds(t * TILE, TILE)
        blocks = blocks_of(t)
        if before is None:
            old = jnp.full((8, TILE), masked_score, F32)
        else:
            old = before[REF_ROW : REF_ROW + 8, cols]
        parts = []
        highest = old
        for b, (term, dead, mask) in enumerate(blocks):
            part = scores[b * BLK : (b + 1) * BLK]
            part = part if mask is None else jnp.where(mask, part, masked_score)
            part = part.reshape(BLK // 8, 8, TILE)
            parts.append(part)
            top = jnp.max(part, axis=0)
            if dead is not None:
                top = jnp.where(dead, masked_score, top)
            highest = jnp.maximum(highest, top)
        reference = jnp.broadcast_to(jnp.max(highest, axis=0, keepdims=True), (8, TILE))
        if before is None:
            total = jnp.zeros((8, TILE), F32)
        else:
            factor = jnp.exp2(old - reference)
            total = before[SUM_ROW : SUM_ROW + 8, cols] * factor
        rounded = []
        for part, (term, dead, mask) in zip(parts, blocks):
            shift = reference if term is UNIT else reference - term[0]
            if dead is not None:
                shift = jnp.where(dead, -masked_score, shift)
            weights = jnp.exp2(part - shift)
            summed = jnp.sum(weights, axis=0)
            total = total + (summed if term is UNIT else summed * term[1])
            rounded.append(weights.reshape(BLK, TILE).astype(BF16))
        rounded = jnp.concatenate(rounded, axis=0) if len(rounded) > 1 else rounded[0]
        product = jnp.dot(values_t, rounded, preferred_element_type=F32)
        if before is not None:
            held = before[:HD, cols].reshape(HD // 8, 8, TILE) * factor
            product = held.reshape(HD, TILE) + product
        after[:HD, cols] = product
        after[REF_ROW : REF_ROW + 8, cols] = reference
        after[SUM_ROW : SUM_ROW + 8, cols] = total


def add_pieces(q, before, after, pieces, ks, meta, extra=None):
    m = meta[META_M]
    n = len(ks)
    reach = jnp.where(((m // 2) * 2) * ROWS < meta[META_SUF], meta[META_LEN], 0)
    counts = [
        jnp.clip(reach - meta[META_J + RUNS * k + r] * BLK, 0, BLK) for k in ks for r in range(RUNS)
    ]
    most = functools.reduce(jnp.maximum, counts)
    ragged = functools.reduce(jnp.logical_or, [(c > 0) & (c < BLK) for c in counts])

    def whole(masked):
        blocks = []
        place = lax.broadcasted_iota(jnp.int32, (BLK, TILE), 0) if masked else None
        for i in range(n):
            tile = pieces[i][2 * PAIR :, :].astype(F32)
            for r in range(RUNS):
                c = counts[RUNS * i + r]
                blocks.append((terms(tile, r),) + ((None, place < c) if masked else (c < BLK, None)))
        keys = []
        for i in range(n):
            tile = pieces[i][2 * PAIR :, :].astype(F32)
            for r in range(RUNS):
                block = pieces[i][r * BLK : (r + 1) * BLK, :]
                keys.append(scaled_keys(block, tile[r : r + 1]))
        values = [pieces[i][PAIR : 2 * PAIR, :].T for i in range(n)]
        blocks_of = lambda t: blocks
        if extra is not None:
            keys = [scaled_keys(extra[0], 1.0)] + keys
            values = [extra[1]] + values
            blocks_of = lambda t: extra[2](t) + blocks
        keys = jnp.concatenate(keys, axis=0)
        values = jnp.concatenate(values, axis=1) if len(values) > 1 else values[0]
        fold(q, keys, values, before, after, blocks_of)

    if extra is None:

        @pl.when(most == 0)
        def _():
            after[...] = before[...]

    some = jnp.bool_(True) if extra is not None else most > 0
    pl.when(some & jnp.logical_not(ragged))(functools.partial(whole, False))
    pl.when(some & ragged)(functools.partial(whole, True))


def state_shapes(slots):
    return [pltpu.VMEM((STATE, BOTH), F32)] * slots


def prepare_kernel(swap, own_q, own_kv, kv, q_all):
    for slot in range(2):
        kv[slot, 0] = own_kv[slot]
        kv[slot, 1, :ROWS, :] = swap[slot, :, WIDE : WIDE + HD]
        kv[slot, 1, ROWS:, :] = swap[slot, :, WIDE + HD :]
        for h in range(PER):
            rows = pl.ds(h * ROWS, ROWS)
            others = pl.ds(WIDE + h * ROWS, ROWS)
            mine = own_q[slot, :, h * HD : (h + 1) * HD].T
            theirs = swap[slot, :, h * HD : (h + 1) * HD].T
            for copy in range(2):
                q_all[slot, copy * HD : (copy + 1) * HD, rows] = mine
                q_all[slot, copy * HD : (copy + 1) * HD, others] = theirs


def prepare_call(swap, own_q, own_kv):
    return pl.pallas_call(
        prepare_kernel,
        out_shape=[pltpu.VMEM((2, 2, 2 * ROWS, HD), BF16), pltpu.VMEM((2, 2 * HD, BOTH), BF16)],
        in_specs=[IN_VMEM] * 3,
        out_specs=[IN_VMEM] * 2,
        compiler_params=pltpu.CompilerParams(vmem_limit_bytes=VMEM_LIMIT),
        cost_estimate=COST,
    )(swap, own_q, own_kv)


def own_kernel(meta, q_all, kv, own, *states):
    m = meta[META_M]
    key = lax.broadcasted_iota(jnp.int32, (BLK, TILE), 0)
    row = lax.broadcasted_iota(jnp.int32, (BLK, TILE), 1) % ROWS
    causal = key <= row
    odd = (m % 2) == 1

    def blocks_of(t):
        if t * TILE < WIDE:
            return [(UNIT, None, causal), (UNIT, jnp.logical_not(odd), None)]
        return [(UNIT, odd, None), (UNIT, None, causal)]

    for slot in range(2):
        keys = jnp.concatenate([kv[slot, side, :ROWS] for side in range(2)], axis=0)
        values = jnp.concatenate([kv[slot, side, ROWS:].T for side in range(2)], axis=1)
        add_pieces(
            q_all.at[slot],
            None,
            states[slot],
            [own.at[slot]],
            (0,),
            meta,
            (keys, values, blocks_of),
        )


def own_call(meta, q_all, kv, own):
    return pl.pallas_call(
        own_kernel,
        out_shape=state_shapes(2),
        in_specs=[IN_SMEM] + [IN_VMEM] * 3,
        out_specs=[IN_VMEM] * 2,
        compiler_params=pltpu.CompilerParams(vmem_limit_bytes=VMEM_LIMIT),
        cost_estimate=COST,
    )(meta, q_all, kv, own)


def add_kernel(slots, ks, early, last, meta, q_all, *refs):
    refs = list(refs)
    take = lambda n: [refs.pop(0) for _ in range(n)]
    before = take(len(slots))
    sources = take(len(ks))
    kv_early = take(1)[0] if early else None
    outs = take(2) if last else None
    after = take(len(slots))
    for w, slot in enumerate(slots):
        pieces = [s.at[slot] if len(s.shape) == 3 else s for s in sources]
        extra = None
        if early:
            unused = meta[META_M] < 2
            extra = (
                jnp.concatenate([kv_early[1 - slot, side, :ROWS] for side in range(2)], axis=0),
                jnp.concatenate([kv_early[1 - slot, side, ROWS:].T for side in range(2)], axis=1),
                lambda t: [(UNIT, unused, None)] * 2,
            )
        add_pieces(q_all.at[slot], before[w], after[w], pieces, ks, meta, extra)
    if last:
        state = after[0]
        for side, out in enumerate(outs):
            member = meta[META_M] ^ side
            row = lax.broadcasted_iota(jnp.int32, (HD, ROWS), 1) + member * ROWS
            for i in range(PER):
                cols = pl.ds(side * WIDE + i * ROWS, ROWS)
                piece = state[:HD, cols] * (1.0 / jnp.sum(state[SUM_ROW : SUM_ROW + 8, cols], axis=0, keepdims=True))
                piece = jnp.where(row < meta[META_SUF], piece, 0.0).astype(BF16)
                out[:, i * HD : (i + 1) * HD] = piece.T


def add_call(meta, q_all, states, sources, slots, ks, early=None, last=False):
    flat = [states[s] for s in slots]
    args = [meta, q_all, *flat, *sources] + ([] if early is None else [early])
    scratch = []
    if last:
        out_shape = [pltpu.VMEM((ROWS, WIDE), BF16)] * 2
        scratch = state_shapes(1)
    else:
        out_shape = state_shapes(len(slots))
    out = pl.pallas_call(
        functools.partial(add_kernel, slots, ks, early is not None, last),
        out_shape=out_shape,
        in_specs=[IN_SMEM] + [IN_VMEM] * (len(args) - 1),
        out_specs=[IN_VMEM] * len(out_shape),
        scratch_shapes=scratch,
        compiler_params=pltpu.CompilerParams(vmem_limit_bytes=VMEM_LIMIT),
        cost_estimate=COST,
    )(*args)
    if last:
        return out
    states = list(states)
    for w, slot in enumerate(slots):
        states[slot] = out[w]
    return states


def join_kernel(meta, *refs):
    out, sems = refs[4:]
    made = []
    for i, src in enumerate(refs[:4]):
        head = meta[META_M] ^ (2 * (i % 2) + i // 2)
        column = pl.multiple_of(head * WIDE, WIDE)
        made.append(pltpu.make_async_copy(src, out.at[:, pl.ds(column, WIDE)], sems.at[i]))
        made[-1].start()
    for x in made:
        x.wait()


def join_call(meta, mine, yours):
    return pl.pallas_call(
        join_kernel,
        out_shape=jax.ShapeDtypeStruct((ROWS, QH * HD), BF16),
        in_specs=[IN_SMEM] + [IN_VMEM] * 4,
        out_specs=IN_HBM,
        scratch_shapes=[pltpu.SemaphoreType.DMA((4,))],
        cost_estimate=COST,
    )(meta, *mine, *yours)


def permute(x, axis, count, k):
    return lax.ppermute(x, axis, [(i, i ^ k) for i in range(count)])


def per_device_small(
    queries, suffix_kv, cache, cache_scale, prefix_len, suffix_len, block_table, session_group
):
    ids = jnp.stack([lax.axis_index("pool"), lax.axis_index("blk")]).astype(jnp.int32)
    tables = [block_table, session_group, prefix_len, suffix_len]
    queries, suffix_kv, cache, scale, *tables = [
        pltpu.with_memory_space_constraint(x, pltpu.HBM)
        for x in (queries, suffix_kv, cache, cache_scale.T, *tables)
    ]
    meta, swap, *parts = gather_call(ids, queries, suffix_kv, cache, tables, scale)
    far, near = parts[:4], parts[4:7]
    own, own_q, own_kv = parts[7:]
    far_in, near_in, across = {}, {}, {}
    swap_in = permute(swap, "blk", 4, 1)
    for k in (4, 5):
        far_in[k] = permute(far[k - 4], "pool", POOL, k)
    for k in (1, 2):
        near_in[k] = permute(near[k - 1], "pool", POOL, k)
    kv, q_all = prepare_call(swap_in, own_q, own_kv)
    early = permute(kv, "blk", 4, 2)
    states = own_call(meta, q_all, kv, own)
    near[2], states = lax.optimization_barrier((near[2], states))
    near_in[3] = permute(near[2], "pool", POOL, 3)
    states = add_call(meta, q_all, states, [near_in[1], near_in[2]], (0, 1), (1, 2), early=early)
    far[2], far[3], far_in[4], far_in[5], states = lax.optimization_barrier(
        (far[2], far[3], far_in[4], far_in[5], states)
    )
    for k in (6, 7):
        far_in[k] = permute(far[k - 4], "pool", POOL, k)
    for k in (4, 5):
        across[k] = permute(far_in[k], "blk", 4, 2)
    states = add_call(meta, q_all, states, [far_in[4], far_in[5]], (0,), (4, 5))
    near_in[3], states = lax.optimization_barrier((near_in[3], states))
    states = add_call(meta, q_all, states, [near_in[3]], (0, 1), (3,))
    far_in[6], far_in[7], states = lax.optimization_barrier((far_in[6], far_in[7], states))
    for k in (6, 7):
        across[k] = permute(far_in[k], "blk", 4, 2)
    states = add_call(meta, q_all, states, [across[4], across[5]], (1,), (4, 5))
    mine, yours = [], []
    for slot, source in ((0, far_in), (1, across)):
        a, b = add_call(meta, q_all, states, [source[6], source[7]], (slot,), (6, 7), last=True)
        mine.append(pltpu.with_memory_space_constraint(a, pltpu.VMEM))
        yours.append(
            pltpu.with_memory_space_constraint(permute(b, "blk", 4, 1), pltpu.VMEM)
        )
    return join_call(meta, mine, yours)


def fold_keys(running, query_heads, key_rows, value_rows, key_scale, value_scale, usable):
    highest, weight_sum, weighted = running
    scores = jnp.einsum("kgrd,nkd->kgrn", query_heads, key_rows, preferred_element_type=jnp.float32)
    scores = scores * jnp.transpose(key_scale)[:, None, None, :]
    scores = jnp.where(usable[None, None], scores, masked_score)
    new_highest = jnp.maximum(highest, jnp.max(scores, axis=3))
    weights = jnp.where(usable[None, None], jnp.exp(scores - new_highest[..., None]), 0.0)
    factor = jnp.exp(highest - new_highest)
    weight_sum = weight_sum * factor + jnp.sum(weights, axis=3)
    rounded = (weights * jnp.transpose(value_scale)[:, None, None, :]).astype(jnp.bfloat16)
    weighted = weighted * factor[..., None] + jnp.einsum(
        "kgrn,nkd->kgrd", rounded, value_rows, preferred_element_type=jnp.float32
    )
    return (new_highest, weight_sum, weighted)


def per_device_any(
    queries, suffix_kv, cache, cache_scale, prefix_len, suffix_len, block_table, session_group
):
    local_rows = queries.shape[0]
    kv_heads = KVH
    per_group = QH // KVH
    head_size = HD
    pool_count = lax.axis_size("pool")
    member_count = lax.axis_size("blk")
    pool_index = lax.axis_index("pool")
    member_index = lax.axis_index("blk")
    slot_count = cache.shape[0]
    block_size = cache.shape[1]
    session_count = block_table.shape[0]
    block_count = block_table.shape[1]
    run_count = block_count // pool_count
    inv_root = 1.0 / math.sqrt(head_size)
    chooser = (
        session_group[:, None] == jnp.arange(session_count, dtype=jnp.int32)[None, :]
    ).astype(jnp.int32)
    tables = jnp.sum(chooser[:, :, None] * block_table[None], axis=1)
    holders = (tables // slot_count).reshape(pool_count, run_count, pool_count)
    places = (tables % slot_count).reshape(pool_count, run_count, pool_count)
    send_slots = jnp.sum(jnp.where(holders == pool_index, places, 0), axis=2)
    own_choice = lax.dynamic_index_in_dim(chooser, pool_index, 0, keepdims=False)
    prefix_length = jnp.sum(own_choice * prefix_len)
    suffix_length = jnp.sum(own_choice * suffix_len)
    own_holders = lax.dynamic_index_in_dim(holders, pool_index, 0, keepdims=False)
    positions = jnp.arange(block_count, dtype=jnp.int32).reshape(run_count, pool_count)
    matches = own_holders[None, :, :] == jnp.arange(pool_count, dtype=jnp.int32)[:, None, None]
    block_place = jnp.sum(jnp.where(matches, positions[None], 0), axis=2)
    scale_rows = cache_scale[send_slots]
    split_cache = cache.reshape(slot_count, block_size, 2 * kv_heads, head_size)
    share_size = 2 * kv_heads // member_count
    outgoing = lax.dynamic_slice_in_dim(
        split_cache[send_slots], member_index * share_size, share_size, 3
    )
    arrived_part, arrived_scale = (
        lax.all_to_all(outgoing, "pool", split_axis=0, concat_axis=0, tiled=True),
        lax.all_to_all(scale_rows, "pool", split_axis=0, concat_axis=0, tiled=True),
    )
    arrived = lax.all_gather(arrived_part, "blk", axis=3, tiled=True)
    prefix_tokens = pool_count * run_count * block_size
    step_tokens = min(1024, prefix_tokens)
    step_count = prefix_tokens // step_tokens
    prefix_stack = arrived.reshape(step_count, step_tokens, 2, kv_heads, head_size)
    token_scale = jnp.broadcast_to(
        arrived_scale.astype(jnp.float32).reshape(pool_count, run_count, 1, 2, kv_heads),
        (pool_count, run_count, block_size, 2, kv_heads),
    ).reshape(step_count, step_tokens, 2, kv_heads)
    token_place = (
        block_place[:, :, None] * block_size
        + jnp.arange(block_size, dtype=jnp.int32)[None, None, :]
    ).reshape(step_count, step_tokens)
    query_heads = jnp.transpose(
        queries.reshape(local_rows, kv_heads, per_group, head_size), (1, 2, 0, 3)
    )
    row_place = member_index * local_rows + jnp.arange(local_rows, dtype=jnp.int32)
    initial = (
        jnp.full((kv_heads, per_group, local_rows), masked_score, jnp.float32),
        jnp.zeros((kv_heads, per_group, local_rows), jnp.float32),
        jnp.zeros((kv_heads, per_group, local_rows, head_size), jnp.float32),
    )
    shard_rows = lax.all_gather(suffix_kv, "blk", axis=0, tiled=True)
    piece_count = shard_rows.shape[0]
    split_rows = shard_rows.reshape(piece_count, 2, kv_heads, head_size)
    key_place = jnp.arange(piece_count, dtype=jnp.int32)
    usable = (key_place[None, :] <= row_place[:, None]) & (key_place[None, :] < suffix_length)
    flat_scale = jnp.full((piece_count, kv_heads), inv_root, jnp.float32)
    unit_scale = jnp.ones((piece_count, kv_heads), jnp.float32)
    running = fold_keys(
        initial, query_heads, split_rows[:, 0], split_rows[:, 1], flat_scale, unit_scale, usable
    )

    def prefix_step(running, step_inputs):
        token_rows, scale_step, place_rows = step_inputs
        usable = (place_rows < prefix_length)[None, :]
        updated = fold_keys(
            running,
            query_heads,
            token_rows[:, 0],
            token_rows[:, 1],
            scale_step[:, 0] * inv_root,
            scale_step[:, 1],
            usable,
        )
        return (updated, None)

    running, unused = lax.scan(prefix_step, running, (prefix_stack, token_scale, token_place))
    highest, weight_sum, weighted = running
    result = weighted / weight_sum[..., None]
    result = jnp.transpose(result, (2, 0, 1, 3)).reshape(local_rows, QH * head_size)
    result = jnp.where((row_place < suffix_length)[:, None], result, 0.0)
    return result.astype(jnp.bfloat16)


def solution(mesh):
    small = dict(mesh.shape) == {"pool": POOL, "blk": 4}
    return jax.shard_map(
        per_device_small if small else per_device_any,
        mesh=mesh,
        in_specs=(
            P(("pool", "blk"), None),
            P(("pool", "blk"), None),
            P("pool", None, None),
            P("pool", None),
            P(),
            P(),
            P(),
            P(),
        ),
        out_specs=P(("pool", "blk"), None),
        check_vma=False,
    )
```

```python
import functools
import math

import jax
import jax.numpy as jnp
from jax import lax
from jax.experimental import pallas as pl
from jax.experimental.pallas import tpu as pltpu
from jax.sharding import PartitionSpec as P

QH = 32
KVH = 4
HD = 128
PER = QH // KVH
LOG2E = math.log2(math.e)
INV_ROOT = 1.0 / math.sqrt(HD)

masked_score = -1e30

RUNS = 2
BLK = 128
PAIR = RUNS * BLK
PIECE = 2 * PAIR + 16
ROWS = 128
WIDE = PER * ROWS
BOTH = 2 * WIDE
REF_ROW = HD
SUM_ROW = HD + 8
STATE = HD + 16
POOL = 8
META_J = 0
META_LEN = 2 * POOL
META_SUF = META_LEN + 1
META_M = META_LEN + 2
META_SIZE = 24
TILE = 1024
VMEM_LIMIT = 24 << 20
BF16 = jnp.bfloat16
F32 = jnp.float32
IN_VMEM = pl.BlockSpec(memory_space=pltpu.VMEM)
IN_SMEM = pl.BlockSpec(memory_space=pltpu.SMEM)
IN_HBM = pl.BlockSpec(memory_space=pltpu.HBM)


COST = pl.CostEstimate(flops=1 << 10, bytes_accessed=1 << 10, transcendentals=0)


def spread_scales(cache_scale, m, spread):
    scales = cache_scale[...].astype(F32).T
    column = lax.broadcasted_iota(jnp.int32, scales.shape, 1)
    for slot in range(2):
        for half in range(2):
            chosen = jnp.where(column == half * KVH + (m ^ (2 * slot)), scales, 0.0)
            one = jnp.sum(chosen, axis=1, keepdims=True)
            spread[2 * slot + half] = jnp.broadcast_to(one, (scales.shape[0], HD))


def write_scales(spread, locals_, slot, dst):
    row = lax.broadcasted_iota(jnp.int32, (16, HD), 0)
    rows = jnp.ones((16, HD), F32)
    for half in range(2):
        for run in range(RUNS):
            one = spread[2 * slot + half, pl.ds(locals_[run], 1), :]
            rows = jnp.where(row == half * RUNS + run, one, rows)
    dst[pl.ds(2 * PAIR, 16), :] = rows.astype(BF16)


PIECE_1 = pltpu.VMEM((PIECE, HD), BF16)
PIECE_2 = pltpu.VMEM((2, PIECE, HD), BF16)
SWAP = WIDE + 2 * HD


def gather_kernel(ids, queries, suffix_kv, cache, *refs):
    loads = list(zip(refs[:5], refs[17:22]))
    meta, swap = refs[5:7]
    far, near, own = refs[7:11], refs[11:14], refs[14]
    own_q, own_kv = refs[15:17]
    table, groups, lengths, suffixes, cache_scale = refs[17:22]
    spread, stage, table_sems, more_sems, stage_sems = refs[22:]
    p = ids[0]
    m = ids[1]
    loads = [
        pltpu.make_async_copy(a, b, table_sems.at[i]) for i, (a, b) in enumerate(loads)
    ]
    for c in loads:
        c.start()
    staged = []
    for i in range(4):
        column = pl.multiple_of((i % 2 * KVH + (m ^ (2 * (i // 2)))) * HD, HD)
        c = pltpu.make_async_copy(
            cache.at[:, :, pl.ds(column, HD)], stage.at[i], stage_sems.at[i]
        )
        c.start()
        staged.append(c)
    made = []
    for slot in range(2):
        mine = m ^ (2 * slot)
        theirs = mine ^ 1
        jobs = [
            (queries, theirs * WIDE, WIDE, swap.at[slot, :, pl.ds(0, WIDE)]),
            (suffix_kv, theirs * HD, HD, swap.at[slot, :, pl.ds(WIDE, HD)]),
            (suffix_kv, (KVH + theirs) * HD, HD, swap.at[slot, :, pl.ds(WIDE + HD, HD)]),
            (queries, mine * WIDE, WIDE, own_q.at[slot]),
            (suffix_kv, mine * HD, HD, own_kv.at[slot, pl.ds(0, ROWS), :]),
            (suffix_kv, (KVH + mine) * HD, HD, own_kv.at[slot, pl.ds(ROWS, ROWS), :]),
        ]
        for src, at, width, dst in jobs:
            src = src.at[:, pl.ds(pl.multiple_of(at, HD), width)]
            c = pltpu.make_async_copy(src, dst, more_sems.at[len(made)])
            c.start()
            made.append(c)
    for c in loads:
        c.wait()
    meta[META_M] = m
    slot_count = cache.shape[0]
    low = p * slot_count
    jobs = [(4 + i, (0,), (ref,)) for i, ref in enumerate(far)]
    jobs += [(1 + i, (0, 1), (ref.at[0], ref.at[1])) for i, ref in enumerate(near)]
    jobs += [(0, (0, 1), (own.at[0], own.at[1]))]
    pending = []
    for k, slots, outs in jobs:
        session = groups[p ^ k]
        locals_ = []
        for run in range(RUNS):
            local = jnp.int32(0)
            for jj in range(POOL):
                at = table[session, run * POOL + jj] - low
                local = jnp.where((at >= 0) & (at < slot_count), at, local)
            locals_.append(local)
        for slot, out in zip(slots, outs):
            pending.append((locals_, slot, out))
    mine = groups[p]
    for run in range(RUNS):
        for jj in range(POOL):
            at = run * POOL + jj
            meta[META_J + RUNS * ((table[mine, at] // slot_count) ^ p) + run] = at
    meta[META_LEN] = lengths[mine]
    meta[META_SUF] = suffixes[mine]
    spread_scales(cache_scale, m, spread)
    for locals_, slot, out in pending:
        write_scales(spread, locals_, slot, out)
    for c in staged:
        c.wait()
    for locals_, slot, out in pending:
        for half in range(2):
            for run in range(RUNS):
                rows = pl.ds(half * PAIR + run * BLK, BLK)
                out[rows, :] = stage[2 * slot + half, locals_[run]]
    for c in made:
        c.wait()


def gather_call(ids, queries, suffix_kv, cache, tables, cache_scale):
    return pl.pallas_call(
        gather_kernel,
        out_shape=[
            jax.ShapeDtypeStruct((META_SIZE,), jnp.int32),
            pltpu.VMEM((2, ROWS, SWAP), BF16),
        ]
        + [PIECE_1] * 4
        + [PIECE_2] * 4
        + [pltpu.VMEM((2, ROWS, WIDE), BF16), pltpu.VMEM((2, 2 * ROWS, HD), BF16)],
        in_specs=[IN_SMEM] + [IN_HBM] * 8,
        out_specs=[IN_SMEM] + [IN_VMEM] * 11,
        scratch_shapes=[pltpu.SMEM(x.shape, jnp.int32) for x in tables]
        + [
            pltpu.VMEM(cache_scale.shape, cache_scale.dtype),
            pltpu.VMEM((4, cache.shape[0], HD), F32),
            pltpu.VMEM((4, cache.shape[0], BLK, HD), BF16),
            pltpu.SemaphoreType.DMA((5,)),
            pltpu.SemaphoreType.DMA((12,)),
            pltpu.SemaphoreType.DMA((4,)),
        ],
        compiler_params=pltpu.CompilerParams(vmem_limit_bytes=VMEM_LIMIT),
        cost_estimate=COST,
    )(ids, queries, suffix_kv, cache, *tables, cache_scale)


def wide(row):
    return jnp.broadcast_to(jnp.concatenate([row] * (TILE // HD), axis=1), (8, TILE))


def terms(tile, run):
    value = tile[RUNS + run : RUNS + run + 1]
    return wide(jnp.log2(value)), wide(1.0 / value)


def scaled_keys(keys, scale):
    whole = keys.astype(F32) * (scale * (LOG2E * INV_ROOT))
    high = whole.astype(BF16)
    return jnp.concatenate([high, (whole - high.astype(F32)).astype(BF16)], axis=1)


UNIT = None


def fold(q, keys, values_t, before, after, blocks_of):
    tiles = BOTH // TILE

    def score(t):
        return jnp.dot(keys, q[:, pl.ds(t * TILE, TILE)], preferred_element_type=F32)

    following = score(0)
    for t in range(tiles):
        scores = following
        if t + 1 < tiles:
            following = score(t + 1)
        cols = pl.ds(t * TILE, TILE)
        blocks = blocks_of(t)
        if before is None:
            old = jnp.full((8, TILE), masked_score, F32)
        else:
            old = before[REF_ROW : REF_ROW + 8, cols]
        parts = []
        highest = old
        for b, (term, dead, mask) in enumerate(blocks):
            part = scores[b * BLK : (b + 1) * BLK]
            part = part if mask is None else jnp.where(mask, part, masked_score)
            part = part.reshape(BLK // 8, 8, TILE)
            parts.append(part)
            top = jnp.max(part, axis=0)
            if dead is not None:
                top = jnp.where(dead, masked_score, top)
            highest = jnp.maximum(highest, top)
        reference = jnp.broadcast_to(jnp.max(highest, axis=0, keepdims=True), (8, TILE))
        if before is None:
            total = jnp.zeros((8, TILE), F32)
        else:
            factor = jnp.exp2(old - reference)
            total = before[SUM_ROW : SUM_ROW + 8, cols] * factor
        rounded = []
        for part, (term, dead, mask) in zip(parts, blocks):
            shift = reference if term is UNIT else reference - term[0]
            if dead is not None:
                shift = jnp.where(dead, -masked_score, shift)
            weights = jnp.exp2(part - shift)
            summed = jnp.sum(weights, axis=0)
            total = total + (summed if term is UNIT else summed * term[1])
            rounded.append(weights.reshape(BLK, TILE).astype(BF16))
        rounded = jnp.concatenate(rounded, axis=0) if len(rounded) > 1 else rounded[0]
        product = jnp.dot(values_t, rounded, preferred_element_type=F32)
        if before is not None:
            held = before[:HD, cols].reshape(HD // 8, 8, TILE) * factor
            product = held.reshape(HD, TILE) + product
        after[:HD, cols] = product
        after[REF_ROW : REF_ROW + 8, cols] = reference
        after[SUM_ROW : SUM_ROW + 8, cols] = total


def add_pieces(q, before, after, pieces, ks, meta, extra=None, needed=None):
    m = meta[META_M]
    n = len(ks)
    reach = jnp.where(((m // 2) * 2) * ROWS < meta[META_SUF], meta[META_LEN], 0)
    counts = [
        jnp.clip(reach - meta[META_J + RUNS * k + r] * BLK, 0, BLK) for k in ks for r in range(RUNS)
    ]
    most = functools.reduce(jnp.maximum, counts)
    ragged = functools.reduce(jnp.logical_or, [(c > 0) & (c < BLK) for c in counts])

    def whole(masked, extra):
        blocks = []
        place = lax.broadcasted_iota(jnp.int32, (BLK, TILE), 0) if masked else None
        for i in range(n):
            tile = pieces[i][2 * PAIR :, :].astype(F32)
            for r in range(RUNS):
                c = counts[RUNS * i + r]
                blocks.append((terms(tile, r),) + ((None, place < c) if masked else (c < BLK, None)))
        keys = []
        for i in range(n):
            tile = pieces[i][2 * PAIR :, :].astype(F32)
            for r in range(RUNS):
                block = pieces[i][r * BLK : (r + 1) * BLK, :]
                keys.append(scaled_keys(block, tile[r : r + 1]))
        values = [pieces[i][PAIR : 2 * PAIR, :].T for i in range(n)]
        blocks_of = lambda t: blocks
        if extra is not None:
            keys = [scaled_keys(extra[0], 1.0)] + keys
            values = [extra[1]] + values
            blocks_of = lambda t: extra[2](t) + blocks
        keys = jnp.concatenate(keys, axis=0)
        values = jnp.concatenate(values, axis=1) if len(values) > 1 else values[0]
        fold(q, keys, values, before, after, blocks_of)

    if extra is None:

        @pl.when(most == 0)
        def _():
            after[...] = before[...]

    some = jnp.bool_(True) if extra is not None else most > 0
    plain = jnp.logical_not(ragged)
    if needed is None:
        pl.when(some & plain)(functools.partial(whole, False, extra))
        pl.when(some & ragged)(functools.partial(whole, True, extra))
    else:
        idle = jnp.logical_not(needed)

        @pl.when(idle & (most == 0))
        def _():
            after[...] = before[...]

        pl.when(needed & plain)(functools.partial(whole, False, extra))
        pl.when(needed & ragged)(functools.partial(whole, True, extra))
        pl.when(idle & plain & (most > 0))(functools.partial(whole, False, None))
        pl.when(idle & ragged)(functools.partial(whole, True, None))


def state_shapes(slots):
    return [pltpu.VMEM((STATE, BOTH), F32)] * slots


def prepare_kernel(swap, own_q, own_kv, kv, q_all):
    for slot in range(2):
        kv[slot, 0] = own_kv[slot]
        kv[slot, 1, :ROWS, :] = swap[slot, :, WIDE : WIDE + HD]
        kv[slot, 1, ROWS:, :] = swap[slot, :, WIDE + HD :]
        for h in range(PER):
            rows = pl.ds(h * ROWS, ROWS)
            others = pl.ds(WIDE + h * ROWS, ROWS)
            mine = own_q[slot, :, h * HD : (h + 1) * HD].T
            theirs = swap[slot, :, h * HD : (h + 1) * HD].T
            for copy in range(2):
                q_all[slot, copy * HD : (copy + 1) * HD, rows] = mine
                q_all[slot, copy * HD : (copy + 1) * HD, others] = theirs


def prepare_call(swap, own_q, own_kv):
    return pl.pallas_call(
        prepare_kernel,
        out_shape=[pltpu.VMEM((2, 2, 2 * ROWS, HD), BF16), pltpu.VMEM((2, 2 * HD, BOTH), BF16)],
        in_specs=[IN_VMEM] * 3,
        out_specs=[IN_VMEM] * 2,
        compiler_params=pltpu.CompilerParams(vmem_limit_bytes=VMEM_LIMIT),
        cost_estimate=COST,
    )(swap, own_q, own_kv)


def own_kernel(meta, q_all, kv, own, *states):
    m = meta[META_M]
    key = lax.broadcasted_iota(jnp.int32, (BLK, TILE), 0)
    row = lax.broadcasted_iota(jnp.int32, (BLK, TILE), 1) % ROWS
    causal = key <= row
    odd = (m % 2) == 1

    def blocks_of(t):
        if t * TILE < WIDE:
            return [(UNIT, None, causal), (UNIT, jnp.logical_not(odd), None)]
        return [(UNIT, odd, None), (UNIT, None, causal)]

    for slot in range(2):
        keys = jnp.concatenate([kv[slot, side, :ROWS] for side in range(2)], axis=0)
        values = jnp.concatenate([kv[slot, side, ROWS:].T for side in range(2)], axis=1)
        add_pieces(
            q_all.at[slot],
            None,
            states[slot],
            [own.at[slot]],
            (0,),
            meta,
            (keys, values, blocks_of),
        )


def own_call(meta, q_all, kv, own):
    return pl.pallas_call(
        own_kernel,
        out_shape=state_shapes(2),
        in_specs=[IN_SMEM] + [IN_VMEM] * 3,
        out_specs=[IN_VMEM] * 2,
        compiler_params=pltpu.CompilerParams(vmem_limit_bytes=VMEM_LIMIT),
        cost_estimate=COST,
    )(meta, q_all, kv, own)


def add_kernel(slots, ks, early, last, meta, q_all, *refs):
    refs = list(refs)
    take = lambda n: [refs.pop(0) for _ in range(n)]
    before = take(len(slots))
    sources = take(len(ks))
    kv_early = take(1)[0] if early else None
    outs = take(2) if last else None
    after = take(len(slots))
    for w, slot in enumerate(slots):
        pieces = [s.at[slot] if len(s.shape) == 3 else s for s in sources]
        extra = None
        if early:
            extra = (
                jnp.concatenate([kv_early[1 - slot, side, :ROWS] for side in range(2)], axis=0),
                jnp.concatenate([kv_early[1 - slot, side, ROWS:].T for side in range(2)], axis=1),
                lambda t: [(UNIT, None, None)] * 2,
            )
        add_pieces(q_all.at[slot], before[w], after[w], pieces, ks, meta, extra, meta[META_M] >= 2 if early else None)
    if last:
        state = after[0]
        for side, out in enumerate(outs):
            member = meta[META_M] ^ side
            row = lax.broadcasted_iota(jnp.int32, (HD, ROWS), 1) + member * ROWS
            for i in range(PER):
                cols = pl.ds(side * WIDE + i * ROWS, ROWS)
                piece = state[:HD, cols] * (1.0 / jnp.sum(state[SUM_ROW : SUM_ROW + 8, cols], axis=0, keepdims=True))
                piece = jnp.where(row < meta[META_SUF], piece, 0.0).astype(BF16)
                out[:, i * HD : (i + 1) * HD] = piece.T


def add_call(meta, q_all, states, sources, slots, ks, early=None, last=False):
    flat = [states[s] for s in slots]
    args = [meta, q_all, *flat, *sources] + ([] if early is None else [early])
    scratch = []
    if last:
        out_shape = [pltpu.VMEM((ROWS, WIDE), BF16)] * 2
        scratch = state_shapes(1)
    else:
        out_shape = state_shapes(len(slots))
    out = pl.pallas_call(
        functools.partial(add_kernel, slots, ks, early is not None, last),
        out_shape=out_shape,
        in_specs=[IN_SMEM] + [IN_VMEM] * (len(args) - 1),
        out_specs=[IN_VMEM] * len(out_shape),
        scratch_shapes=scratch,
        compiler_params=pltpu.CompilerParams(vmem_limit_bytes=VMEM_LIMIT),
        cost_estimate=COST,
    )(*args)
    if last:
        return out
    states = list(states)
    for w, slot in enumerate(slots):
        states[slot] = out[w]
    return states


def join_kernel(meta, *refs):
    out, sems = refs[4:]
    made = []
    for i, src in enumerate(refs[:4]):
        head = meta[META_M] ^ (2 * (i % 2) + i // 2)
        column = pl.multiple_of(head * WIDE, WIDE)
        made.append(pltpu.make_async_copy(src, out.at[:, pl.ds(column, WIDE)], sems.at[i]))
        made[-1].start()
    for x in made:
        x.wait()


def join_call(meta, mine, yours):
    return pl.pallas_call(
        join_kernel,
        out_shape=jax.ShapeDtypeStruct((ROWS, QH * HD), BF16),
        in_specs=[IN_SMEM] + [IN_VMEM] * 4,
        out_specs=IN_HBM,
        scratch_shapes=[pltpu.SemaphoreType.DMA((4,))],
        cost_estimate=COST,
    )(meta, *mine, *yours)


def permute(x, axis, count, k):
    return lax.ppermute(x, axis, [(i, i ^ k) for i in range(count)])


def per_device_small(
    queries, suffix_kv, cache, cache_scale, prefix_len, suffix_len, block_table, session_group
):
    ids = jnp.stack([lax.axis_index("pool"), lax.axis_index("blk")]).astype(jnp.int32)
    tables = [block_table, session_group, prefix_len, suffix_len]
    queries, suffix_kv, cache, scale, *tables = [
        pltpu.with_memory_space_constraint(x, pltpu.HBM)
        for x in (queries, suffix_kv, cache, cache_scale.T, *tables)
    ]
    meta, swap, *parts = gather_call(ids, queries, suffix_kv, cache, tables, scale)
    far, near = parts[:4], parts[4:7]
    own, own_q, own_kv = parts[7:]
    far_in, near_in, across = {}, {}, {}
    swap_in = permute(swap, "blk", 4, 1)
    for k in (4, 5):
        far_in[k] = permute(far[k - 4], "pool", POOL, k)
    for k in (1, 2):
        near_in[k] = permute(near[k - 1], "pool", POOL, k)
    kv, q_all = prepare_call(swap_in, own_q, own_kv)
    early = permute(kv, "blk", 4, 2)
    states = own_call(meta, q_all, kv, own)
    near[2], states = lax.optimization_barrier((near[2], states))
    near_in[3] = permute(near[2], "pool", POOL, 3)
    states = add_call(meta, q_all, states, [near_in[1], near_in[2]], (0, 1), (1, 2), early=early)
    far[2], far[3], far_in[4], far_in[5], states = lax.optimization_barrier(
        (far[2], far[3], far_in[4], far_in[5], states)
    )
    for k in (6, 7):
        far_in[k] = permute(far[k - 4], "pool", POOL, k)
    for k in (4, 5):
        across[k] = permute(far_in[k], "blk", 4, 2)
    states = add_call(meta, q_all, states, [far_in[4], far_in[5]], (0,), (4, 5))
    near_in[3], states = lax.optimization_barrier((near_in[3], states))
    states = add_call(meta, q_all, states, [near_in[3]], (0, 1), (3,))
    far_in[6], far_in[7], states = lax.optimization_barrier((far_in[6], far_in[7], states))
    for k in (6, 7):
        across[k] = permute(far_in[k], "blk", 4, 2)
    states = add_call(meta, q_all, states, [across[4], across[5]], (1,), (4, 5))
    mine, yours = [], []
    for slot, source in ((0, far_in), (1, across)):
        a, b = add_call(meta, q_all, states, [source[6], source[7]], (slot,), (6, 7), last=True)
        mine.append(pltpu.with_memory_space_constraint(a, pltpu.VMEM))
        yours.append(
            pltpu.with_memory_space_constraint(permute(b, "blk", 4, 1), pltpu.VMEM)
        )
    return join_call(meta, mine, yours)


def fold_keys(running, query_heads, key_rows, value_rows, key_scale, value_scale, usable):
    highest, weight_sum, weighted = running
    scores = jnp.einsum("kgrd,nkd->kgrn", query_heads, key_rows, preferred_element_type=jnp.float32)
    scores = scores * jnp.transpose(key_scale)[:, None, None, :]
    scores = jnp.where(usable[None, None], scores, masked_score)
    new_highest = jnp.maximum(highest, jnp.max(scores, axis=3))
    weights = jnp.where(usable[None, None], jnp.exp(scores - new_highest[..., None]), 0.0)
    factor = jnp.exp(highest - new_highest)
    weight_sum = weight_sum * factor + jnp.sum(weights, axis=3)
    rounded = (weights * jnp.transpose(value_scale)[:, None, None, :]).astype(jnp.bfloat16)
    weighted = weighted * factor[..., None] + jnp.einsum(
        "kgrn,nkd->kgrd", rounded, value_rows, preferred_element_type=jnp.float32
    )
    return (new_highest, weight_sum, weighted)


def per_device_any(
    queries, suffix_kv, cache, cache_scale, prefix_len, suffix_len, block_table, session_group
):
    local_rows = queries.shape[0]
    kv_heads = KVH
    per_group = QH // KVH
    head_size = HD
    pool_count = lax.axis_size("pool")
    member_count = lax.axis_size("blk")
    pool_index = lax.axis_index("pool")
    member_index = lax.axis_index("blk")
    slot_count = cache.shape[0]
    block_size = cache.shape[1]
    session_count = block_table.shape[0]
    block_count = block_table.shape[1]
    run_count = block_count // pool_count
    inv_root = 1.0 / math.sqrt(head_size)
    chooser = (
        session_group[:, None] == jnp.arange(session_count, dtype=jnp.int32)[None, :]
    ).astype(jnp.int32)
    tables = jnp.sum(chooser[:, :, None] * block_table[None], axis=1)
    holders = (tables // slot_count).reshape(pool_count, run_count, pool_count)
    places = (tables % slot_count).reshape(pool_count, run_count, pool_count)
    send_slots = jnp.sum(jnp.where(holders == pool_index, places, 0), axis=2)
    own_choice = lax.dynamic_index_in_dim(chooser, pool_index, 0, keepdims=False)
    prefix_length = jnp.sum(own_choice * prefix_len)
    suffix_length = jnp.sum(own_choice * suffix_len)
    own_holders = lax.dynamic_index_in_dim(holders, pool_index, 0, keepdims=False)
    positions = jnp.arange(block_count, dtype=jnp.int32).reshape(run_count, pool_count)
    matches = own_holders[None, :, :] == jnp.arange(pool_count, dtype=jnp.int32)[:, None, None]
    block_place = jnp.sum(jnp.where(matches, positions[None], 0), axis=2)
    scale_rows = cache_scale[send_slots]
    split_cache = cache.reshape(slot_count, block_size, 2 * kv_heads, head_size)
    share_size = 2 * kv_heads // member_count
    outgoing = lax.dynamic_slice_in_dim(
        split_cache[send_slots], member_index * share_size, share_size, 3
    )
    arrived_part, arrived_scale = (
        lax.all_to_all(outgoing, "pool", split_axis=0, concat_axis=0, tiled=True),
        lax.all_to_all(scale_rows, "pool", split_axis=0, concat_axis=0, tiled=True),
    )
    arrived = lax.all_gather(arrived_part, "blk", axis=3, tiled=True)
    prefix_tokens = pool_count * run_count * block_size
    step_tokens = min(1024, prefix_tokens)
    step_count = prefix_tokens // step_tokens
    prefix_stack = arrived.reshape(step_count, step_tokens, 2, kv_heads, head_size)
    token_scale = jnp.broadcast_to(
        arrived_scale.astype(jnp.float32).reshape(pool_count, run_count, 1, 2, kv_heads),
        (pool_count, run_count, block_size, 2, kv_heads),
    ).reshape(step_count, step_tokens, 2, kv_heads)
    token_place = (
        block_place[:, :, None] * block_size
        + jnp.arange(block_size, dtype=jnp.int32)[None, None, :]
    ).reshape(step_count, step_tokens)
    query_heads = jnp.transpose(
        queries.reshape(local_rows, kv_heads, per_group, head_size), (1, 2, 0, 3)
    )
    row_place = member_index * local_rows + jnp.arange(local_rows, dtype=jnp.int32)
    initial = (
        jnp.full((kv_heads, per_group, local_rows), masked_score, jnp.float32),
        jnp.zeros((kv_heads, per_group, local_rows), jnp.float32),
        jnp.zeros((kv_heads, per_group, local_rows, head_size), jnp.float32),
    )
    shard_rows = lax.all_gather(suffix_kv, "blk", axis=0, tiled=True)
    piece_count = shard_rows.shape[0]
    split_rows = shard_rows.reshape(piece_count, 2, kv_heads, head_size)
    key_place = jnp.arange(piece_count, dtype=jnp.int32)
    usable = (key_place[None, :] <= row_place[:, None]) & (key_place[None, :] < suffix_length)
    flat_scale = jnp.full((piece_count, kv_heads), inv_root, jnp.float32)
    unit_scale = jnp.ones((piece_count, kv_heads), jnp.float32)
    running = fold_keys(
        initial, query_heads, split_rows[:, 0], split_rows[:, 1], flat_scale, unit_scale, usable
    )

    def prefix_step(running, step_inputs):
        token_rows, scale_step, place_rows = step_inputs
        usable = (place_rows < prefix_length)[None, :]
        updated = fold_keys(
            running,
            query_heads,
            token_rows[:, 0],
            token_rows[:, 1],
            scale_step[:, 0] * inv_root,
            scale_step[:, 1],
            usable,
        )
        return (updated, None)

    running, unused = lax.scan(prefix_step, running, (prefix_stack, token_scale, token_place))
    highest, weight_sum, weighted = running
    result = weighted / weight_sum[..., None]
    result = jnp.transpose(result, (2, 0, 1, 3)).reshape(local_rows, QH * head_size)
    result = jnp.where((row_place < suffix_length)[:, None], result, 0.0)
    return result.astype(jnp.bfloat16)


def solution(mesh):
    small = dict(mesh.shape) == {"pool": POOL, "blk": 4}
    return jax.shard_map(
        per_device_small if small else per_device_any,
        mesh=mesh,
        in_specs=(
            P(("pool", "blk"), None),
            P(("pool", "blk"), None),
            P("pool", None, None),
            P("pool", None),
            P(),
            P(),
            P(),
            P(),
        ),
        out_specs=P(("pool", "blk"), None),
        check_vma=False,
    )
```
